32 devices in a mesh: seq: 8 (over y, x, core), head: 4 (over z).
Axes of the slice: x: 2, y: 2, z: 4, core: 2. Of those that a mesh axis runs over, the one named last changes fastest.
Arguments:
- stream: float32 [2, 8192, 1024], P(None, 'seq'), may hold values from -20 to 20
- cotangent: float32 [2, 8192, 1024], P(None, 'seq'), may hold values from -6 to 6
- mixer_in: bfloat16 [1024, 4, 1024], P(None, None, 'head'), may hold values from -0.1875 to 0.1875
- memory_in: bfloat16 [1024, 3, 1024], P(None, None, 'head'), may hold values from -0.1875 to 0.1875
- mixer_out: bfloat16 [1024, 1024], P('head'), may hold values from -0.5 to 0.5
- ffn_in: bfloat16 [1024, 2, 2816], P(None, None, 'head'), may hold values from -0.1875 to 0.1875
- ffn_out: bfloat16 [2816, 1024], P('head'), may hold values from -0.109375 to 0.109375
- persistent: bfloat16 [32, 1024], P(None, 'head'), may hold values from -5 to 5
- norm_gains: float32 [2, 1024], replicated, may hold values from 0.1 to 1.9
- conv_weight: float32 [4, 1024], replicated, may hold values from -3 to 3
- decays: float32 [2, 8, 8192], P(None, 'head', 'seq'), may hold values from 0 to 1
- doc_starts: int32 [2, 8], replicated, may hold values from 1 to 8192, as said below
Outputs:
- result: float32 [2, 8192, 1024], P(None, 'seq', 'head')
- grad_stream: float32 [2, 8192, 1024], P(None, 'seq', 'head')
- grad_mixer_in: float32 [1024, 4, 1024], P('seq', None, 'head')
- grad_memory_in: float32 [1024, 3, 1024], P('seq', None, 'head')
- grad_mixer_out: float32 [1024, 1024], P('head', 'seq')
- grad_ffn_in: float32 [1024, 2, 2816], P('seq', None, 'head')
- grad_ffn_out: float32 [2816, 1024], P('head', 'seq')
- grad_persistent: float32 [32, 1024], P('seq', 'head')
- grad_norm_gains: float32 [2, 1024], replicated
- grad_conv_weight: float32 [4, 1024], replicated
- rms_values: float32 [4], replicated
The draws below stay inside these ranges and needn't reach their ends.
Inputs may be any that keep to these rules, and one draw needn't show every extreme that they name: `doc_starts`: in each stream either every entry equals 8192, so that the whole stream is one document, or the entries are strictly increasing and entry k lies in the k-th of 8 equal stretches of the stream; position 0 always begins a document.
All inputs are finite; a program needn't handle non-finite values.
Results may differ from the reference program's by a relative error of at most 0.012.
The reference program's roundings to bfloat16 on the way count: a program that leaves them out, or rounds other values in their place, can miss the bound.
Values may be sent and summed in bfloat16 or wider, within the bound.
No kernel may reach another device: no remote copies, remote signals or barrier semaphores. Data moves between devices by JAX's collectives and lax.ppermute only.
A program may use at most 256 MiB of HBM per device.

```python
import math
from functools import partial
import jax
import jax.numpy as jnp
from jax import lax

D = 1024
HEAD_TOTAL = 8
HD = 128
FF = 2816
KC = 4
PERSIST = 16
SEG = 1024
DOCS = 8
BATCH_STREAMS = 2
STREAM_LENGTH = 8192


def draw_stream(key, part):
    key = jax.random.fold_in(key, 11)
    key_noise, key_rows = jax.random.split(key)
    spot_frac = jnp.arange(STREAM_LENGTH, dtype=jnp.float32) / STREAM_LENGTH
    base_noise = jnp.clip(jax.random.normal(key_noise, (BATCH_STREAMS, STREAM_LENGTH, D)), -5.0, 5.0)
    row_scale = jax.random.uniform(key_rows, (BATCH_STREAMS, STREAM_LENGTH, 1), minval=0.7, maxval=1.4)
    rise_factor = 0.5 + spot_frac
    return base_noise * row_scale * rise_factor[None, :, None]


def draw_decays(key, part):
    key = jax.random.fold_in(key, 23)
    key_head, key_block, key_jitter, key_locations, key_loss = jax.random.split(key, 5)
    head_pick = jax.random.uniform(key_head, (BATCH_STREAMS, HEAD_TOTAL, 1))
    slowness = jnp.sqrt(head_pick)
    fast_log = math.log(1.0 / 40.0)
    slow_log = math.log(1.0 / (8.0 * STREAM_LENGTH))
    decay_speed = jnp.exp(fast_log + (slow_log - fast_log) * slowness)
    block_multiplier = jnp.exp(jax.random.uniform(key_block, (BATCH_STREAMS, HEAD_TOTAL, STREAM_LENGTH // SEG, 1), minval=-0.7, maxval=0.7))
    block_multiplier = jnp.broadcast_to(block_multiplier, (BATCH_STREAMS, HEAD_TOTAL, STREAM_LENGTH // SEG, SEG)).reshape(BATCH_STREAMS, HEAD_TOTAL, STREAM_LENGTH)
    random_perturbation = jax.random.uniform(key_jitter, (BATCH_STREAMS, HEAD_TOTAL, STREAM_LENGTH), minval=0.5, maxval=1.5)
    spike_positions = jax.random.randint(key_locations, (BATCH_STREAMS, HEAD_TOTAL, 6, 1), 0, STREAM_LENGTH)
    loss_values = jax.random.uniform(key_loss, (BATCH_STREAMS, HEAD_TOTAL, 6, 1), minval=0.22, maxval=0.69)
    location_list = jnp.arange(STREAM_LENGTH, dtype=jnp.int32)[None, None, None, :]
    spike_loss = jnp.sum(jnp.where(spike_positions == location_list, loss_values, 0.0), axis=2)
    return jnp.exp(-decay_speed * block_multiplier * random_perturbation - spike_loss)


def draw_doc_starts(key, part):
    key = jax.random.fold_in(key, 37)
    key_offsets, key_pick, key_near, key_whole = jax.random.split(key, 4)
    stretch = STREAM_LENGTH // DOCS
    bases = jnp.arange(DOCS, dtype=jnp.int32) * stretch
    offsets = jax.random.randint(key_offsets, (BATCH_STREAMS, DOCS), 1, stretch)
    picked = jax.random.randint(key_pick, (BATCH_STREAMS, 1), 1, DOCS)
    near = jax.random.randint(key_near, (BATCH_STREAMS, 1), 0, 3)
    lanes = jnp.arange(DOCS, dtype=jnp.int32)[None, :]
    offsets = jnp.where(lanes == picked, near, offsets)
    starts = (bases[None, :] + offsets).astype(jnp.int32)
    whole_row = jax.random.randint(key_whole, (), 0, BATCH_STREAMS)
    row_ids = jnp.arange(BATCH_STREAMS, dtype=jnp.int32)[:, None]
    return jnp.where(row_ids == whole_row, STREAM_LENGTH, starts).astype(jnp.int32)


def block_scale(key, extent, pieces, least, largest):
    level = 1.0
    for position, parts in pieces:
        steps = jax.random.uniform(jax.random.fold_in(jax.random.fold_in(key, 6), position), (parts,), jnp.float32, least / len(pieces), largest / len(pieces))
        level = level * jnp.repeat(jnp.exp(steps), extent[position] // parts).reshape((-1,) + (1,) * (len(extent) - 1 - position))
    return level


def centred(rng, extent, spread, bound, pieces=(), kind=jnp.bfloat16):
    values = jax.random.normal(rng, extent, jnp.float32) * spread
    if len(pieces) > 0:
        values = block_scale(rng, extent, pieces, -0.22, 0.18) * values
    return jnp.clip(values, min=-bound, max=bound).astype(kind)


def setup_inputs(seed: int = 0) -> dict:
    streams_of = jax.random.split(jax.random.key(seed), 13)
    stream = draw_stream(jax.random.fold_in(streams_of[12], 71), 0)
    cotangent = centred(streams_of[1], (BATCH_STREAMS, STREAM_LENGTH, D), 1.0, 6.0, ((1, 8),), jnp.float32)
    mixer_in = centred(streams_of[2], (D, 4, HEAD_TOTAL * HD), D ** -0.5, 0.1875, ((2, 4),))
    memory_in = centred(streams_of[3], (D, 3, HEAD_TOTAL * HD), D ** -0.5, 0.1875, ((2, 4),))
    mixer_out = centred(streams_of[4], (HEAD_TOTAL * HD, D), HD ** -0.5, 0.5, ((0, 4),))
    ffn_in = centred(streams_of[5], (D, 2, FF), D ** -0.5, 0.1875, ((2, 4),))
    ffn_out = centred(streams_of[6], (FF, D), FF ** -0.5, 0.109375, ((0, 4),))
    persistent = centred(streams_of[7], (2 * PERSIST, HEAD_TOTAL * HD), 1.0, 5.0, ((1, 4),))
    norm_gains = jnp.clip(1.0 + 0.18 * jax.random.normal(streams_of[8], (2, D), jnp.float32), 0.1, 1.9)
    conv_weight = centred(streams_of[9], (KC, D), 0.5, 3.0, (), jnp.float32)
    decays = draw_decays(jax.random.fold_in(streams_of[12], 71), 0)
    doc_starts = draw_doc_starts(jax.random.fold_in(streams_of[12], 71), 0)
    return {"stream": stream, "cotangent": cotangent, "mixer_in": mixer_in, "memory_in": memory_in, "mixer_out": mixer_out, "ffn_in": ffn_in, "ffn_out": ffn_out, "persistent": persistent, "norm_gains": norm_gains, "conv_weight": conv_weight, "decays": decays, "doc_starts": doc_starts}


@jax.custom_vjp
def low(v):
    return lax.optimization_barrier(v.astype(jnp.bfloat16)).astype(jnp.float32)

@jax.custom_vjp
def low_back(v):
    return v

def low_keep(v):
    return (low(v), None)

def low_pass(kept, grad):
    return (grad,)

def back_keep(v):
    return (v, None)

def back_low(kept, grad):
    return (low(grad),)
low.defvjp(low_keep, low_pass)
low_back.defvjp(back_keep, back_low)
EPS = 1e-06
HIGH = lax.Precision.HIGHEST

def rms_norm(values, gain_row):
    return values * lax.rsqrt(lax.optimization_barrier(jnp.mean(values * values, axis=-1, keepdims=True)) + EPS) * gain_row

def unit_rows(values):
    return values * lax.rsqrt(lax.optimization_barrier(jnp.sum(values * values, axis=-1, keepdims=True)) + EPS)

def doc_index(doc_starts, positions):
    return lax.optimization_barrier(jnp.sum((doc_starts[:, None, :] <= positions[None, :, None]).astype(jnp.int32), axis=-1))

def split_heads(values):
    return jnp.transpose(values.reshape(values.shape[0], SEG, HEAD_TOTAL, HD), (0, 2, 1, 3))

def segment_step(params, doc_starts, carried, inputs):
    mixer_in, memory_in, mixer_out, ffn_in, ffn_out, persistent, norm_gains, conv_weight = params
    memory_state, rim_rows = carried
    seg_index, seg_stream, seg_decays = inputs
    first_pos = seg_index * SEG
    positions = first_pos + jnp.arange(SEG, dtype=jnp.int32)
    doc_ids = doc_index(doc_starts, positions)
    rim_ids = doc_index(doc_starts, first_pos - (KC - 1) + jnp.arange(KC - 1, dtype=jnp.int32))
    prev_ids = doc_index(doc_starts, jnp.reshape(first_pos - 1, (1,)))
    normed = low(rms_norm(seg_stream, norm_gains[0]))
    extended = jnp.concatenate([rim_rows, normed], axis=1)
    ext_ids = jnp.concatenate([rim_ids, doc_ids], axis=1)
    conv_sum = jnp.zeros_like(seg_stream)
    for tap_index in range(KC):
        lead_row = KC - 1 - tap_index
        same_doc = (ext_ids[:, lead_row:lead_row + SEG] == doc_ids)[..., None]
        conv_sum = conv_sum + jnp.where(same_doc, extended[:, lead_row:lead_row + SEG], 0.0) * conv_weight[tap_index]
    conv_out = low(conv_sum)
    projected = jnp.einsum('btd,dkc->btkc', normed, mixer_in, precision=HIGH)
    queries = split_heads(low(low_back(projected[:, :, 0])))
    keys_seg = split_heads(low(low_back(projected[:, :, 1])))
    values_seg = split_heads(low(low_back(projected[:, :, 2])))
    gate_open = split_heads(jax.nn.sigmoid(low_back(projected[:, :, 3])))
    per_keys = persistent[:PERSIST].reshape(PERSIST, HEAD_TOTAL, HD)
    per_values = persistent[PERSIST:].reshape(PERSIST, HEAD_TOTAL, HD)
    score_scale = HD ** (-0.5)
    allowed = (positions[:, None] >= positions[None, :])[None] & (doc_ids[:, :, None] == doc_ids[:, None, :])
    seg_scores = low_back(score_scale * jnp.einsum('bhtc,bhsc->bhts', queries, keys_seg, precision=HIGH))
    seg_scores = jnp.where(allowed[:, None], seg_scores, -1e+30)
    per_scores = low_back(score_scale * jnp.einsum('bhtc,phc->bhtp', queries, per_keys, precision=HIGH))
    row_top = jnp.maximum(lax.optimization_barrier(jnp.max(seg_scores, axis=-1)), lax.optimization_barrier(jnp.max(per_scores, axis=-1)))[..., None]
    seg_exp = jnp.exp(seg_scores - row_top)
    per_exp = jnp.exp(per_scores - row_top)
    row_total = lax.optimization_barrier(jnp.sum(seg_exp, axis=-1, keepdims=True)) + lax.optimization_barrier(jnp.sum(per_exp, axis=-1, keepdims=True))
    attended = jnp.einsum('bhts,bhsc->bhtc', low(seg_exp / row_total), values_seg, precision=HIGH)
    attended = attended + jnp.einsum('bhtp,phc->bhtc', low(per_exp / row_total), per_values, precision=HIGH)
    memory_proj = jnp.einsum('btd,dkc->btkc', conv_out, memory_in, precision=HIGH)
    mem_query = low(unit_rows(split_heads(low_back(memory_proj[:, :, 0]))))
    mem_key = low(unit_rows(split_heads(low_back(memory_proj[:, :, 1]))))
    mem_value = split_heads(low(low_back(memory_proj[:, :, 2])))
    log_sums = jnp.cumsum(jnp.log(seg_decays), axis=-1)
    log_gaps = log_sums[..., :, None] - log_sums[..., None, :]
    decay_grid = jnp.where(allowed[:, None], jnp.exp(jnp.minimum(log_gaps, 0.0)), 0.0)
    mem_scores = low_back(jnp.einsum('bhtc,bhsc->bhts', mem_query, mem_key, precision=HIGH))
    recalled = jnp.einsum('bhts,bhsc->bhtc', low(mem_scores * decay_grid), mem_value, precision=HIGH)
    valid_rows = (doc_ids == prev_ids).astype(jnp.float32)
    inflow = jnp.exp(log_sums) * valid_rows[:, None, :]
    recalled = low_back(recalled + jnp.einsum('bhtc,bhcd->bhtd', mem_query * inflow[..., None], memory_state, precision=HIGH))
    end_ids = doc_ids[:, SEG - 1:]
    keep_weights = jnp.exp(log_sums[..., SEG - 1:] - log_sums) * (doc_ids == end_ids).astype(jnp.float32)[:, None, :]
    carry_decay = jnp.exp(log_sums[..., SEG - 1]) * (end_ids == prev_ids).astype(jnp.float32)
    new_state = carry_decay[..., None, None] * memory_state + jnp.einsum('bhsc,bhsd->bhcd', mem_key * keep_weights[..., None], mem_value, precision=HIGH)
    branch = low(low_back(attended + gate_open * recalled))
    flat_branch = jnp.transpose(branch, (0, 2, 1, 3)).reshape(seg_stream.shape[0], SEG, HEAD_TOTAL * HD)
    mixed_out = low_back(jnp.einsum('btc,cd->btd', flat_branch, mixer_out, precision=HIGH))
    middle = seg_stream + mixed_out
    normed_two = low(rms_norm(middle, norm_gains[1]))
    up_pair = jnp.einsum('btd,dkf->btkf', normed_two, ffn_in, precision=HIGH)
    hidden = low(jax.nn.silu(low_back(up_pair[:, :, 0])) * low_back(up_pair[:, :, 1]))
    ffn_result = low_back(jnp.einsum('btf,fd->btd', hidden, ffn_out, precision=HIGH))
    result = middle + ffn_result
    return ((new_state, normed[:, SEG - (KC - 1):]), (result, mixed_out, ffn_result))

def forward(stream, params, decays, doc_starts):
    seg_count = STREAM_LENGTH // SEG
    seg_streams = jnp.transpose(stream.reshape(BATCH_STREAMS, seg_count, SEG, D), (1, 0, 2, 3))
    seg_decays = jnp.transpose(decays.reshape(BATCH_STREAMS, HEAD_TOTAL, seg_count, SEG), (2, 0, 1, 3))
    initial = (jnp.zeros((BATCH_STREAMS, HEAD_TOTAL, HD, HD), jnp.float32), jnp.zeros((BATCH_STREAMS, KC - 1, D), jnp.float32))
    step_fn = jax.checkpoint(partial(segment_step, params, doc_starts))
    unused, outputs = lax.scan(step_fn, initial, (jnp.arange(seg_count, dtype=jnp.int32), seg_streams, seg_decays))
    return tuple((jnp.transpose(piece, (1, 0, 2, 3)).reshape(BATCH_STREAMS, STREAM_LENGTH, D) for piece in outputs))

def reference(stream, cotangent, mixer_in, memory_in, mixer_out, ffn_in, ffn_out, persistent, norm_gains, conv_weight, decays, doc_starts):
    params = tuple((weight.astype(jnp.float32) for weight in (mixer_in, memory_in, mixer_out, ffn_in, ffn_out, persistent, norm_gains, conv_weight)))

    def run(stream_in, params_in):
        return forward(stream_in, params_in, decays, doc_starts)
    outputs, pullback = jax.vjp(run, stream, params)
    result, mixed_out, ffn_result = outputs
    grad_stream, grads = pullback((cotangent, jnp.zeros_like(mixed_out), jnp.zeros_like(ffn_result)))
    cell_count = float(BATCH_STREAMS * STREAM_LENGTH * D)
    squares = jnp.stack([jnp.sum(stream * stream), jnp.sum(mixed_out * mixed_out), jnp.sum(ffn_result * ffn_result), jnp.sum(result * result)])
    rms_values = jnp.sqrt(squares / cell_count)
    return (result, grad_stream, grads[0], grads[1], grads[2], grads[3], grads[4], grads[5], grads[6], grads[7], rms_values)
```

```python
import jax
import jax.numpy as jnp
from jax import lax
from jax.sharding import PartitionSpec as P

HD = 128
EPS = 1e-06
F32 = jnp.float32
BF16 = jnp.bfloat16


def doc_index(doc_starts, positions):
    return jnp.sum((doc_starts[:, None, :] <= positions[None, :, None]).astype(jnp.int32), axis=-1)


def dot(a, b, dims):
    return lax.dot_general(a, b, (dims, ((), ())), preferred_element_type=F32)


class Place:
    def __init__(self, batches):
        self.ns = lax.axis_size("seq")
        self.nz = lax.axis_size("head")
        self.nl = self.nz // batches
        self.seq = lax.axis_index("seq")
        self.z = lax.axis_index("head")
        self.p = self.z // self.nl
        self.l = self.z % self.nl
        self.bits = [1 << i for i in range(self.ns.bit_length() - 1)]

    def across(self, value, bit):
        return lax.ppermute(value, "seq", [(i, i ^ bit) for i in range(self.ns)])

    def along(self, value, steps):
        first, last = max(0, -steps), min(self.ns, self.ns - steps)
        return lax.ppermute(value, "seq", [(i, i + steps) for i in range(first, last)])

    def other(self, value):
        return lax.ppermute(value, "head", [(i, (i + self.nl) % self.nz) for i in range(self.nz)])

    def group(self, value, steps):
        nl = self.nl
        return lax.ppermute(
            value,
            "head",
            [(i, i // nl * nl + (i % nl + steps) % nl) for i in range(self.nz)],
        )

    def bit_of(self, bit):
        return (self.seq // bit) % 2

    def fetch(self, weight, order):
        rows = weight.shape[0] // self.ns
        part = self.other(lax.dynamic_slice_in_dim(weight, self.seq * rows, rows, 0))
        done = []
        part = part[None]
        for bit in order:
            got = self.across(part, bit)
            mine = self.bit_of(bit) == 0
            pair = (jnp.where(mine, part, got), jnp.where(mine, got, part))
            done = sorted(done + [bit], reverse=True)
            axis = done.index(bit)
            lead = (2,) * axis
            split = (2,) * (len(done) - 1)
            tail = part.shape[1:]
            pair = [jnp.reshape(a, split + tail) for a in pair]
            part = jnp.stack(pair, axis=axis).reshape((-1,) + tail)
        return part.reshape(weight.shape)

    def scatter(self, grad, order):
        rows, cols = grad.shape
        left = list(reversed(self.bits))
        cur = grad.reshape((2,) * len(left) + (rows // self.ns, cols))
        for bit in order:
            axis = left.index(bit)
            mine = self.bit_of(bit)
            keep = lax.dynamic_index_in_dim(cur, mine, axis, False)
            send = lax.dynamic_index_in_dim(cur, 1 - mine, axis, False)
            got = self.across(send.astype(BF16), bit)
            cur = keep.astype(F32) + got.astype(F32)
            left.remove(bit)
        return cur

    def everywhere(self, value):
        for bit in self.bits:
            value = value + self.across(value, bit)
        return value

    def all_heads(self, value):
        total = value
        for steps in range(1, self.nz):
            total = total + lax.ppermute(
                value, "head", [(i, (i + steps) % self.nz) for i in range(self.nz)]
            )
        return total

    def scan(self, decay, state, reverse):
        pre_d, pre_s = jnp.ones_like(decay), jnp.zeros_like(state)
        tot_d, tot_s = decay, state
        for bit in self.bits:
            got_d, got_s = self.across(tot_d, bit), self.across(tot_s, bit)
            high = (self.bit_of(bit) == 1) ^ reverse
            new_pre_d = jnp.where(high, got_d * pre_d, pre_d)
            new_pre_s = jnp.where(high, pre_d[:, None, None] * got_s + pre_s, pre_s)
            early_d, early_s = jnp.where(high, got_d, tot_d), jnp.where(high, got_s, tot_s)
            late_d, late_s = jnp.where(high, tot_d, got_d), jnp.where(high, tot_s, got_s)
            tot_d = early_d * late_d
            tot_s = late_d[:, None, None] * early_s + late_s
            pre_d, pre_s = new_pre_d, new_pre_s
        return pre_s


def heads_of(values, count):
    return jnp.transpose(values.reshape(values.shape[0], count, HD), (1, 0, 2))


def flat_of(values):
    return jnp.transpose(values, (1, 0, 2)).reshape(values.shape[1], -1)


def unit_back(raw_rows, inv_len, grad_rows):
    unit_vals = raw_rows * inv_len
    return inv_len * (
        grad_rows - unit_vals * jnp.sum(unit_vals * grad_rows, axis=-1, keepdims=True)
    )


def norm_back(values, inv_len, gain_row, grad_rows):
    hat_rows = values * inv_len
    scaled = grad_rows * gain_row
    grad_values = inv_len * (
        scaled - hat_rows * jnp.mean(scaled * hat_rows, axis=-1, keepdims=True)
    )
    return (grad_values, jnp.sum(grad_rows * hat_rows, axis=0))


def local(
    stream,
    cotangent,
    mixer_in,
    memory_in,
    mixer_out,
    ffn_in,
    ffn_out,
    persistent,
    norm_gains,
    conv_weight,
    decays,
    doc_starts,
):
    batches, seg_len, width = stream.shape
    at = Place(batches)
    own_heads = mixer_out.shape[0] // HD
    heads = 2 * own_heads
    own_cols = own_heads * HD
    own_hidden = ffn_out.shape[0]
    taps = conv_weight.shape[0]
    rim = taps - 1
    persist = persistent.shape[0] // 2
    scale = HD**-0.5
    high_bits = list(reversed(at.bits[1:]))
    order_a = high_bits + at.bits[:1]
    order_b = at.bits[1:] + at.bits[:1]
    back_a = at.bits[:1] + high_bits
    back_b = at.bits[:1] + at.bits[1:]

    mixer_two = jnp.concatenate(
        [mixer_in.reshape(width, -1), at.fetch(mixer_in.reshape(width, -1), order_a)], axis=1
    ).reshape(width, 2, 4, own_cols)
    memory_two = jnp.concatenate(
        [memory_in.reshape(width, -1), at.fetch(memory_in.reshape(width, -1), order_b)], axis=1
    ).reshape(width, 2, 3, own_cols)
    out_two = jnp.concatenate([mixer_out, at.fetch(mixer_out, order_b)], axis=0)
    ffn_in_two = jnp.concatenate([ffn_in, at.fetch(ffn_in.reshape(width, -1), order_a).reshape(ffn_in.shape)], axis=2)
    ffn_out_two = jnp.concatenate([ffn_out, at.fetch(ffn_out, order_b)], axis=0)
    persist_two = jnp.concatenate([persistent, at.other(persistent)], axis=1)
    pick = lambda a: lax.dynamic_index_in_dim(a, at.p, 0, False)
    drop = lambda a: lax.dynamic_index_in_dim(a, 1 - at.p, 0, False)
    decay_two = jnp.concatenate([pick(decays), at.other(drop(decays))], axis=0)
    rows_in = pick(stream)
    cot = pick(cotangent)
    starts = lax.dynamic_slice_in_dim(doc_starts, at.p, 1, 0)

    first_pos = at.seq * seg_len
    positions = first_pos + jnp.arange(seg_len, dtype=jnp.int32)
    doc_ids = doc_index(starts, positions)[0]
    rim_ids = doc_index(starts, first_pos - rim + jnp.arange(rim, dtype=jnp.int32))[0]
    prev_id = doc_index(starts, jnp.reshape(first_pos - 1, (1,)))[0]
    end_id = doc_ids[seg_len - 1 :]
    allowed = (positions[:, None] >= positions[None, :]) & (doc_ids[:, None] == doc_ids[None, :])

    inv_one = lax.rsqrt(jnp.mean(rows_in * rows_in, axis=-1, keepdims=True) + EPS)
    normed = (rows_in * inv_one * norm_gains[0]).astype(BF16)
    rim_rows = at.along(normed[seg_len - rim :], 1)
    extended = jnp.concatenate([rim_rows, normed], axis=0).astype(F32)
    ext_ids = jnp.concatenate([rim_ids, doc_ids], axis=0)
    tap_masks = []
    conv_sum = jnp.zeros(rows_in.shape, F32)
    for tap in range(taps):
        lead = rim - tap
        same = (ext_ids[lead : lead + seg_len] == doc_ids)[:, None]
        tap_masks.append(same)
        conv_sum = conv_sum + jnp.where(same, extended[lead : lead + seg_len], 0.0) * conv_weight[tap]
    conv_out = conv_sum.astype(BF16)

    def project(values, weight, count):
        full = dot(values, weight.reshape(width, -1), ((1,), (0,)))
        full = full.reshape(seg_len, 2, count, own_heads, HD)
        return [
            jnp.transpose(full[:, :, i].reshape(seg_len, heads, HD), (1, 0, 2)) for i in range(count)
        ]

    queries, keys, values, gate_pre_mix = project(normed, mixer_two, 4)
    queries, keys, values = queries.astype(BF16), keys.astype(BF16), values.astype(BF16)
    gate_open = jax.nn.sigmoid(gate_pre_mix)
    per_keys = heads_of(persist_two[:persist], heads)
    per_values = heads_of(persist_two[persist:], heads)

    def bdot(a, b, ca, cb):
        return lax.dot_general(a, b, (((ca,), (cb,)), ((0,), (0,))), preferred_element_type=F32)

    def scores():
        seg = jnp.where(allowed[None], scale * bdot(queries, keys, 2, 2), -1e30)
        per = scale * bdot(queries, per_keys, 2, 2)
        return seg, per

    seg_scores, per_scores = scores()
    row_top = jnp.maximum(jnp.max(seg_scores, -1), jnp.max(per_scores, -1))[..., None]
    seg_exp = jnp.exp(seg_scores - row_top)
    per_exp = jnp.exp(per_scores - row_top)
    row_total = jnp.sum(seg_exp, -1, keepdims=True) + jnp.sum(per_exp, -1, keepdims=True)
    log_total = row_top + jnp.log(row_total)
    attended = bdot((seg_exp / row_total).astype(BF16), values, 2, 1)
    attended = attended + bdot((per_exp / row_total).astype(BF16), per_values, 2, 1)

    query_raw, key_raw, value_raw = project(conv_out, memory_two, 3)
    query_inv = lax.rsqrt(jnp.sum(query_raw * query_raw, -1, keepdims=True) + EPS)
    key_inv = lax.rsqrt(jnp.sum(key_raw * key_raw, -1, keepdims=True) + EPS)
    mem_query = (query_raw * query_inv).astype(BF16)
    mem_key = (key_raw * key_inv).astype(BF16)
    mem_value = value_raw.astype(BF16)
    log_sums = jnp.cumsum(jnp.log(decay_two), axis=-1)
    gaps = log_sums[:, :, None] - log_sums[:, None, :]
    decay_grid = jnp.where(allowed[None], jnp.exp(jnp.minimum(gaps, 0.0)), 0.0)
    mem_weights = (bdot(mem_query, mem_key, 2, 2) * decay_grid).astype(BF16)
    recalled = bdot(mem_weights, mem_value, 2, 1)
    inflow = jnp.exp(log_sums) * (doc_ids == prev_id).astype(F32)[None]
    keep = jnp.exp(log_sums[:, seg_len - 1 :] - log_sums) * (doc_ids == end_id).astype(F32)[None]
    carry = jnp.exp(log_sums[:, seg_len - 1]) * (end_id == prev_id).astype(F32)
    kept_keys = (mem_key.astype(F32) * keep[..., None]).astype(BF16)
    state_in = at.scan(carry, bdot(kept_keys, mem_value, 1, 1), False)
    in_queries = (mem_query.astype(F32) * inflow[..., None]).astype(BF16)
    state_low = state_in.astype(BF16)
    recalled = recalled + bdot(in_queries, state_low, 2, 1)
    branch = (attended + gate_open * recalled).astype(BF16)
    flat_branch = flat_of(branch)

    def group_sum(part):
        total = part.astype(F32)
        for steps in range(1, at.nl):
            total = total + at.group(part, steps).astype(F32)
        return total

    mixed_out = group_sum(dot(flat_branch, out_two, ((1,), (0,))).astype(BF16))
    middle = rows_in + mixed_out
    inv_two = lax.rsqrt(jnp.mean(middle * middle, axis=-1, keepdims=True) + EPS)
    normed_two = (middle * inv_two * norm_gains[1]).astype(BF16)
    gate_pre = dot(normed_two, ffn_in_two[:, 0], ((1,), (0,)))
    up_part = dot(normed_two, ffn_in_two[:, 1], ((1,), (0,)))
    gate_sigmoid = jax.nn.sigmoid(gate_pre)
    silu_gate = gate_pre * gate_sigmoid
    hidden = (silu_gate * up_part).astype(BF16)
    ffn_part = dot(hidden, ffn_out_two, ((1,), (0,))).astype(BF16)

    col = width // at.nz

    def columns(value):
        return lax.dynamic_index_in_dim(value.reshape(seg_len, batches, at.nl, col), at.l, 2, False)

    def group_scatter(part):
        total = columns(part).astype(F32)
        view = part.reshape(seg_len, batches, at.nl, col)
        for steps in range(1, at.nl):
            send = lax.dynamic_index_in_dim(view, (at.l + steps) % at.nl, 2, False)
            total = total + at.group(send, steps).astype(F32)
        return total

    def placed(share):
        mine = lax.dynamic_index_in_dim(share, at.p, 1, False)
        got = at.other(lax.dynamic_index_in_dim(share, 1 - at.p, 1, False).astype(BF16)).astype(F32)
        return jnp.where(at.p == 0, jnp.stack([mine, got]), jnp.stack([got, mine]))

    ffn_share = group_scatter(ffn_part)
    result_share = columns(middle) + ffn_share
    result = placed(result_share)

    grad_ffn = cot.astype(BF16)
    grad_hidden = dot(grad_ffn, ffn_out_two, ((1,), (1,)))
    silu_slope = gate_sigmoid * (1.0 + gate_pre * (1.0 - gate_sigmoid))
    grad_gate_pre = (grad_hidden * up_part * silu_slope).astype(BF16)
    grad_up = (grad_hidden * silu_gate).astype(BF16)
    grad_normed_two = dot(grad_gate_pre, ffn_in_two[:, 0], ((1,), (1,))) + dot(
        grad_up, ffn_in_two[:, 1], ((1,), (1,))
    )
    grad_normed_two = group_sum(grad_normed_two.astype(BF16))

    def weight_grad(a, b, order):
        return at.scatter(dot(a, b, ((0,), (0,))).astype(BF16), order)

    h = own_hidden
    fg = weight_grad(normed_two, grad_gate_pre, back_a)
    fu = weight_grad(normed_two, grad_up, back_b)
    fo = weight_grad(grad_ffn, hidden, back_a)

    def both(mine, theirs):
        return mine + at.other(theirs.astype(BF16)).astype(F32)

    grad_ffn_in = jnp.stack([both(fg[:, :h], fg[:, h:]), both(fu[:, :h], fu[:, h:])], axis=1)
    grad_ffn_out = both(fo[:, :h], fo[:, h:]).T

    grad_norm, grad_gain_two = norm_back(middle, inv_two, norm_gains[1], grad_normed_two)
    grad_mid = grad_norm + cot
    grad_mix = grad_mid.astype(BF16)
    fm = weight_grad(grad_mix, flat_branch, back_b)
    grad_mixer_out = both(fm[:, :own_cols], fm[:, own_cols:]).T
    grad_flat = dot(grad_mix, out_two, ((1,), (1,))).astype(BF16)
    grad_branch = heads_of(grad_flat, heads)
    gb_wide = grad_branch.astype(F32)
    grad_recalled = (gb_wide * gate_open).astype(BF16)
    grad_gate_mix = (gb_wide * recalled * gate_open * (1.0 - gate_open)).astype(BF16)
    grad_state = at.scan(carry, bdot(in_queries, grad_recalled, 1, 1), True)
    gs_low = grad_state.astype(BF16)

    seg_scores, per_scores = scores()
    seg_probs = jnp.exp(seg_scores - log_total)
    per_probs = jnp.exp(per_scores - log_total)
    seg_gp = bdot(grad_branch, values, 2, 2)
    per_gp = bdot(grad_branch, per_values, 2, 2)
    delta = jnp.sum(seg_probs * seg_gp, -1, keepdims=True) + jnp.sum(per_probs * per_gp, -1, keepdims=True)
    seg_gs = (seg_probs * (seg_gp - delta)).astype(BF16)
    per_gs = (per_probs * (per_gp - delta)).astype(BF16)
    grad_queries = scale * (bdot(seg_gs, keys, 2, 1) + bdot(per_gs, per_keys, 2, 1))
    grad_keys = scale * bdot(seg_gs, queries, 1, 1)
    grad_per_keys = scale * bdot(per_gs, queries, 1, 1)
    grad_values = bdot(seg_probs.astype(BF16), grad_branch, 1, 1)
    grad_per_values = bdot(per_probs.astype(BF16), grad_branch, 1, 1)
    grad_persist = jnp.concatenate([flat_of(grad_per_keys), flat_of(grad_per_values)], axis=0)

    grad_ms = (bdot(grad_recalled, mem_value, 2, 2) * decay_grid).astype(BF16)
    grad_mq = bdot(grad_ms, mem_key, 2, 1) + inflow[..., None] * bdot(grad_recalled, state_low, 2, 2)
    grad_mk = bdot(grad_ms, mem_query, 1, 1) + keep[..., None] * bdot(mem_value, gs_low, 2, 2)
    grad_mv = bdot(mem_weights, grad_recalled, 1, 1) + bdot(kept_keys, gs_low, 2, 1)
    grad_qr = unit_back(query_raw, query_inv, grad_mq)
    grad_kr = unit_back(key_raw, key_inv, grad_mk)

    def cat(parts):
        stacked = [jnp.transpose(a.astype(BF16), (1, 0, 2)).reshape(seg_len, 2, own_cols) for a in parts]
        return jnp.stack(stacked, axis=2).reshape(seg_len, -1)

    mem_cat = cat([grad_qr, grad_kr, grad_mv])
    mix_cat = cat([grad_queries, grad_keys, grad_values, grad_gate_mix])
    mm = weight_grad(conv_out, mem_cat, back_a)
    half = mm.shape[1] // 2
    grad_memory_in = both(mm[:, :half], mm[:, half:]).reshape(-1, 3, own_cols)
    mi = weight_grad(normed, mix_cat, back_b)
    half = mi.shape[1] // 2
    grad_mixer_in = both(mi[:, :half], mi[:, half:]).reshape(-1, 4, own_cols)
    grad_conv_out = dot(mem_cat, memory_two.reshape(width, -1), ((1,), (1,)))
    grad_normed = dot(mix_cat, mixer_two.reshape(width, -1), ((1,), (1,)))
    grad_ext = jnp.zeros((seg_len + rim, width), F32)
    conv_terms = []
    for tap in range(taps):
        lead = rim - tap
        masked = jnp.where(tap_masks[tap], grad_conv_out, 0.0)
        conv_terms.append(jnp.sum(masked * extended[lead : lead + seg_len], axis=0))
        grad_ext = grad_ext + jnp.pad(masked * conv_weight[tap], ((lead, tap), (0, 0)))
    grad_conv = jnp.stack(conv_terms)
    rim_grads = at.along(grad_ext[:rim], -1)
    grad_normed = grad_normed + grad_ext[rim:] + jnp.pad(rim_grads, ((seg_len - rim, 0), (0, 0)))
    grad_in, grad_gain_one = norm_back(rows_in, inv_one, norm_gains[0], grad_normed)
    grad_stream = placed(group_scatter(grad_in.astype(BF16)) + columns(grad_mid))

    share = 1.0 / at.nl
    squares = jnp.stack(
        [
            jnp.sum(rows_in * rows_in) * share,
            jnp.sum(mixed_out * mixed_out) * share,
            jnp.sum(ffn_share * ffn_share),
            jnp.sum(result_share * result_share),
        ]
    )
    small = jnp.concatenate(
        [
            grad_gain_one[None],
            grad_gain_two[None] * share,
            grad_conv,
            jnp.pad(squares, (0, width - 4))[None],
        ],
        axis=0,
    )
    small = at.all_heads(at.everywhere(small))
    rows_p = persistent.shape[0] // at.ns
    gp = at.everywhere(grad_persist)
    gp = lax.dynamic_slice_in_dim(gp, at.seq * rows_p, rows_p, 0)
    grad_persistent = gp[:, :own_cols] + at.other(gp[:, own_cols:])
    cells = float(batches * seg_len * at.ns * width)
    rms_values = jnp.sqrt(small[2 + taps, :4] / cells)
    return (
        result,
        grad_stream,
        grad_mixer_in,
        grad_memory_in,
        grad_mixer_out,
        grad_ffn_in,
        grad_ffn_out,
        grad_persistent,
        small[:2],
        small[2 : 2 + taps],
        rms_values,
    )


def solution(mesh):
    placed = (
        P(None, "seq", None),
        P(None, "seq", None),
        P(None, None, "head"),
        P(None, None, "head"),
        P("head", None),
        P(None, None, "head"),
        P("head", None),
        P(None, "head"),
        P(),
        P(),
        P(None, "head", "seq"),
        P(),
    )
    return jax.shard_map(
        local,
        mesh=mesh,
        in_specs=placed,
        out_specs=(
            P(None, "seq", "head"),
            P(None, "seq", "head"),
            P("seq", None, "head"),
            P("seq", None, "head"),
            P("head", "seq"),
            P("seq", None, "head"),
            P("head", "seq"),
            P("seq", "head"),
            P(),
            P(),
            P(),
        ),
        check_vma=False,
    )
```

```python
import functools
import math

import jax
import jax.numpy as jnp
from jax import lax
from jax.experimental import pallas as pl
from jax.experimental.pallas import tpu as pltpu
from jax.sharding import PartitionSpec as P

HD = 128
EPS = 1e-06
F32 = jnp.float32
BF16 = jnp.bfloat16


def dot(a, b, dims):
    return lax.dot_general(a, b, (dims, ((), ())), preferred_element_type=F32)


class Place:
    def __init__(self, batches):
        self.ns = lax.axis_size("seq")
        self.nz = lax.axis_size("head")
        self.nl = self.nz // batches
        self.seq = lax.axis_index("seq")
        self.z = lax.axis_index("head")
        self.p = self.z // self.nl
        self.l = self.z % self.nl
        self.bits = [1 << i for i in range(self.ns.bit_length() - 1)]

    def across(self, value, bit):
        return lax.ppermute(value, "seq", [(i, i ^ bit) for i in range(self.ns)])

    def along(self, value, steps):
        first, last = max(0, -steps), min(self.ns, self.ns - steps)
        return lax.ppermute(value, "seq", [(i, i + steps) for i in range(first, last)])

    def other(self, value):
        return lax.ppermute(value, "head", [(i, (i + self.nl) % self.nz) for i in range(self.nz)])

    def group(self, value, steps):
        nl = self.nl
        return lax.ppermute(
            value,
            "head",
            [(i, i // nl * nl + (i % nl + steps) % nl) for i in range(self.nz)],
        )

    def bit_of(self, bit):
        return (self.seq // bit) % 2


LOG2E = 1.4426950408889634
BLOCK = 256
LANES = 128
BATCH, GROUP, CORE, CHIP = 0, 1, 2, 3
DECAY, INFLOW, KEEP, START, AGE = 0, 4, 8, 12, 13


class Line:
    def __init__(self, place):
        self.place = place
        self.waits = []

    def wait(self, *arrays):
        self.waits += arrays

    def run(self, kernel, grid, ins, outs, scratch=(), flops=0, trans=0, onto=(), relay=()):
        moved = sum(a.size * a.dtype.itemsize for a, _, _ in ins)
        moved += sum(math.prod(s) * jnp.dtype(d).itemsize for s, d, _, _ in outs)
        waits, self.waits = self.waits, []
        extra = (*onto, *relay, *waits)
        n_ins, n_outs = len(ins), len(outs)

        def body(place_ref, *refs):
            inputs, outputs = refs[:n_ins], refs[n_ins + len(extra) : n_ins + len(extra) + n_outs]
            rest = refs[n_ins + len(extra) + n_outs + len(relay) :]
            for i in range(place_ref.shape[0]):
                rest[0][i] = place_ref[i]
            kernel(place_ref, *inputs, *outputs, *rest[1:])

        anywhere = pl.BlockSpec(memory_space=pl.ANY)
        spec = pltpu.PrefetchScalarGridSpec(
            num_scalar_prefetch=1,
            grid=grid,
            in_specs=[pl.BlockSpec(b, m) for _, b, m in ins] + [anywhere] * len(extra),
            out_specs=[pl.BlockSpec(b, m) for _, _, b, m in outs]
            + [anywhere] * len(relay)
            + [pl.BlockSpec(memory_space=pltpu.SMEM)],
            scratch_shapes=list(scratch),
        )
        aliases = {1 + n_ins + i: i for i in range(len(onto))}
        aliases |= {1 + n_ins + len(onto) + i: n_outs + i for i in range(len(relay))}
        got = pl.pallas_call(
            body,
            grid_spec=spec,
            out_shape=[jax.ShapeDtypeStruct(s, d) for s, d, _, _ in outs]
            + [jax.ShapeDtypeStruct(a.shape, a.dtype) for a in relay]
            + [jax.ShapeDtypeStruct(self.place.shape, jnp.int32)],
            input_output_aliases=aliases,
            compiler_params=pltpu.CompilerParams(
                dimension_semantics=("arbitrary",) * len(grid), vmem_limit_bytes=56 * 2**20
            ),
            cost_estimate=pl.CostEstimate(flops=int(flops), bytes_accessed=int(moved), transcendentals=int(trans)),
        )(self.place, *[a for a, _, _ in ins], *extra)
        self.place = got[-1]
        return got[:-1]


def rows_map(i, *_):
    return (i, 0)


def whole(rank):
    return lambda *_: (0,) * rank


def column(table, index):
    return table[:, index : index + 1]


def pick_column(table, index):
    lane = lax.broadcasted_iota(jnp.int32, table.shape, 1)
    return jnp.sum(jnp.where(lane == index, table, 0.0), axis=-1, keepdims=True)


def norm_conv_kernel(p_ref, x_ref, gain_ref, rim_ref, table_ref, taps_ref, normed_ref, conv_ref, tail):
    x = x_ref[0]
    inv = lax.rsqrt(jnp.mean(x * x, axis=-1, keepdims=True) + EPS)
    normed = (x * inv * gain_ref[0:1]).astype(BF16)
    normed_ref[...] = normed
    wide = normed.astype(F32)

    @pl.when(pl.program_id(0) == 0)
    def _():
        tail[...] = rim_ref[...].astype(F32)

    ext = jnp.concatenate([tail[...], wide], axis=0)
    age = column(table_ref[...], AGE)
    total = wide * taps_ref[0:1]
    for tap in range(1, taps_ref.shape[0]):
        back = pltpu.roll(ext, tap, 0)[8:]
        total = total + jnp.where(age >= tap, back, 0.0) * taps_ref[tap : tap + 1]
    conv_ref[...] = total.astype(BF16)
    tail[...] = wide[-8:]


def project_kernel(place, x_ref, c_ref, w_ref, table_ref, qkv_ref, gate_ref, mem_ref, inv_ref, state_ref):
    cols = gate_ref.shape[1]
    count = cols // HD
    proj = dot(x_ref[...], w_ref[:, : 4 * cols], ((1,), (0,)))
    qkv_ref[...] = proj[:, : 3 * cols].astype(BF16)
    gate_ref[...] = jax.nn.sigmoid(proj[:, 3 * cols :])
    mem = dot(c_ref[...], w_ref[:, 4 * cols : 7 * cols], ((1,), (0,)))
    lane = lax.broadcasted_iota(jnp.int32, inv_ref.shape[1:], 1)
    invs = jnp.zeros(inv_ref.shape[1:], F32)
    units = []
    for i in range(2 * count):
        raw = mem[:, i * HD : (i + 1) * HD]
        inv = lax.rsqrt(jnp.sum(raw * raw, axis=-1, keepdims=True) + EPS)
        units.append((raw * inv).astype(BF16))
        mem_ref[:, i * HD : (i + 1) * HD] = units[-1]
        invs = jnp.where(lane == i, inv, invs)
    inv_ref[0] = invs
    value = mem[:, 2 * cols :].astype(BF16)
    mem_ref[:, 2 * cols :] = value

    @pl.when(pl.program_id(0) == 0)
    def _():
        state_ref[...] = jnp.zeros_like(state_ref)

    table = table_ref[...]
    for h in range(count):
        kept = (units[count + h].astype(F32) * column(table, KEEP + h)).astype(BF16)
        state_ref[h, :HD] += dot(kept, value[:, h * HD : (h + 1) * HD], ((0,), (0,)))
        carry = column(table, INFLOW + h)[-8:]
        state_ref[h, HD:] = jnp.broadcast_to(carry[7:8], (8, HD))


def joined(early, late):
    state = early[:, :HD] * late[:, HD : HD + 1] + late[:, :HD]
    return jnp.concatenate([state, early[:, HD:] * late[:, HD:]], axis=1)


def pair_scan_kernel(reverse, place, mine_ref, got_ref, out_ref):
    mine, got = mine_ref[...], got_ref[...]
    high = (place[CORE] == 1) ^ reverse
    out_ref[...] = joined(jnp.where(high, got, mine), jnp.where(high, mine, got))


def chip_scan_kernel(reverse, chips, place, got_ref, *refs):
    pairs, out_ref = refs[:-1], refs[-1]
    here = place[place.shape[0] - 1]
    total = None
    for step in range(chips):
        chip = chips - 1 - step if reverse else step
        away = here ^ chip
        block = pairs[0][...]
        for r in range(1, chips):
            block = jnp.where(away == r, pairs[r][...], block)
        before = chip > here if reverse else chip < here
        row = lax.broadcasted_iota(jnp.int32, block.shape, 1)
        block = jnp.where(before, block, jnp.where(row < HD, 0.0, 1.0))
        total = block if total is None else joined(total, block)
    high = (place[CORE] == 1) ^ reverse
    total = jnp.where(high, joined(total, got_ref[...]), total)
    out_ref[...] = total[:, :HD].astype(BF16)


def add_kernel(place, *refs):
    total = refs[0][...]
    for part in refs[1:-1]:
        total = total + part[...]
    refs[-1][...] = total


def assemble_kernel(place, mine_ref, theirs_ref, out_ref):
    share = mine_ref.shape[1]
    first = place[CORE] == 0
    mine, theirs = mine_ref[0], theirs_ref[0]
    out_ref[0, :share] = jnp.where(first, mine, theirs)
    out_ref[0, share:] = jnp.where(first, theirs, mine)


def parted(chips, bit):
    return [r for r in range(chips) if not r & bit], [r for r in range(chips) if r & bit]


def core_sum_kernel(bits, place, keep_ref, got_ref, *outs):
    total = keep_ref[0].astype(F32) + got_ref[0].astype(F32)
    half = total.shape[1] // 2
    for side, bit in enumerate(bits):
        part = total[:, side * half : (side + 1) * half].astype(BF16)
        for out, rs in zip(outs[2 * side : 2 * side + 2], parted(2 * outs[0].shape[0], bit)):
            for i, r in enumerate(rs):

                @pl.when(pl.program_id(0) == r)
                def _():
                    out[i] = part


def chip_step_kernel(rests, place, *refs):
    keeps, gots, outs = refs[:2], refs[2:4], refs[4:]
    for side, (keep, got) in enumerate(zip(keeps, gots)):
        total = [keep[i].astype(F32) + got[i].astype(F32) for i in range(keep.shape[0])]
        if rests is None:
            outs[side][...] = total[0].astype(outs[side].dtype)
            continue
        for out, places in zip(outs[2 * side : 2 * side + 2], rests[side]):
            for i, at in enumerate(places):
                out[i] = total[at].astype(BF16)


def split_columns(place, held, outs):
    batches = 2
    col = outs[0].shape[1] // batches
    group = len(outs)
    for r, out in enumerate(outs):
        target = lax.rem(place[GROUP] + r, group)
        for b in range(batches):
            first = pl.multiple_of((b * group + target) * col, col)
            out[:, b * col : (b + 1) * col] = held[:, pl.ds(first, col)].astype(BF16)


def result_kernel(parts, place, *refs):
    mine_ref, send_ref, squares = refs[-3:]

    @pl.when(pl.program_id(0) == 0)
    def _():
        squares[...] = jnp.zeros_like(squares)

    for side, out in enumerate((mine_ref, send_ref)):
        x_ref, m_a, m_b, n_a, n_b, *shares = refs[side * (5 + parts) : (side + 1) * (5 + parts)]
        x = x_ref[0]
        early = pl.program_id(0) < pl.num_programs(0) // 2
        mixed = jnp.where(early, m_a[...].astype(F32) + m_b[...].astype(F32), n_a[...].astype(F32) + n_b[...].astype(F32))
        ffn = shares[0][...].astype(F32)
        for share in shares[1:]:
            ffn = ffn + share[...].astype(F32)
        result = x + mixed + ffn
        for i, a in enumerate((x, mixed, ffn, result)):
            squares[i : i + 1] += jnp.sum(a * a, axis=0, keepdims=True)
        out[...] = result.astype(out.dtype)


def stream_grad_kernel(parts, place, *refs):
    mine_ref, send_ref = refs[-2:]
    for side, out in enumerate((mine_ref, send_ref)):
        mid, *shares = refs[side * (1 + parts) : (side + 1) * (1 + parts)]
        total = mid[...]
        for share in shares:
            total = total + share[...].astype(F32)
        out[...] = total.astype(out.dtype)


def allowed_block(table, first, rows, count):
    start = column(table, START)[first : first + rows].astype(jnp.int32)
    col = lax.broadcasted_iota(jnp.int32, (rows, count), 1)
    row = lax.broadcasted_iota(jnp.int32, (rows, count), 0) + first
    return (col >= start) & (col <= row)


def attend_kernel(
    scale, place, q_ref, k_ref, v_ref, mq_ref, mk_ref, mv_ref, pk_ref, pv_ref, table_ref, decay_ref,
    att_ref, rec_ref, log_ref,
):
    h = pl.program_id(0)
    seg = q_ref.shape[0]
    table = table_ref[0]
    down = pick_column(table, DECAY + h)
    across = decay_ref[0]
    lane = lax.broadcasted_iota(jnp.int32, (BLOCK, LANES), 1)
    pk, pv = pk_ref[...], pv_ref[...]
    for first in range(0, seg, BLOCK):
        rows, end = slice(first, first + BLOCK), first + BLOCK
        ok = allowed_block(table, first, BLOCK, end)
        query = q_ref[rows]
        s = jnp.where(ok, dot(query, k_ref[:end], ((1,), (1,))) * (scale * LOG2E), -1e30)
        ps = dot(query, pk, ((1,), (1,))) * (scale * LOG2E)
        top = jnp.maximum(jnp.max(s, axis=-1, keepdims=True), jnp.max(ps, axis=-1, keepdims=True))
        e, pe = jnp.exp2(s - top), jnp.exp2(ps - top)
        total = jnp.sum(e, axis=-1, keepdims=True) + jnp.sum(pe, axis=-1, keepdims=True)
        att = dot(e.astype(BF16), v_ref[:end], ((1,), (0,))) + dot(pe.astype(BF16), pv, ((1,), (0,)))
        att_ref[rows] = att / total
        logs = top + jnp.log2(total)
        before = jnp.where(h == 0, 0.0, log_ref[0, rows])
        log_ref[0, rows] = jnp.where(lane == h, logs, before)
        w = dot(mq_ref[rows], mk_ref[:end], ((1,), (1,)))
        grid = jnp.exp2(jnp.minimum(down[rows] - across[:, :end], 0.0))
        w = jnp.where(ok, w * grid, 0.0).astype(BF16)
        rec_ref[rows] = dot(w, mv_ref[:end], ((1,), (0,)))


def mix_kernel(
    place, att_ref, rec_ref, gate_ref, mem_ref, table_a, table_b, state_ref, out_a, out_b,
    recalled_ref, branch_ref, mixed_ref,
):
    cols = out_a.shape[1]
    count = cols // HD
    mixed = None
    for side, (table_ref, out) in enumerate(((table_a, out_a), (table_b, out_b))):
        table = table_ref[...]
        for h in range(count):
            query = mem_ref[:, (3 * side * count + h) * HD : (3 * side * count + h + 1) * HD]
            inward = (query.astype(F32) * column(table, INFLOW + h)).astype(BF16)
            here = slice((side * count + h) * HD, (side * count + h + 1) * HD)
            recalled = rec_ref[:, here] + dot(inward, state_ref[side * count + h], ((1,), (0,)))
            recalled_ref[:, here] = recalled
            branch_ref[:, here] = (att_ref[:, here] + gate_ref[:, here] * recalled).astype(BF16)
        part = dot(branch_ref[:, side * cols : (side + 1) * cols], out[...], ((1,), (1,)))
        mixed = part if mixed is None else mixed + part
    mixed_ref[...] = mixed.astype(BF16)


def ffn_kernel(place, x_ref, m_a, m_b, cot_ref, gain_ref, w_a, w_b, normed_ref, acts_ref, *outs):
    outs, back_ref, held = outs[:-2], outs[-2], outs[-1]
    middle = x_ref[0] + m_a[...].astype(F32) + m_b[...].astype(F32)
    inv = lax.rsqrt(jnp.mean(middle * middle, axis=-1, keepdims=True) + EPS)
    normed = (middle * inv * gain_ref[1:2]).astype(BF16)
    normed_ref[...] = normed
    grad_ffn = cot_ref[0].astype(BF16)
    n = w_a.shape[1] // 3
    part, back = None, None
    for side, w in enumerate((w_a, w_b)):
        pair = dot(normed, w[:, : 2 * n], ((1,), (0,)))
        pre, up = pair[:, :n], pair[:, n:]
        grad_hidden = dot(grad_ffn, w[:, 2 * n :], ((1,), (0,)))
        sig = jax.nn.sigmoid(pre)
        silu = pre * sig
        hidden = (silu * up).astype(BF16)
        slope = sig + silu * (1.0 - sig)
        grad_pre = (grad_hidden * up * slope).astype(BF16)
        grad_up = (grad_hidden * silu).astype(BF16)
        grad_pair = jnp.concatenate([grad_pre, grad_up], axis=1)
        acts_ref[:, 3 * side * n : (3 * side + 2) * n] = grad_pair
        acts_ref[:, (3 * side + 2) * n : (3 * side + 3) * n] = hidden
        one = dot(hidden, w[:, 2 * n :], ((1,), (1,)))
        two = dot(grad_pair, w[:, : 2 * n], ((1,), (1,)))
        part = one if part is None else part + one
        back = two if back is None else back + two
    held[...] = part
    split_columns(place, held, outs)
    back_ref[...] = back.astype(BF16)


def mid_back_kernel(
    place, x_ref, m_a, m_b, g_a, g_b, cot_ref, gain_ref, out_a, out_b, gate_in, recalled_ref, mem_ref,
    table_a, table_b, gain_in, state_in, mid_ref, mix_ref, branch_ref, rec_ref, gate_ref, gain_out, state_ref,
):
    @pl.when(pl.program_id(0) == 0)
    def _():
        gain_out[...] = gain_in[...]
        state_ref[...] = state_in[...]

    middle = x_ref[0] + m_a[...].astype(F32) + m_b[...].astype(F32)
    inv = lax.rsqrt(jnp.mean(middle * middle, axis=-1, keepdims=True) + EPS)
    hat = middle * inv
    grad = g_a[...].astype(F32) + g_b[...].astype(F32)
    scaled = grad * gain_ref[1:2]
    grad_mid = inv * (scaled - hat * jnp.mean(scaled * hat, axis=-1, keepdims=True)) + cot_ref[0]
    gain_out[0:1] += jnp.sum(grad * hat, axis=0, keepdims=True)
    mid_ref[...] = grad_mid
    mix = grad_mid.astype(BF16)
    mix_ref[...] = mix
    cols = out_a.shape[1]
    count = cols // HD
    for side, (out, table_ref) in enumerate(((out_a, table_a), (out_b, table_b))):
        table = table_ref[...]
        here = slice(side * cols, (side + 1) * cols)
        branch = dot(mix, out[...], ((1,), (0,))).astype(BF16)
        branch_ref[:, here] = branch
        wide = branch.astype(F32)
        gate = gate_in[:, here]
        rec = (wide * gate).astype(BF16)
        rec_ref[:, here] = rec
        gate_ref[:, here] = (wide * recalled_ref[:, here] * gate * (1.0 - gate)).astype(BF16)
        for h in range(count):
            query = mem_ref[:, (3 * side * count + h) * HD : (3 * side * count + h + 1) * HD]
            inward = (query.astype(F32) * column(table, INFLOW + h)).astype(BF16)
            state_ref[side * count + h, :HD] += dot(inward, rec[:, h * HD : (h + 1) * HD], ((0,), (0,)))
            carry = column(table, INFLOW + h)[-8:]
            state_ref[side * count + h, HD:] = jnp.broadcast_to(carry[7:8], (8, HD))


def side_columns(head, own):
    first = head // own * 3 * own + lax.rem(head, own)
    return [pl.ds(pl.multiple_of((first + part * own) * HD, HD), HD) for part in range(3)]


def attend_back_kernel(
    scale, place, q_ref, k_ref, v_ref, g_ref, pk_ref, pv_ref, table_ref, log_ref,
    out_ref, dper_ref, dk_sum, dv_sum,
):
    h = pl.program_id(0)
    own = pl.num_programs(0)
    seg = q_ref.shape[0]
    table = table_ref[0]
    logs = pick_column(log_ref[0], h)
    dq_at, dk_at, dv_at = side_columns(h, own)
    pk, pv = pk_ref[...], pv_ref[...]
    persist = pk.shape[0]
    dk_sum[...] = jnp.zeros_like(dk_sum)
    dv_sum[...] = jnp.zeros_like(dv_sum)
    dpk = jnp.zeros(pk.shape, F32)
    dpv = jnp.zeros(pv.shape, F32)
    for first in range(0, seg, BLOCK):
        rows, end = slice(first, first + BLOCK), first + BLOCK
        ok = allowed_block(table, first, BLOCK, end)
        query, grad = q_ref[rows], g_ref[rows]
        s = dot(query, k_ref[:end], ((1,), (1,))) * (scale * LOG2E)
        p = jnp.where(ok, jnp.exp2(s - logs[rows]), 0.0)
        pp = jnp.exp2(dot(query, pk, ((1,), (1,))) * (scale * LOG2E) - logs[rows])
        dp = dot(grad, v_ref[:end], ((1,), (1,)))
        dpp = dot(grad, pv, ((1,), (1,)))
        delta = jnp.sum(p * dp, axis=-1, keepdims=True) + jnp.sum(pp * dpp, axis=-1, keepdims=True)
        ds = (p * (dp - delta)).astype(BF16)
        dps = (pp * (dpp - delta)).astype(BF16)
        dq = dot(ds, k_ref[:end], ((1,), (0,))) + dot(dps, pk, ((1,), (0,)))
        out_ref[rows, dq_at] = (scale * dq).astype(BF16)
        dk_sum[:end] += dot(ds, query, ((0,), (0,)))
        dv_sum[:end] += dot(p.astype(BF16), grad, ((0,), (0,)))
        dpk = dpk + dot(dps, query, ((0,), (0,)))
        dpv = dpv + dot(pp.astype(BF16), grad, ((0,), (0,)))
    out_ref[:, dk_at] = (scale * dk_sum[...]).astype(BF16)
    out_ref[:, dv_at] = dv_sum[...].astype(BF16)
    dper_ref[0, :persist] = scale * dpk
    dper_ref[0, persist:] = dpv


def unit_grad(unit, inv, grad):
    unit = unit.astype(F32)
    return inv * (grad - unit * jnp.sum(unit * grad, axis=-1, keepdims=True))


def memory_back(
    head, count, mq_ref, mk_ref, mv_ref, g_ref, inv_ref, table_ref, decay_ref, state_ref, gstate_ref,
    out_ref, dk_sum, dv_sum,
):
    h = lax.rem(head, count)
    dq_at, dk_at, dv_at = side_columns(head, count)
    seg = mq_ref.shape[0]
    table = table_ref[0]
    invs = inv_ref[0]
    down = pick_column(table, DECAY + h)
    inflow = pick_column(table, INFLOW + h)
    keep = pick_column(table, KEEP + h)
    query_inv, key_inv = pick_column(invs, h), pick_column(invs, count + h)
    across = decay_ref[0]
    state, gstate = state_ref[0], gstate_ref[0]
    dk_sum[...] = jnp.zeros_like(dk_sum)
    dv_sum[...] = jnp.zeros_like(dv_sum)
    for first in range(0, seg, BLOCK):
        rows, end = slice(first, first + BLOCK), first + BLOCK
        ok = allowed_block(table, first, BLOCK, end)
        query, grad = mq_ref[rows], g_ref[rows]
        grid = jnp.where(ok, jnp.exp2(jnp.minimum(down[rows] - across[:, :end], 0.0)), 0.0)
        w = (dot(query, mk_ref[:end], ((1,), (1,))) * grid).astype(BF16)
        dw = (dot(grad, mv_ref[:end], ((1,), (1,))) * grid).astype(BF16)
        dq = dot(dw, mk_ref[:end], ((1,), (0,))) + inflow[rows] * dot(grad, state, ((1,), (1,)))
        out_ref[rows, dq_at] = unit_grad(query, query_inv[rows], dq).astype(BF16)
        dk_sum[:end] += dot(dw, query, ((0,), (0,)))
        dv_sum[:end] += dot(w, grad, ((0,), (0,)))
    key, value = mk_ref[...], mv_ref[...]
    dk = dk_sum[...] + keep * dot(value, gstate, ((1,), (1,)))
    out_ref[:, dk_at] = unit_grad(key, key_inv, dk).astype(BF16)
    kept = (key.astype(F32) * keep).astype(BF16)
    out_ref[:, dv_at] = (dv_sum[...] + dot(kept, gstate, ((1,), (0,)))).astype(BF16)


def in_back_kernel(
    place, x_ref, normed_ref, rim_ref, table_ref, gain_ref, taps_ref, rim_grad_ref,
    dqkv_ref, gate_ref, dmem_ref, w_a, w_b, gain_out, taps_out, *outs,
):
    outs, carried, held = outs[:-2], outs[-2], outs[-1]
    step = pl.program_id(0)
    block = pl.num_programs(0) - 1 - step
    rows = x_ref.shape[1]
    cols = gate_ref.shape[1] // 2
    taps = taps_ref.shape[0]

    @pl.when(step == 0)
    def _():
        gain_out[...] = jnp.zeros_like(gain_out)
        taps_out[...] = jnp.zeros_like(taps_out)
        carried[...] = rim_grad_ref[...]

    mix_a = jnp.concatenate([dqkv_ref[:, : 3 * cols], gate_ref[:, :cols]], axis=1)
    mix_b = jnp.concatenate([dqkv_ref[:, 3 * cols :], gate_ref[:, cols:]], axis=1)
    conv_grad = dot(dmem_ref[:, : 3 * cols], w_a[:, 4 * cols : 7 * cols], ((1,), (1,)))
    conv_grad = conv_grad + dot(dmem_ref[:, 3 * cols :], w_b[:, 4 * cols : 7 * cols], ((1,), (1,)))
    grad = dot(mix_a, w_a[:, : 4 * cols], ((1,), (1,))) + dot(mix_b, w_b[:, : 4 * cols], ((1,), (1,)))
    normed = normed_ref[pl.ds(pl.multiple_of(block * rows, rows), rows)].astype(F32)
    before = normed_ref[pl.ds(pl.multiple_of(jnp.maximum(block * rows - 16, 0), 16), 16)].astype(F32)[8:]
    before = jnp.where(block == 0, rim_ref[...].astype(F32), before)
    ext = jnp.concatenate([before, normed], axis=0)
    age = column(table_ref[...], AGE)
    taps_out[0:1] += jnp.sum(conv_grad * normed, axis=0, keepdims=True)
    grad = grad + conv_grad * taps_ref[0:1]
    spread = jnp.zeros((rows + 8, x_ref.shape[2]), F32)
    zeros = jnp.zeros((8, x_ref.shape[2]), F32)
    for tap in range(1, taps):
        masked = jnp.where(age >= tap, conv_grad, 0.0)
        taps_out[tap : tap + 1] += jnp.sum(masked * pltpu.roll(ext, tap, 0)[8:], axis=0, keepdims=True)
        term = jnp.concatenate([zeros, masked * taps_ref[tap : tap + 1]], axis=0)
        spread = spread + pltpu.roll(term, rows + 8 - tap, 0)
    grad = grad + spread[8:]
    grad = jnp.concatenate([grad[: rows - 8], grad[rows - 8 :] + carried[...]], axis=0)
    carried[...] = spread[:8]
    x = x_ref[0]
    inv = lax.rsqrt(jnp.mean(x * x, axis=-1, keepdims=True) + EPS)
    hat = x * inv
    scaled = grad * gain_ref[0:1]
    held[...] = inv * (scaled - hat * jnp.mean(scaled * hat, axis=-1, keepdims=True))
    split_columns(place, held, outs)
    gain_out[0:1] += jnp.sum(grad * hat, axis=0, keepdims=True)


def put_grad(place, grad, keep_ref, keep_at, sends):
    mine = place[CORE] == 0
    share = keep_ref.shape[1]
    grad = grad.astype(BF16)
    n = grad.shape[1]
    wide = sends[0].shape[2]
    for i in range(grad.shape[0] // (2 * share)):
        low = grad[2 * i * share : (2 * i + 1) * share]
        high = grad[(2 * i + 1) * share : (2 * i + 2) * share]
        keep_ref[i, :, keep_at : keep_at + n] = jnp.where(mine, low, high)
        send = jnp.where(mine, high, low)
        for first in range(keep_at // wide * wide, keep_at + n, wide):
            low_at, high_at = max(first, keep_at), min(first + wide, keep_at + n)
            sends[first // wide][i, :, low_at - first : high_at - first] = send[:, low_at - keep_at : high_at - keep_at]


def memory_weights_kernel(
    heads, place, mq_ref, mk_ref, mv_ref, g_ref, inv_ref, table_ref, decay_ref, state_ref, gstate_ref,
    normed_ref, conv_ref, mix_ref, dqkv_ref, gate_ref, branch_ref, dmem_ref, keep_ref, *refs,
):
    sends, (dk_sum, dv_sum) = refs[:-2], refs[-2:]
    step = pl.program_id(0)
    own = heads // 2
    cols = own * HD

    @pl.when(step < heads)
    def _():
        memory_back(
            step, own, mq_ref, mk_ref, mv_ref, g_ref, inv_ref, table_ref, decay_ref, state_ref, gstate_ref,
            dmem_ref, dk_sum, dv_sum,
        )

    @pl.when(step >= heads)
    def _():
        normed, conv, mix = normed_ref[...].T, conv_ref[...].T, mix_ref[...].T
        for side in range(2):
            one, three = slice(side * cols, (side + 1) * cols), slice(3 * side * cols, 3 * (side + 1) * cols)
            first = 8 * side * cols
            put_grad(place, dot(normed, dqkv_ref[:, three], ((1,), (0,))), keep_ref, first, sends)
            put_grad(place, dot(normed, gate_ref[:, one], ((1,), (0,))), keep_ref, first + 3 * cols, sends)
            put_grad(place, dot(mix, branch_ref[:, one], ((1,), (0,))), keep_ref, first + 4 * cols, sends)
            put_grad(place, dot(conv, dmem_ref[:, three], ((1,), (0,))), keep_ref, first + 5 * cols, sends)


def final_ffn_kernel(hidden, place, mine_ref, got_ref, in_ref, out_ref):
    total = mine_ref[...] + got_ref[...].astype(F32)
    wide = total.shape[1] // 3
    in_ref[:, 0, :] = total[:, :hidden]
    in_ref[:, 1, :] = total[:, wide : wide + hidden]
    out_ref[...] = total[:, 2 * wide :].T[:hidden]


def final_mixer_kernel(place, mine_ref, got_ref, mixer_ref, memory_ref, out_ref):
    total = mine_ref[...] + got_ref[...].astype(F32)
    cols = total.shape[1] // 8
    for i in range(4):
        mixer_ref[:, i, :] = total[:, i * cols : (i + 1) * cols]
    for i in range(3):
        memory_ref[:, i, :] = total[:, (5 + i) * cols : (6 + i) * cols]
    out_ref[...] = total[:, 4 * cols : 5 * cols].T


def placed_kernel(place, mine_ref, got_ref, out_ref):
    mine, got = mine_ref[...], got_ref[...].astype(F32)
    first = place[BATCH] == 0
    out_ref[0] = jnp.where(first, mine, got)
    out_ref[1] = jnp.where(first, got, mine)


def ffn_grad_kernel(place, normed_ref, cot_ref, acts_ref, keep_ref, *refs):
    send, normed_t, cot_t = refs
    step = pl.program_id(0)

    @pl.when(step == 0)
    def _():
        normed_t[...] = normed_ref[...].T
        cot_t[...] = cot_ref[0].astype(BF16).T

    @pl.when(step < 2)
    def _():
        grad = dot(normed_t[...], acts_ref[...], ((1,), (0,)))
        put_grad(place, grad, keep_ref, 0, [send])

    @pl.when(step == 2)
    def _():
        grad = dot(cot_t[...], acts_ref[...], ((1,), (0,)))
        put_grad(place, grad, keep_ref, 0, [send])


def local(
    stream,
    cotangent,
    mixer_in,
    memory_in,
    mixer_out,
    ffn_in,
    ffn_out,
    persistent,
    norm_gains,
    conv_weight,
    decays,
    doc_starts,
):
    batches, seg, width = stream.shape
    at = Place(batches)
    cols = mixer_out.shape[0]
    own = cols // HD
    heads = 2 * own
    hidden = ffn_out.shape[0]
    wide = -(-hidden // LANES) * LANES
    taps = conv_weight.shape[0]
    persist = persistent.shape[0] // 2
    scale = HD**-0.5
    steps = seg // BLOCK
    chips = at.ns // 2
    share = width // at.ns
    col = width // at.nz
    pick = lambda a: lax.dynamic_index_in_dim(a, at.p, 0, False)
    drop = lambda a: lax.dynamic_index_in_dim(a, 1 - at.p, 0, False)
    place = jnp.stack([at.p, at.l] + [at.bit_of(bit) for bit in at.bits] + [at.seq // 2])
    last_place = place.shape[0] - 1
    line = Line(place.astype(jnp.int32))
    run = line.run

    per_a, decay_a = persistent, pick(decays)

    last = lax.dynamic_slice(stream, (at.p, seg - 8, 0), (1, 8, width))[0]
    last = last * lax.rsqrt(jnp.mean(last * last, axis=-1, keepdims=True) + EPS)
    rim_rows = at.along((last * norm_gains[0]).astype(BF16), 1)

    first_row = at.seq * share
    rows_of = lambda a: lax.dynamic_slice_in_dim(a, first_row, share, 0)
    cols_of = lambda a: lax.dynamic_slice_in_dim(a, first_row, share, 1)

    def joined(into, memory, out):
        return jnp.concatenate(
            [into.reshape(into.shape[0], -1), memory.reshape(into.shape[0], -1), out.T], axis=1
        )

    pad = lambda a: jnp.pad(a, ((0, 0), (0, wide - hidden)))

    def ffn_joined(into, out):
        return jnp.concatenate([pad(into[:, 0]), pad(into[:, 1]), pad(out.T)], axis=1)

    part_w = at.other(joined(rows_of(mixer_in), rows_of(memory_in), cols_of(mixer_out)))
    part_f = ffn_joined(rows_of(ffn_in), cols_of(ffn_out))
    other_decay = drop(decays)
    w_a = joined(mixer_in, memory_in, mixer_out)
    f_a = ffn_joined(ffn_in, ffn_out)

    def spread(part):
        return (part, *[at.across(part, 2 * r) for r in range(1, chips)])

    def assemble(parts, relay=()):
        mine = jnp.stack(parts)
        theirs = at.across(mine, 1)
        n = mine.shape[2]
        block = lambda r, s: (r, 0, 0)
        out, *relayed = run(
            assemble_kernel,
            (chips,),
            [(mine, (1, share, n), block), (theirs, (1, share, n), block)],
            [((chips, 2 * share, n), BF16, (1, 2 * share, n), lambda r, s: (s[last_place] ^ r, 0, 0))],
            relay=relay,
        )
        return (out.reshape(width, n), *relayed)

    first_pos = at.seq * seg
    positions = first_pos + jnp.arange(seg, dtype=jnp.int32)
    marks = pick(doc_starts)
    starts = jnp.max(jnp.where(marks[None, :] <= positions[:, None], marks[None, :], 0), axis=-1)

    def token_table(decay):
        log_sums = jnp.cumsum(jnp.log(decay), axis=-1)
        inflow = jnp.exp(log_sums) * (starts < first_pos).astype(F32)
        keep = jnp.exp(log_sums[:, seg - 1 :] - log_sums) * (positions >= starts[seg - 1]).astype(F32)
        scaled_sums = log_sums * LOG2E
        gap = jnp.zeros((4 - own, seg), F32)
        table = jnp.concatenate(
            [
                scaled_sums, gap, inflow, gap, keep, gap,
                jnp.maximum(starts - first_pos, 0).astype(F32)[None],
                (positions - starts).astype(F32)[None],
            ],
            axis=0,
        )
        return jnp.pad(table, ((0, LANES - table.shape[0]), (0, 0))).T, scaled_sums[:, None]

    table_a, decay_rows_a = token_table(decay_a)

    blk = (BLOCK, width)
    batch_rows = lambda i, s: (s[BATCH], i, 0)
    gains_in = (norm_gains, norm_gains.shape, whole(2))
    taps_in = (conv_weight, conv_weight.shape, whole(2))
    stream_in = (stream, (1,) + blk, batch_rows)
    cot_in = (cotangent, (1,) + blk, batch_rows)

    def full(a):
        return (a, a.shape, whole(a.ndim))

    def tiled(a, n=None):
        return (a, (BLOCK, n or a.shape[1]), rows_map)

    def out_rows(n, dtype):
        return ((seg, n), dtype, (BLOCK, n), rows_map)

    def fixed(shape, dtype=F32):
        return (shape, dtype, shape, whole(len(shape)))

    normed, conv_out, other_decay, part_f = run(
        norm_conv_kernel,
        (steps,),
        [stream_in, gains_in, full(rim_rows), tiled(table_a), taps_in],
        [out_rows(width, BF16), out_rows(width, BF16)],
        scratch=[pltpu.VMEM((8, width), F32)],
        flops=20 * seg * width,
        relay=(other_decay, part_f),
    )
    parts_w = spread(lax.optimization_barrier((part_w, normed))[0])
    part_f = at.other(part_f)
    decay_b, per_b = at.other(other_decay), at.other(persistent)

    def project(side, w, table, onto=()):
        half_cols = lambda n, dtype: ((seg, 2 * n), dtype, (BLOCK, n), lambda i, s: (i, side))
        return run(
            project_kernel,
            (steps,),
            [tiled(normed), tiled(conv_out), full(w), tiled(table)],
            [
                half_cols(3 * cols, BF16), half_cols(cols, F32), half_cols(3 * cols, BF16),
                ((2, seg, LANES), F32, (1, BLOCK, LANES), lambda i, s: (side, i, 0)),
                ((heads, HD + 8, HD), F32, (own, HD + 8, HD), lambda i, s: (side, 0, 0)),
            ],
            flops=2 * seg * width * 7 * cols,
            onto=onto,
        )

    def head_cols(a, part, first=0):
        return (
            a,
            (seg, HD),
            lambda h, s: (0, (first + jnp.minimum(h, heads - 1 - first)) // own * 3 * own + part * own + lax.rem(first + jnp.minimum(h, heads - 1 - first), own)),
        )

    pair_flops = own * seg * seg * HD * 1.25

    def attend(side, qkv, mem, per, table, rows, onto=(), relay=()):
        first = side * own
        return run(
            functools.partial(attend_kernel, scale),
            (own,),
            [head_cols(qkv, i, first) for i in range(3)]
            + [head_cols(mem, i, first) for i in range(3)]
            + [(per, (persist, HD), lambda h, s: (0, h)), (per, (persist, HD), lambda h, s: (1, h))]
            + [full(table[None]), (rows, (1, 1, seg), lambda h, s: (h, 0, 0))],
            [((seg, 2 * cols), F32, (seg, HD), lambda h, s: (0, first + h))] * 2
            + [((2, seg, LANES), F32, (1, seg, LANES), lambda h, s: (side, 0, 0))],
            flops=4 * pair_flops,
            trans=own * seg * seg * 1.25,
            onto=onto,
            relay=relay,
        )

    def scan(mine, reverse, first, second, relay):
        got = at.across(mine, 1)
        first()
        (pair,) = run(functools.partial(pair_scan_kernel, reverse), (1,), [full(mine), full(got)], [fixed(mine.shape)])
        pairs = [pair] + [at.across(pair, 2 * r) for r in range(1, chips)]
        second()
        return run(
            functools.partial(chip_scan_kernel, reverse, chips),
            (1,),
            [full(got)] + [full(a) for a in pairs],
            [fixed((heads, HD, HD), BF16)],
            relay=relay(),
        )

    kept = {}

    projected = project(0, w_a, table_a)
    *attended, part_w, part_f = attend(
        0, projected[0], projected[2], per_a, table_a, decay_rows_a, relay=(parts_w[0], part_f)
    )
    parts_f = spread(part_f)
    (w_b,) = assemble((part_w, *parts_w[1:]))
    table_b, decay_rows_b = token_table(decay_b)
    qkv, gate, mem, inv, state = project(1, w_b, table_b, projected)

    def attend_other():
        kept["att"] = attend(1, qkv, mem, per_b, table_b, decay_rows_b, attended)

    nothing = lambda: None
    state_in, *parts_f = scan(state, False, nothing, attend_other, lambda: parts_f)
    att, rec, logs = kept["att"]
    tables = jnp.stack([table_a, table_b])
    decay_rows = jnp.concatenate([decay_rows_a, decay_rows_b], axis=0)
    per_two = jnp.concatenate([per_a, per_b], axis=1)
    out_block = lambda w: (w, (width, cols), lambda i, s: (0, 7))

    half = steps // 2

    def half_in(a, part, n=None):
        return (a, (BLOCK, n or a.shape[1]), lambda i, s: (i + part * half, 0))

    def half_out(n, dtype, part):
        return ((seg, n), dtype, (BLOCK, n), lambda i, s: (i + part * half, 0))

    def half_batch(a, part):
        return (a, (1,) + blk, lambda i, s: (s[BATCH], i + part * half, 0))

    sent_half = ((seg // 2, width), BF16, blk, rows_map)

    def group_sum(part):
        got = [at.group(part, n) for n in range(1, at.nl)]
        total = got[0]
        for more in got[1:]:
            total = (total.astype(F32) + more.astype(F32)).astype(BF16)
        return total

    mixed, mixed_got, onto = [], [], ()
    for part in range(2):
        recalled, branch, mixed_part = run(
            mix_kernel,
            (half,),
            [half_in(a, part) for a in (att, rec, gate, mem, table_a, table_b)]
            + [full(state_in), out_block(w_a), out_block(w_b)],
            [half_out(2 * cols, F32, part), half_out(2 * cols, BF16, part), sent_half],
            flops=seg * width * 2 * cols,
            onto=onto,
        )
        onto = (recalled, branch)
        mixed.append(mixed_part)
        mixed_got.append(group_sum(mixed_part))

    (f_b,) = assemble(parts_f)
    back, back_got, onto = [], [], ()
    for part in range(2):
        normed_two, acts, *ffn_parts, back_part = run(
            ffn_kernel,
            (half,),
            [half_batch(stream, part), tiled(mixed[part]), tiled(mixed_got[part]), half_batch(cotangent, part)]
            + [gains_in, full(f_a), full(f_b)],
            [half_out(width, BF16, part), half_out(6 * wide, BF16, part)]
            + [half_out(batches * col, BF16, part)] * at.nl
            + [sent_half],
            scratch=[pltpu.VMEM(blk, F32)],
            flops=seg * width * wide * 12,
            onto=onto,
        )
        onto = (normed_two, acts, *ffn_parts)
        back.append(back_part)
        back_got.append(group_sum(back_part))
    chip_bits = [bit // 2 for bit in at.bits[1:]]
    orders = (list(reversed(chip_bits)), chip_bits)

    def exchange(parts, step):
        return [parts[0], parts[2]], [at.across(parts[2 * i + 1], 2 * orders[i][step]) for i in range(2)]

    def core_sum(keep_part, got):
        n = got.shape[2]
        there = lambda r, s: (s[last_place] ^ r, 0, 0)
        parts = run(
            functools.partial(core_sum_kernel, (orders[0][0], orders[1][0])),
            (chips,),
            [(a, (1, share, n), there) for a in (keep_part, got)],
            [fixed((chips // 2, share, n // 2), BF16)] * 4,
        )
        return exchange(parts, 0)

    def chip_step(keeps, gots, step):
        half_n = keeps[0].shape[2]
        ins = [full(a) for a in (*keeps, *gots)]
        if step == len(chip_bits):
            mine, theirs = run(
                functools.partial(chip_step_kernel, None),
                (1,),
                ins,
                [fixed((share, half_n)), fixed((share, half_n), BF16)],
            )
            return mine, at.other(theirs)
        rests = []
        for order in orders:
            gone = sum(order[:step])
            held = [r for r in range(chips) if not r & gone]
            rests.append(tuple([i for i, r in enumerate(held) if bool(r & order[step]) == sent] for sent in (False, True)))
        parts = run(
            functools.partial(chip_step_kernel, rests),
            (1,),
            ins,
            [fixed((len(places), share, half_n), BF16) for rest in rests for places in rest],
        )
        return exchange(parts, step)

    def middle_steps(sums):
        for step in range(1, len(chip_bits)):
            sums = chip_step(*sums, step)
        return sums

    def ffn_grads(first, onto=()):
        return run(
            ffn_grad_kernel,
            (3,),
            [
                full(normed_two),
                (cotangent, (1, seg, width), lambda i, s: (s[BATCH], 0, 0)),
                (acts, (seg, wide), lambda i, s: (0, i + first)),
            ],
            [((chips, share, 6 * wide), BF16, (chips, share, wide), lambda i, s: (0, 0, i + first))] * 2,
            scratch=[pltpu.VMEM((width, seg), BF16)] * 2,
            flops=2 * seg * width * wide * 3,
            onto=onto,
        )

    half_f = ffn_grads(0)
    line.wait(back_got[0])
    keep_f, send_f = ffn_grads(3, half_f)

    gain_two, state_terms = jnp.zeros((8, width), F32), jnp.zeros((heads, HD + 8, HD), F32)
    onto = ()
    for part in range(2):
        grad_mid, grad_mix, grad_branch, grad_rec, grad_gate, gain_two, state_terms, *relayed = run(
            mid_back_kernel,
            (half,),
            [half_batch(stream, part)]
            + [tiled(a[part]) for a in (mixed, mixed_got, back, back_got)]
            + [half_batch(cotangent, part), gains_in, out_block(w_a), out_block(w_b)]
            + [half_in(a, part) for a in (gate, recalled, mem, table_a, table_b)]
            + [full(gain_two), full(state_terms)],
            [half_out(width, F32, part), half_out(width, BF16, part)]
            + [half_out(2 * cols, BF16, part)] * 3
            + [fixed((8, width)), fixed((heads, HD + 8, HD))],
            flops=seg * width * 2 * cols,
            onto=onto,
            relay=tuple(ffn_parts[1:]) if part == 0 else (),
        )
        if part == 0:
            ffn_shares = [ffn_parts[0]] + [at.group(a, r + 1) for r, a in enumerate(relayed)]
        onto = (grad_mid, grad_mix, grad_branch, grad_rec, grad_gate)

    def of_side(a):
        return (a, (1, *a.shape[1:]), lambda h, s: (jnp.minimum(h, heads - 1) // own, 0, 0))

    def of_head(a):
        return (a, (1, *a.shape[1:]), lambda h, s: (jnp.minimum(h, heads - 1), 0, 0))

    def head_block(a):
        return (a, (seg, HD), lambda h, s: (0, jnp.minimum(h, heads - 1)))

    def attend_back(side, onto=()):
        first = side * own
        return run(
            functools.partial(attend_back_kernel, scale),
            (own,),
            [head_cols(qkv, i, first) for i in range(3)]
            + [(grad_branch, (seg, HD), lambda h, s: (0, first + h))]
            + [(per_two, (persist, HD), lambda h, s: (0, first + h)), (per_two, (persist, HD), lambda h, s: (1, first + h))]
            + [(a, (1, seg, LANES), lambda h, s: (side, 0, 0)) for a in (tables, logs)],
            [
                ((seg, 6 * cols), BF16, (seg, 3 * cols), lambda h, s: (0, side)),
                ((heads, 2 * persist, HD), F32, (1, 2 * persist, HD), lambda h, s: (first + h, 0, 0)),
            ],
            scratch=[pltpu.VMEM((seg, HD), F32)] * 2,
            flops=5 * pair_flops,
            trans=own * seg * seg * 0.6,
            onto=onto,
        )

    def during_scan():
        kept["back"] = attend_back(0)

    got_f = at.across(lax.optimization_barrier((send_f, grad_mix))[0], 1)
    (grad_state,) = scan(state_terms, True, nothing, during_scan, lambda: ())
    line.wait(*ffn_shares[1:])
    sums_f = core_sum(keep_f, got_f)
    dqkv, per_grad = attend_back(1, kept["back"])

    def share_ins(arrays, side):
        return [(a, (BLOCK, col), lambda i, s: (i, lax.rem(s[BATCH] + side, batches))) for a in arrays]

    def wide_in(a, side):
        return (a, (BLOCK, col), lambda i, s: (i, lax.rem(s[BATCH] + side, batches) * at.nl + s[GROUP]))

    ins = []
    for side in range(2):
        ins.append(
            (
                stream,
                (1, BLOCK, col),
                lambda i, s, side=side: (s[BATCH], i, lax.rem(s[BATCH] + side, batches) * at.nl + s[GROUP]),
            )
        )
        ins += [
            (
                a,
                (BLOCK, col),
                lambda i, s, side=side, part=part: (
                    jnp.clip(i - part * half, 0, half - 1),
                    lax.rem(s[BATCH] + side, batches) * at.nl + s[GROUP],
                ),
            )
            for part in range(2)
            for a in (mixed[part], mixed_got[part])
        ] + share_ins(ffn_shares, side)
    result_mine, result_send, squares = run(
        functools.partial(result_kernel, at.nl),
        (steps,),
        ins,
        [out_rows(col, F32), out_rows(col, BF16), fixed((8, col))],
    )
    result_got = at.other(result_send)
    sums_f = middle_steps(sums_f)

    span = max(2 * share, 256)
    pairs = span // (2 * share)
    turn_of = lambda i: jnp.maximum(i - heads, 0)
    left_in = lambda a: (a, (seg, span), lambda i, s: (0, turn_of(i)))
    grad_out = lambda n: ((chips, share, n), BF16, (pairs, share, n), lambda i, s: (turn_of(i), 0, 0))
    dmem, keep_x, send_x = run(
        functools.partial(memory_weights_kernel, heads),
        (heads + width // span,),
        [head_cols(mem, i) for i in range(3)]
        + [head_block(grad_rec), of_side(inv), of_side(tables), of_head(decay_rows), of_head(state_in), of_head(grad_state)]
        + [left_in(normed), left_in(conv_out), left_in(grad_mix), full(dqkv), full(grad_gate), full(branch)],
        [fixed((seg, 6 * cols), BF16), grad_out(16 * cols), grad_out(16 * cols)],
        scratch=[pltpu.VMEM((seg, HD), F32)] * 2,
        flops=10 * pair_flops + 2 * seg * width * 16 * cols,
        trans=2 * own * seg * seg * 0.6,
    )

    def placed(mine, got):
        return run(placed_kernel, (1,), [full(mine), full(got)], [fixed((batches, seg, col))])[0]

    result = placed(result_mine, result_got)
    f_mine, f_got = chip_step(*sums_f, len(chip_bits))
    got_x = at.across(lax.optimization_barrier((send_x, f_mine))[0], 1)
    sums_x = core_sum(keep_x, got_x)

    first_grad = dot(dmem[:8, : 3 * cols], w_a[:, 4 * cols : 7 * cols], ((1,), (1,))) + dot(
        dmem[:8, 3 * cols :], w_b[:, 4 * cols : 7 * cols], ((1,), (1,))
    )
    ages = (positions - starts)[:8, None]
    rim_back = jnp.zeros((8, width), F32)
    for tap in range(1, taps):
        term = jnp.where(ages >= tap, first_grad, 0.0)[:tap] * conv_weight[tap]
        rim_back = rim_back + jnp.pad(term, ((8 - tap, 0), (0, 0)))
    rim_back = at.along(rim_back, -1)

    line.wait(f_got)
    turned = lambda i, s: (steps - 1 - i, 0)
    turn = lambda a: (a, (BLOCK, a.shape[1]), turned)
    gain_one, grad_conv, *in_parts = run(
        in_back_kernel,
        (steps,),
        [
            (stream, (1,) + blk, lambda i, s: (s[BATCH], steps - 1 - i, 0)), full(normed), full(rim_rows), turn(table_a),
            gains_in, taps_in, full(rim_back),
        ]
        + [turn(a) for a in (dqkv, grad_gate, dmem)]
        + [full(w_a), full(w_b)],
        [fixed((8, width)), fixed((8, width))]
        + [((seg, batches * col), BF16, (BLOCK, batches * col), turned)] * at.nl,
        scratch=[pltpu.VMEM((8, width), F32), pltpu.VMEM(blk, F32)],
        flops=2 * seg * width * 14 * cols,
    )
    in_shares = [in_parts[0]] + [at.group(a, r) for r, a in enumerate(in_parts) if r > 0]


    grad_ffn_in, grad_ffn_out = run(
        functools.partial(final_ffn_kernel, hidden),
        (1,),
        [full(f_mine), full(f_got)],
        [fixed((share, 2, hidden)), fixed((hidden, share))],
    )
    small = jnp.concatenate(
        [
            gain_one[:1], gain_two[:1] / at.nl, grad_conv[:taps],
            jnp.pad(jnp.sum(squares[:4], axis=-1), (0, width - 4))[None],
            per_grad.reshape(-1, width),
        ],
        axis=0,
    )
    small = jnp.pad(small, ((0, -small.shape[0] % 8), (0, 0)))

    def added(parts):
        return run(add_kernel, (1,), [full(a) for a in parts], [fixed(parts[0].shape)])[0]

    small_got = at.across(small, 1)
    sums_x = middle_steps(sums_x)
    small = added([small, small_got])

    ins = []
    for side in range(2):
        ins += [wide_in(grad_mid, side)] + share_ins(in_shares, side)
    stream_mine, stream_send = run(
        functools.partial(stream_grad_kernel, at.nl), (steps,), ins, [out_rows(col, F32), out_rows(col, BF16)]
    )
    stream_got = at.other(stream_send)
    for bit in at.bits[1:-1]:
        small = added([small, at.across(small, bit)])
    x_mine, x_got = chip_step(*sums_x, len(chip_bits))
    small = added([small, at.across(small, at.bits[-1])])
    head_parts = [small] + [
        lax.ppermute(small, "head", [(i, (i + n) % at.nz) for i in range(at.nz)]) for n in range(1, at.nz)
    ]
    grad_stream = placed(stream_mine, stream_got)
    grad_mixer_in, grad_memory_in, grad_mixer_out = run(
        final_mixer_kernel,
        (1,),
        [full(x_mine), full(x_got)],
        [fixed((share, 4, cols)), fixed((share, 3, cols)), fixed((cols, share))],
    )

    sums = sum(a[: 3 + taps] for a in head_parts[1:]) + small[: 3 + taps]
    rows_p = persistent.shape[0] // at.ns

    def persist_rows(a):
        a = a[3 + taps : 3 + taps + heads * 2 * persist * HD // width].reshape(heads, 2 * persist, HD)
        a = lax.dynamic_slice_in_dim(a, at.seq * rows_p, rows_p, 1)
        return jnp.transpose(a, (1, 0, 2)).reshape(rows_p, -1)

    grad_persistent = persist_rows(small)[:, :cols] + persist_rows(head_parts[at.nl])[:, cols:]
    cells = float(batches * seg * at.ns * width)
    rms_values = jnp.sqrt(sums[2 + taps, :4] / cells)
    return (
        result,
        grad_stream,
        grad_mixer_in,
        grad_memory_in,
        grad_mixer_out,
        grad_ffn_in,
        grad_ffn_out,
        grad_persistent,
        sums[:2],
        sums[2 : 2 + taps],
        rms_values,
    )


def solution(mesh):
    placed = (
        P(None, "seq", None),
        P(None, "seq", None),
        P(None, None, "head"),
        P(None, None, "head"),
        P("head", None),
        P(None, None, "head"),
        P("head", None),
        P(None, "head"),
        P(),
        P(),
        P(None, "head", "seq"),
        P(),
    )
    return jax.shard_map(
        local,
        mesh=mesh,
        in_specs=placed,
        out_specs=(
            P(None, "seq", "head"),
            P(None, "seq", "head"),
            P("seq", None, "head"),
            P("seq", None, "head"),
            P("head", "seq"),
            P("seq", None, "head"),
            P("head", "seq"),
            P("seq", "head"),
            P(),
            P(),
            P(),
        ),
        check_vma=False,
    )
```

```python
import functools
import math

import jax
import jax.numpy as jnp
from jax import lax
from jax.experimental import pallas as pl
from jax.experimental.pallas import tpu as pltpu
from jax.sharding import PartitionSpec as P

HD = 128
EPS = 1e-06
F32 = jnp.float32
BF16 = jnp.bfloat16


def dot(a, b, dims):
    return lax.dot_general(a, b, (dims, ((), ())), preferred_element_type=F32)


class Place:
    def __init__(self, batches):
        self.ns = lax.axis_size("seq")
        self.nz = lax.axis_size("head")
        self.nl = self.nz // batches
        self.seq = lax.axis_index("seq")
        self.z = lax.axis_index("head")
        self.p = self.z // self.nl
        self.l = self.z % self.nl
        self.bits = [1 << i for i in range(self.ns.bit_length() - 1)]

    def across(self, value, bit):
        return lax.ppermute(value, "seq", [(i, i ^ bit) for i in range(self.ns)])

    def along(self, value, steps):
        first, last = max(0, -steps), min(self.ns, self.ns - steps)
        return lax.ppermute(value, "seq", [(i, i + steps) for i in range(first, last)])

    def other(self, value):
        return lax.ppermute(value, "head", [(i, (i + self.nl) % self.nz) for i in range(self.nz)])

    def group(self, value, steps):
        nl = self.nl
        return lax.ppermute(
            value,
            "head",
            [(i, i // nl * nl + (i % nl + steps) % nl) for i in range(self.nz)],
        )

    def bit_of(self, bit):
        return (self.seq // bit) % 2


LOG2E = 1.4426950408889634
BLOCK = 256
LANES = 128
BATCH, GROUP, CORE, CHIP = 0, 1, 2, 3
DECAY, INFLOW, KEEP, START, AGE = 0, 4, 8, 12, 13


class Line:
    def __init__(self, place):
        self.place = place
        self.waits = []
        self.last = None

    def wait(self, *arrays):
        self.waits += arrays

    def run(self, kernel, grid, ins, outs, scratch=(), flops=0, trans=0, onto=(), relay=(), placed=True):
        moved = sum(a.size * a.dtype.itemsize for a, _, _ in ins)
        moved += sum(math.prod(s) * jnp.dtype(d).itemsize for s, d, _, _ in outs)
        blocks = sum(2 * math.prod(b) * a.dtype.itemsize for a, b, _ in ins)
        blocks += sum(2 * math.prod(b) * jnp.dtype(d).itemsize for _, d, b, _ in outs)
        blocks += sum(math.prod(a.shape) * jnp.dtype(a.dtype).itemsize for a in scratch)
        waits, self.waits = self.waits, []
        if self.last is not None and not any(self.last is a for a in (*[a for a, _, _ in ins], *onto, *relay, *waits)):
            waits = [*waits, self.last]
        extra = (*onto, *relay, *waits)
        n_ins, n_outs, lead = len(ins), len(outs), 1 if placed else 0

        def body(*refs):
            place_ref, refs = (refs[0] if placed else None), refs[lead:]
            inputs, outputs = refs[:n_ins], refs[n_ins + len(extra) : n_ins + len(extra) + n_outs]
            kernel(place_ref, *inputs, *outputs, *refs[n_ins + len(extra) + n_outs + len(relay) :])

        def mapped(index_map):
            return index_map if placed else lambda *at: index_map(*at, None)

        anywhere = pl.BlockSpec(memory_space=pl.ANY)
        spec = pltpu.PrefetchScalarGridSpec(
            num_scalar_prefetch=lead,
            grid=grid,
            in_specs=[pl.BlockSpec(b, mapped(m)) for _, b, m in ins] + [anywhere] * len(extra),
            out_specs=[pl.BlockSpec(b, mapped(m)) for _, _, b, m in outs] + [anywhere] * len(relay),
            scratch_shapes=list(scratch),
        )
        aliases = {lead + n_ins + i: i for i in range(len(onto))}
        aliases |= {lead + n_ins + len(onto) + i: n_outs + i for i in range(len(relay))}
        got = pl.pallas_call(
            body,
            grid_spec=spec,
            out_shape=[jax.ShapeDtypeStruct(s, d) for s, d, _, _ in outs]
            + [jax.ShapeDtypeStruct(a.shape, a.dtype) for a in relay],
            input_output_aliases=aliases,
            compiler_params=pltpu.CompilerParams(
                dimension_semantics=("arbitrary",) * len(grid), vmem_limit_bytes=blocks + 8 * 2**20
            ),
            cost_estimate=pl.CostEstimate(flops=int(flops), bytes_accessed=int(moved), transcendentals=int(trans)),
        )(*((self.place,) if placed else ()), *[a for a, _, _ in ins], *extra)
        self.last = min(got[:n_outs], key=lambda a: a.size * a.dtype.itemsize)
        return got


def rows_map(i, *_):
    return (i, 0)


def whole(rank):
    return lambda *_: (0,) * rank


def column(table, index):
    return table[:, index : index + 1]


def pick_column(table, index):
    lane = lax.broadcasted_iota(jnp.int32, table.shape, 1)
    return jnp.sum(jnp.where(lane == index, table, 0.0), axis=-1, keepdims=True)


def norm_conv_kernel(p_ref, x_ref, gain_ref, rim_ref, table_ref, taps_ref, normed_ref, conv_ref, tail):
    x = x_ref[0]
    inv = lax.rsqrt(jnp.mean(x * x, axis=-1, keepdims=True) + EPS)
    normed = (x * inv * gain_ref[0:1]).astype(BF16)
    normed_ref[...] = normed
    wide = normed.astype(F32)

    @pl.when(pl.program_id(0) == 0)
    def _():
        tail[...] = rim_ref[...].astype(F32)

    ext = jnp.concatenate([tail[...], wide], axis=0)
    age = column(table_ref[...], 0)
    total = wide * taps_ref[0:1]
    for tap in range(1, taps_ref.shape[0]):
        back = pltpu.roll(ext, tap, 0)[8:]
        total = total + jnp.where(age >= tap, back, 0.0) * taps_ref[tap : tap + 1]
    conv_ref[...] = total.astype(BF16)
    tail[...] = wide[-8:]


def project_kernel(place, x_ref, c_ref, w_ref, table_ref, qkv_ref, gate_ref, mem_ref, inv_ref, state_ref):
    cols = gate_ref.shape[1]
    count = cols // HD
    proj = dot(x_ref[...], w_ref[:, : 4 * cols], ((1,), (0,)))
    qkv_ref[...] = proj[:, : 3 * cols].astype(BF16)
    gate_ref[...] = jax.nn.sigmoid(proj[:, 3 * cols :])
    mem = dot(c_ref[...], w_ref[:, 4 * cols : 7 * cols], ((1,), (0,)))
    lane = lax.broadcasted_iota(jnp.int32, inv_ref.shape[1:], 1)
    invs = jnp.zeros(inv_ref.shape[1:], F32)
    units = []
    for i in range(2 * count):
        raw = mem[:, i * HD : (i + 1) * HD]
        inv = lax.rsqrt(jnp.sum(raw * raw, axis=-1, keepdims=True) + EPS)
        units.append((raw * inv).astype(BF16))
        mem_ref[:, i * HD : (i + 1) * HD] = units[-1]
        invs = jnp.where(lane == i, inv, invs)
    inv_ref[0] = invs
    value = mem[:, 2 * cols :].astype(BF16)
    mem_ref[:, 2 * cols :] = value

    @pl.when(pl.program_id(0) == 0)
    def _():
        state_ref[...] = jnp.zeros_like(state_ref)

    table = table_ref[...]
    for h in range(count):
        kept = (units[count + h].astype(F32) * column(table, KEEP + h)).astype(BF16)
        state_ref[h, :HD] += dot(kept, value[:, h * HD : (h + 1) * HD], ((0,), (0,)))
        carry = column(table, INFLOW + h)[-8:]
        state_ref[h, HD:] = jnp.broadcast_to(carry[7:8], (8, HD))


def joined(early, late):
    state = early[:, :HD] * late[:, HD : HD + 1] + late[:, :HD]
    return jnp.concatenate([state, early[:, HD:] * late[:, HD:]], axis=1)


def pair_scan_kernel(reverse, place, mine_ref, got_ref, out_ref):
    mine, got = mine_ref[...], got_ref[...]
    high = (place[CORE] == 1) ^ reverse
    out_ref[...] = joined(jnp.where(high, got, mine), jnp.where(high, mine, got))


def chip_scan_kernel(reverse, chips, place, got_ref, *refs):
    pairs, out_ref = refs[:-1], refs[-1]
    here = place[place.shape[0] - 1]
    total = None
    for step in range(chips):
        chip = chips - 1 - step if reverse else step
        away = here ^ chip
        block = pairs[0][...]
        for r in range(1, chips):
            block = jnp.where(away == r, pairs[r][...], block)
        before = chip > here if reverse else chip < here
        row = lax.broadcasted_iota(jnp.int32, block.shape, 1)
        block = jnp.where(before, block, jnp.where(row < HD, 0.0, 1.0))
        total = block if total is None else joined(total, block)
    high = (place[CORE] == 1) ^ reverse
    total = jnp.where(high, joined(total, got_ref[...]), total)
    out_ref[...] = total[:, :HD].astype(BF16)


def add_kernel(place, *refs):
    total = refs[0][...]
    for part in refs[1:-1]:
        total = total + part[...]
    refs[-1][...] = total


def stack_kernel(place, *refs):
    for i, ref in enumerate(refs[:-1]):
        refs[-1][i] = ref[...]


def assemble_kernel(place, mine_ref, theirs_ref, out_ref):
    share = mine_ref.shape[1]
    first = place[CORE] == 0
    mine, theirs = mine_ref[0], theirs_ref[0]
    out_ref[0, :share] = jnp.where(first, mine, theirs)
    out_ref[0, share:] = jnp.where(first, theirs, mine)


def parted(chips, bit):
    return [r for r in range(chips) if not r & bit], [r for r in range(chips) if r & bit]


def core_sum_kernel(bits, place, keep_ref, got_ref, *outs):
    total = keep_ref[0].astype(F32) + got_ref[0].astype(F32)
    half = total.shape[1] // 2
    for side, bit in enumerate(bits):
        part = total[:, side * half : (side + 1) * half].astype(BF16)
        for out, rs in zip(outs[2 * side : 2 * side + 2], parted(2 * outs[0].shape[0], bit)):
            for i, r in enumerate(rs):

                @pl.when(pl.program_id(0) == r)
                def _():
                    out[i] = part


def chip_step_kernel(rests, place, *refs):
    keeps, gots, outs = refs[:2], refs[2:4], refs[4:]
    for side, (keep, got) in enumerate(zip(keeps, gots)):
        total = [keep[i].astype(F32) + got[i].astype(F32) for i in range(keep.shape[0])]
        if rests is None:
            outs[side][...] = total[0].astype(outs[side].dtype)
            continue
        for out, places in zip(outs[2 * side : 2 * side + 2], rests[side]):
            for i, at in enumerate(places):
                out[i] = total[at].astype(BF16)


def split_columns(place, held, outs):
    batches = 2
    col = outs[0].shape[1] // batches
    group = len(outs)
    for r, out in enumerate(outs):
        target = lax.rem(place[GROUP] + r, group)
        for b in range(batches):
            first = pl.multiple_of((b * group + target) * col, col)
            out[:, b * col : (b + 1) * col] = held[:, pl.ds(first, col)].astype(BF16)


def result_kernel(parts, place, *refs):
    mine_ref, send_ref, squares = refs[-3:]

    @pl.when(pl.program_id(0) == 0)
    def _():
        squares[...] = jnp.zeros_like(squares)

    for side, out in enumerate((mine_ref, send_ref)):
        x_ref, m_a, m_b, n_a, n_b, *shares = refs[side * (5 + parts) : (side + 1) * (5 + parts)]
        x = x_ref[0]
        early = pl.program_id(0) < pl.num_programs(0) // 2
        mixed = jnp.where(early, m_a[...].astype(F32) + m_b[...].astype(F32), n_a[...].astype(F32) + n_b[...].astype(F32))
        ffn = shares[0][...].astype(F32)
        for share in shares[1:]:
            ffn = ffn + share[...].astype(F32)
        result = x + mixed + ffn
        for i, a in enumerate((x, mixed, ffn, result)):
            squares[i : i + 1] += jnp.sum(a * a, axis=0, keepdims=True)
        out[...] = result.astype(out.dtype)


def stream_grad_kernel(parts, place, *refs):
    mine_ref, send_ref = refs[-2:]
    for side, out in enumerate((mine_ref, send_ref)):
        mid, *shares = refs[side * (1 + parts) : (side + 1) * (1 + parts)]
        total = mid[...]
        for share in shares:
            total = total + share[...].astype(F32)
        out[...] = total.astype(out.dtype)


def allowed_block(table, first, rows, count):
    start = column(table, START)[first : first + rows].astype(jnp.int32)
    col = lax.broadcasted_iota(jnp.int32, (rows, count), 1)
    row = lax.broadcasted_iota(jnp.int32, (rows, count), 0) + first
    return (col >= start) & (col <= row)


def attend_kernel(
    scale, place, q_ref, k_ref, v_ref, mq_ref, mk_ref, mv_ref, pk_ref, pv_ref, table_ref, decay_ref,
    att_ref, rec_ref, log_ref,
):
    h = pl.program_id(0)
    seg = q_ref.shape[0]
    table = table_ref[0]
    down = pick_column(table, DECAY + h)
    across = decay_ref[0]
    lane = lax.broadcasted_iota(jnp.int32, (BLOCK, LANES), 1)
    pk, pv = pk_ref[...], pv_ref[...]
    for first in range(0, seg, BLOCK):
        rows, end = slice(first, first + BLOCK), first + BLOCK
        ok = allowed_block(table, first, BLOCK, end)
        query = q_ref[rows]
        s = jnp.where(ok, dot(query, k_ref[:end], ((1,), (1,))) * (scale * LOG2E), -1e30)
        ps = dot(query, pk, ((1,), (1,))) * (scale * LOG2E)
        top = jnp.maximum(jnp.max(s, axis=-1, keepdims=True), jnp.max(ps, axis=-1, keepdims=True))
        e, pe = jnp.exp2(s - top), jnp.exp2(ps - top)
        total = jnp.sum(e, axis=-1, keepdims=True) + jnp.sum(pe, axis=-1, keepdims=True)
        att = dot(e.astype(BF16), v_ref[:end], ((1,), (0,))) + dot(pe.astype(BF16), pv, ((1,), (0,)))
        att_ref[rows] = att / total
        logs = top + jnp.log2(total)
        before = jnp.where(h == 0, 0.0, log_ref[0, rows])
        log_ref[0, rows] = jnp.where(lane == h, logs, before)
        w = dot(mq_ref[rows], mk_ref[:end], ((1,), (1,)))
        grid = jnp.exp2(jnp.minimum(down[rows] - across[:, :end], 0.0))
        w = jnp.where(ok, w * grid, 0.0).astype(BF16)
        rec_ref[rows] = dot(w, mv_ref[:end], ((1,), (0,)))


def mix_kernel(
    place, att_ref, rec_ref, gate_ref, mem_ref, table_a, table_b, state_ref, out_a, out_b,
    recalled_ref, branch_ref, mixed_ref,
):
    cols = out_a.shape[1]
    count = cols // HD
    mixed = None
    for side, (table_ref, out) in enumerate(((table_a, out_a), (table_b, out_b))):
        table = table_ref[...]
        for h in range(count):
            query = mem_ref[:, (3 * side * count + h) * HD : (3 * side * count + h + 1) * HD]
            inward = (query.astype(F32) * column(table, INFLOW + h)).astype(BF16)
            here = slice((side * count + h) * HD, (side * count + h + 1) * HD)
            recalled = rec_ref[:, here] + dot(inward, state_ref[side * count + h], ((1,), (0,)))
            recalled_ref[:, here] = recalled
            branch_ref[:, here] = (att_ref[:, here] + gate_ref[:, here] * recalled).astype(BF16)
        part = dot(branch_ref[:, side * cols : (side + 1) * cols], out[...], ((1,), (1,)))
        mixed = part if mixed is None else mixed + part
    mixed_ref[...] = mixed.astype(BF16)


def ffn_kernel(place, x_ref, m_a, m_b, cot_ref, gain_ref, w_a, w_b, normed_ref, cot_out, acts_ref, *outs):
    outs, back_ref, held = outs[:-2], outs[-2], outs[-1]
    middle = x_ref[0] + m_a[...].astype(F32) + m_b[...].astype(F32)
    inv = lax.rsqrt(jnp.mean(middle * middle, axis=-1, keepdims=True) + EPS)
    normed = (middle * inv * gain_ref[1:2]).astype(BF16)
    normed_ref[...] = normed.T
    grad_ffn = cot_ref[0].astype(BF16)
    cot_out[...] = grad_ffn.T
    n = w_a.shape[1] // 3
    part, back = None, None
    for side, w in enumerate((w_a, w_b)):
        pair = dot(normed, w[:, : 2 * n], ((1,), (0,)))
        pre, up = pair[:, :n], pair[:, n:]
        grad_hidden = dot(grad_ffn, w[:, 2 * n :], ((1,), (0,)))
        sig = jax.nn.sigmoid(pre)
        silu = pre * sig
        hidden = (silu * up).astype(BF16)
        slope = sig + silu * (1.0 - sig)
        grad_pre = (grad_hidden * up * slope).astype(BF16)
        grad_up = (grad_hidden * silu).astype(BF16)
        grad_pair = jnp.concatenate([grad_pre, grad_up], axis=1)
        acts_ref[:, 3 * side * n : (3 * side + 2) * n] = grad_pair
        acts_ref[:, (3 * side + 2) * n : (3 * side + 3) * n] = hidden
        one = dot(hidden, w[:, 2 * n :], ((1,), (1,)))
        two = dot(grad_pair, w[:, : 2 * n], ((1,), (1,)))
        part = one if part is None else part + one
        back = two if back is None else back + two
    held[...] = part
    split_columns(place, held, outs)
    back_ref[...] = back.astype(BF16)


def mid_back_kernel(
    place, x_ref, m_a, m_b, g_a, g_b, cot_ref, gain_ref, out_a, out_b, gate_in, recalled_ref, mem_ref,
    table_a, table_b, gain_in, state_in, mid_ref, mix_ref, branch_ref, rec_ref, gate_ref, gain_out, state_ref,
):
    @pl.when(pl.program_id(0) == 0)
    def _():
        gain_out[...] = gain_in[...]
        state_ref[...] = state_in[...]

    middle = x_ref[0] + m_a[...].astype(F32) + m_b[...].astype(F32)
    inv = lax.rsqrt(jnp.mean(middle * middle, axis=-1, keepdims=True) + EPS)
    hat = middle * inv
    grad = g_a[...].astype(F32) + g_b[...].astype(F32)
    scaled = grad * gain_ref[1:2]
    grad_mid = inv * (scaled - hat * jnp.mean(scaled * hat, axis=-1, keepdims=True)) + cot_ref[0]
    gain_out[0:1] += jnp.sum(grad * hat, axis=0, keepdims=True)
    mid_ref[...] = grad_mid
    mix = grad_mid.astype(BF16)
    mix_ref[...] = mix
    cols = out_a.shape[1]
    count = cols // HD
    for side, (out, table_ref) in enumerate(((out_a, table_a), (out_b, table_b))):
        table = table_ref[...]
        here = slice(side * cols, (side + 1) * cols)
        branch = dot(mix, out[...], ((1,), (0,))).astype(BF16)
        branch_ref[:, here] = branch
        wide = branch.astype(F32)
        gate = gate_in[:, here]
        rec = (wide * gate).astype(BF16)
        rec_ref[:, here] = rec
        gate_ref[:, here] = (wide * recalled_ref[:, here] * gate * (1.0 - gate)).astype(BF16)
        for h in range(count):
            query = mem_ref[:, (3 * side * count + h) * HD : (3 * side * count + h + 1) * HD]
            inward = (query.astype(F32) * column(table, INFLOW + h)).astype(BF16)
            state_ref[side * count + h, :HD] += dot(inward, rec[:, h * HD : (h + 1) * HD], ((0,), (0,)))
            carry = column(table, INFLOW + h)[-8:]
            state_ref[side * count + h, HD:] = jnp.broadcast_to(carry[7:8], (8, HD))


def side_columns(head, own):
    first = head // own * 3 * own + lax.rem(head, own)
    return [pl.ds(pl.multiple_of((first + part * own) * HD, HD), HD) for part in range(3)]


def attend_back_kernel(
    scale, place, q_ref, k_ref, v_ref, g_ref, pk_ref, pv_ref, table_ref, log_ref,
    out_ref, dper_ref, dk_sum, dv_sum,
):
    h = pl.program_id(0)
    own = pl.num_programs(0)
    seg = q_ref.shape[0]
    table = table_ref[0]
    logs = pick_column(log_ref[0], h)
    dq_at, dk_at, dv_at = side_columns(h, own)
    pk, pv = pk_ref[...], pv_ref[...]
    persist = pk.shape[0]
    dk_sum[...] = jnp.zeros_like(dk_sum)
    dv_sum[...] = jnp.zeros_like(dv_sum)
    dpk = jnp.zeros(pk.shape, F32)
    dpv = jnp.zeros(pv.shape, F32)
    for first in range(0, seg, BLOCK):
        rows, end = slice(first, first + BLOCK), first + BLOCK
        ok = allowed_block(table, first, BLOCK, end)
        query, grad = q_ref[rows], g_ref[rows]
        s = dot(query, k_ref[:end], ((1,), (1,))) * (scale * LOG2E)
        p = jnp.where(ok, jnp.exp2(s - logs[rows]), 0.0)
        pp = jnp.exp2(dot(query, pk, ((1,), (1,))) * (scale * LOG2E) - logs[rows])
        dp = dot(grad, v_ref[:end], ((1,), (1,)))
        dpp = dot(grad, pv, ((1,), (1,)))
        delta = jnp.sum(p * dp, axis=-1, keepdims=True) + jnp.sum(pp * dpp, axis=-1, keepdims=True)
        ds = (p * (dp - delta)).astype(BF16)
        dps = (pp * (dpp - delta)).astype(BF16)
        dq = dot(ds, k_ref[:end], ((1,), (0,))) + dot(dps, pk, ((1,), (0,)))
        out_ref[rows, dq_at] = (scale * dq).astype(BF16)
        dk_sum[:end] += dot(ds, query, ((0,), (0,)))
        dv_sum[:end] += dot(p.astype(BF16), grad, ((0,), (0,)))
        dpk = dpk + dot(dps, query, ((0,), (0,)))
        dpv = dpv + dot(pp.astype(BF16), grad, ((0,), (0,)))
    out_ref[:, dk_at] = (scale * dk_sum[...]).astype(BF16)
    out_ref[:, dv_at] = dv_sum[...].astype(BF16)
    dper_ref[0, :persist] = scale * dpk
    dper_ref[0, persist:] = dpv


def unit_grad(unit, inv, grad):
    unit = unit.astype(F32)
    return inv * (grad - unit * jnp.sum(unit * grad, axis=-1, keepdims=True))


def memory_back(
    head, count, mq_ref, mk_ref, mv_ref, g_ref, inv_ref, table_ref, decay_ref, state_ref, gstate_ref,
    out_ref, dk_sum, dv_sum,
):
    h = lax.rem(head, count)
    dq_at, dk_at, dv_at = side_columns(head, count)
    seg = mq_ref.shape[0]
    table = table_ref[0]
    invs = inv_ref[0]
    down = pick_column(table, DECAY + h)
    inflow = pick_column(table, INFLOW + h)
    keep = pick_column(table, KEEP + h)
    query_inv, key_inv = pick_column(invs, h), pick_column(invs, count + h)
    across = decay_ref[0]
    state, gstate = state_ref[0], gstate_ref[0]
    dk_sum[...] = jnp.zeros_like(dk_sum)
    dv_sum[...] = jnp.zeros_like(dv_sum)
    for first in range(0, seg, BLOCK):
        rows, end = slice(first, first + BLOCK), first + BLOCK
        ok = allowed_block(table, first, BLOCK, end)
        query, grad = mq_ref[rows], g_ref[rows]
        grid = jnp.where(ok, jnp.exp2(jnp.minimum(down[rows] - across[:, :end], 0.0)), 0.0)
        w = (dot(query, mk_ref[:end], ((1,), (1,))) * grid).astype(BF16)
        dw = (dot(grad, mv_ref[:end], ((1,), (1,))) * grid).astype(BF16)
        dq = dot(dw, mk_ref[:end], ((1,), (0,))) + inflow[rows] * dot(grad, state, ((1,), (1,)))
        out_ref[rows, dq_at] = unit_grad(query, query_inv[rows], dq).astype(BF16)
        dk_sum[:end] += dot(dw, query, ((0,), (0,)))
        dv_sum[:end] += dot(w, grad, ((0,), (0,)))
    key, value = mk_ref[...], mv_ref[...]
    dk = dk_sum[...] + keep * dot(value, gstate, ((1,), (1,)))
    out_ref[:, dk_at] = unit_grad(key, key_inv, dk).astype(BF16)
    kept = (key.astype(F32) * keep).astype(BF16)
    out_ref[:, dv_at] = (dv_sum[...] + dot(kept, gstate, ((1,), (0,)))).astype(BF16)


def in_back_kernel(
    place, x_ref, normed_ref, rim_ref, table_ref, gain_ref, taps_ref, rim_grad_ref,
    dqkv_ref, gate_ref, dmem_ref, w_a, w_b, gain_out, taps_out, *outs,
):
    outs, carried, held = outs[:-2], outs[-2], outs[-1]
    step = pl.program_id(0)
    block = pl.num_programs(0) - 1 - step
    rows = x_ref.shape[1]
    cols = gate_ref.shape[1] // 2
    taps = taps_ref.shape[0]

    @pl.when(step == 0)
    def _():
        gain_out[...] = jnp.zeros_like(gain_out)
        taps_out[...] = jnp.zeros_like(taps_out)
        carried[...] = rim_grad_ref[...]

    mix_a = jnp.concatenate([dqkv_ref[:, : 3 * cols], gate_ref[:, :cols]], axis=1)
    mix_b = jnp.concatenate([dqkv_ref[:, 3 * cols :], gate_ref[:, cols:]], axis=1)
    conv_grad = dot(dmem_ref[:, : 3 * cols], w_a[:, 4 * cols : 7 * cols], ((1,), (1,)))
    conv_grad = conv_grad + dot(dmem_ref[:, 3 * cols :], w_b[:, 4 * cols : 7 * cols], ((1,), (1,)))
    grad = dot(mix_a, w_a[:, : 4 * cols], ((1,), (1,))) + dot(mix_b, w_b[:, : 4 * cols], ((1,), (1,)))
    normed = normed_ref[pl.ds(pl.multiple_of(block * rows, rows), rows)].astype(F32)
    before = normed_ref[pl.ds(pl.multiple_of(jnp.maximum(block * rows - 16, 0), 16), 16)].astype(F32)[8:]
    before = jnp.where(block == 0, rim_ref[...].astype(F32), before)
    ext = jnp.concatenate([before, normed], axis=0)
    age = column(table_ref[...], AGE)
    taps_out[0:1] += jnp.sum(conv_grad * normed, axis=0, keepdims=True)
    grad = grad + conv_grad * taps_ref[0:1]
    spread = jnp.zeros((rows + 8, x_ref.shape[2]), F32)
    zeros = jnp.zeros((8, x_ref.shape[2]), F32)
    for tap in range(1, taps):
        masked = jnp.where(age >= tap, conv_grad, 0.0)
        taps_out[tap : tap + 1] += jnp.sum(masked * pltpu.roll(ext, tap, 0)[8:], axis=0, keepdims=True)
        term = jnp.concatenate([zeros, masked * taps_ref[tap : tap + 1]], axis=0)
        spread = spread + pltpu.roll(term, rows + 8 - tap, 0)
    grad = grad + spread[8:]
    grad = jnp.concatenate([grad[: rows - 8], grad[rows - 8 :] + carried[...]], axis=0)
    carried[...] = spread[:8]
    x = x_ref[0]
    inv = lax.rsqrt(jnp.mean(x * x, axis=-1, keepdims=True) + EPS)
    hat = x * inv
    scaled = grad * gain_ref[0:1]
    held[...] = inv * (scaled - hat * jnp.mean(scaled * hat, axis=-1, keepdims=True))
    split_columns(place, held, outs)
    gain_out[0:1] += jnp.sum(grad * hat, axis=0, keepdims=True)


def put_grad(place, grad, keep_ref, keep_at, sends):
    mine = place[CORE] == 0
    share = keep_ref.shape[1]
    grad = grad.astype(BF16)
    n = grad.shape[1]
    wide = sends[0].shape[2]
    for i in range(grad.shape[0] // (2 * share)):
        low = grad[2 * i * share : (2 * i + 1) * share]
        high = grad[(2 * i + 1) * share : (2 * i + 2) * share]
        keep_ref[i, :, keep_at : keep_at + n] = jnp.where(mine, low, high)
        send = jnp.where(mine, high, low)
        for first in range(keep_at // wide * wide, keep_at + n, wide):
            low_at, high_at = max(first, keep_at), min(first + wide, keep_at + n)
            sends[first // wide][i, :, low_at - first : high_at - first] = send[:, low_at - keep_at : high_at - keep_at]


def memory_back_kernel(place, *refs):
    memory_back(pl.program_id(0), pl.num_programs(0) // 2, *refs)


def weight_grad_kernel(
    place, normed_ref, conv_ref, mix_ref, dqkv_ref, gate_ref, branch_ref, dmem_ref, keep_ref, send_ref
):
    cols = gate_ref.shape[1] // 2
    sends = [send_ref]
    normed, conv, mix = normed_ref[...].T, conv_ref[...].T, mix_ref[...].T
    for side in range(2):
        one, three = slice(side * cols, (side + 1) * cols), slice(3 * side * cols, 3 * (side + 1) * cols)
        first = 8 * side * cols
        put_grad(place, dot(normed, dqkv_ref[:, three], ((1,), (0,))), keep_ref, first, sends)
        put_grad(place, dot(normed, gate_ref[:, one], ((1,), (0,))), keep_ref, first + 3 * cols, sends)
        put_grad(place, dot(mix, branch_ref[:, one], ((1,), (0,))), keep_ref, first + 4 * cols, sends)
        put_grad(place, dot(conv, dmem_ref[:, three], ((1,), (0,))), keep_ref, first + 5 * cols, sends)


def final_ffn_kernel(hidden, place, mine_ref, got_ref, in_ref, out_ref):
    total = mine_ref[...] + got_ref[...].astype(F32)
    wide = total.shape[1] // 3
    in_ref[:, 0, :] = total[:, :hidden]
    in_ref[:, 1, :] = total[:, wide : wide + hidden]
    out_ref[...] = total[:, 2 * wide :].T[:hidden]


def final_mixer_kernel(place, mine_ref, got_ref, mixer_ref, memory_ref, out_ref):
    total = mine_ref[...] + got_ref[...].astype(F32)
    cols = total.shape[1] // 8
    for i in range(4):
        mixer_ref[:, i, :] = total[:, i * cols : (i + 1) * cols]
    for i in range(3):
        memory_ref[:, i, :] = total[:, (5 + i) * cols : (6 + i) * cols]
    out_ref[...] = total[:, 4 * cols : 5 * cols].T


def placed_kernel(place, *refs):
    parts, out_ref = refs[:-1], refs[-1]
    first = place[BATCH] == 0
    rows = parts[0].shape[0]
    count = len(parts) // 2
    for i in range(count):
        mine, got = parts[i][...], parts[count + i][...].astype(F32)
        out_ref[0, i * rows : (i + 1) * rows] = jnp.where(first, mine, got)
        out_ref[1, i * rows : (i + 1) * rows] = jnp.where(first, got, mine)


def ffn_grad_kernel(place, left_ref, acts_ref, keep_ref, send_ref):
    put_grad(place, dot(left_ref[...], acts_ref[...], ((1,), (0,))), keep_ref, 0, [send_ref])


def local(
    stream,
    cotangent,
    mixer_in,
    memory_in,
    mixer_out,
    ffn_in,
    ffn_out,
    persistent,
    norm_gains,
    conv_weight,
    decays,
    doc_starts,
):
    batches, seg, width = stream.shape
    at = Place(batches)
    cols = mixer_out.shape[0]
    own = cols // HD
    heads = 2 * own
    hidden = ffn_out.shape[0]
    wide = -(-hidden // LANES) * LANES
    taps = conv_weight.shape[0]
    persist = persistent.shape[0] // 2
    scale = HD**-0.5
    steps = seg // BLOCK
    chips = at.ns // 2
    share = width // at.ns
    col = width // at.nz
    pick = lambda a: lax.dynamic_index_in_dim(a, at.p, 0, False)
    drop = lambda a: lax.dynamic_index_in_dim(a, 1 - at.p, 0, False)
    place = jnp.stack([at.p, at.l] + [at.bit_of(bit) for bit in at.bits] + [at.seq // 2])
    last_place = place.shape[0] - 1
    line = Line(place.astype(jnp.int32))
    run = line.run

    per_a, decay_a = persistent, pick(decays)
    decay_b = at.other(drop(decays))

    last = lax.dynamic_slice(stream, (at.p, seg - 8, 0), (1, 8, width))[0]
    last = last * lax.rsqrt(jnp.mean(last * last, axis=-1, keepdims=True) + EPS)
    rim_rows = at.along((last * norm_gains[0]).astype(BF16), 1)

    first_row = at.seq * share
    rows_of = lambda a: lax.dynamic_slice_in_dim(a, first_row, share, 0)
    cols_of = lambda a: lax.dynamic_slice_in_dim(a, first_row, share, 1)

    def joined(into, memory, out):
        return jnp.concatenate(
            [into.reshape(into.shape[0], -1), memory.reshape(into.shape[0], -1), out.T], axis=1
        )

    pad = lambda a: jnp.pad(a, ((0, 0), (0, wide - hidden)))

    def ffn_joined(into, out):
        return jnp.concatenate([pad(into[:, 0]), pad(into[:, 1]), pad(out.T)], axis=1)

    part_w = at.other(joined(rows_of(mixer_in), rows_of(memory_in), cols_of(mixer_out)))
    part_f = ffn_joined(rows_of(ffn_in), cols_of(ffn_out))

    def spread(part):
        return (part, *[at.across(part, 2 * r) for r in range(1, chips)])

    def stacked(parts):
        n = parts[0].shape[1]
        (mine,) = run(
            stack_kernel, (1,), [full(a) for a in parts], [fixed((chips, share, n), BF16)], placed=False
        )
        return mine, at.across(mine, 1)

    def assemble(mine, theirs):
        n = mine.shape[2]
        block = lambda r, s: (r, 0, 0)
        (out,) = run(
            assemble_kernel,
            (chips,),
            [(mine, (1, share, n), block), (theirs, (1, share, n), block)],
            [((chips, 2 * share, n), BF16, (1, 2 * share, n), lambda r, s: (s[last_place] ^ r, 0, 0))],
        )
        return out.reshape(width, n)

    first_pos = at.seq * seg
    positions = first_pos + jnp.arange(seg, dtype=jnp.int32)
    marks = pick(doc_starts)
    starts = jnp.max(jnp.where(marks[None, :] <= positions[:, None], marks[None, :], 0), axis=-1)

    def token_table(decay):
        log_sums = jnp.cumsum(jnp.log(decay), axis=-1)
        inflow = jnp.exp(log_sums) * (starts < first_pos).astype(F32)
        keep = jnp.exp(log_sums[:, seg - 1 :] - log_sums) * (positions >= starts[seg - 1]).astype(F32)
        scaled_sums = log_sums * LOG2E
        gap = jnp.zeros((4 - own, seg), F32)
        table = jnp.concatenate(
            [
                scaled_sums, gap, inflow, gap, keep, gap,
                jnp.maximum(starts - first_pos, 0).astype(F32)[None],
                (positions - starts).astype(F32)[None],
            ],
            axis=0,
        )
        return jnp.pad(table, ((0, LANES - table.shape[0]), (0, 0))).T, scaled_sums[:, None]


    blk = (BLOCK, width)
    batch_rows = lambda i, s: (s[BATCH], i, 0)
    gains_in = (norm_gains, norm_gains.shape, whole(2))
    taps_in = (conv_weight, conv_weight.shape, whole(2))
    stream_in = (stream, (1,) + blk, batch_rows)
    cot_in = (cotangent, (1,) + blk, batch_rows)

    def full(a):
        return (a, a.shape, whole(a.ndim))

    def tiled(a, n=None):
        return (a, (BLOCK, n or a.shape[1]), rows_map)

    def out_rows(n, dtype):
        return ((seg, n), dtype, (BLOCK, n), rows_map)

    def fixed(shape, dtype=F32):
        return (shape, dtype, shape, whole(len(shape)))

    ages = jnp.broadcast_to((positions - starts)[:, None], (seg, LANES))
    normed, conv_out, part_f = run(
        norm_conv_kernel,
        (steps,),
        [stream_in, gains_in, full(rim_rows), tiled(ages), taps_in],
        [out_rows(width, BF16), out_rows(width, BF16)],
        scratch=[pltpu.VMEM((8, width), F32)],
        flops=20 * seg * width,
        relay=(part_f,),
    )
    part_f = at.other(part_f)
    mixer_in, memory_in, mixer_out, decay_a, _ = lax.optimization_barrier(
        (mixer_in, memory_in, mixer_out, decay_a, conv_out)
    )
    w_a = joined(mixer_in, memory_in, mixer_out)
    table_a, decay_rows_a = token_table(decay_a)
    per_b = at.other(persistent)

    def project(side, w, table, onto=(), relay=()):
        half_cols = lambda n, dtype: ((seg, 2 * n), dtype, (BLOCK, n), lambda i, s: (i, side))
        return run(
            project_kernel,
            (steps,),
            [tiled(normed), tiled(conv_out), full(w), tiled(table)],
            [
                half_cols(3 * cols, BF16), half_cols(cols, F32), half_cols(3 * cols, BF16),
                ((2, seg, LANES), F32, (1, BLOCK, LANES), lambda i, s: (side, i, 0)),
                ((heads, HD + 8, HD), F32, (own, HD + 8, HD), lambda i, s: (side, 0, 0)),
            ],
            placed=False,
            flops=2 * seg * width * 7 * cols,
            onto=onto,
            relay=relay,
        )

    def head_cols(a, part, first=0):
        return (
            a,
            (seg, HD),
            lambda h, s: (0, (first + jnp.minimum(h, heads - 1 - first)) // own * 3 * own + part * own + lax.rem(first + jnp.minimum(h, heads - 1 - first), own)),
        )

    pair_flops = own * seg * seg * HD * 1.25

    def attend(side, qkv, mem, per, table, rows, onto=(), relay=()):
        first = side * own
        return run(
            functools.partial(attend_kernel, scale),
            (own,),
            [head_cols(qkv, i, first) for i in range(3)]
            + [head_cols(mem, i, first) for i in range(3)]
            + [(per, (persist, HD), lambda h, s: (0, h)), (per, (persist, HD), lambda h, s: (1, h))]
            + [full(table[None]), (rows, (1, 1, seg), lambda h, s: (h, 0, 0))],
            [((seg, 2 * cols), F32, (seg, HD), lambda h, s: (0, first + h))] * 2
            + [((2, seg, LANES), F32, (1, seg, LANES), lambda h, s: (side, 0, 0))],
            placed=False,
            flops=4 * pair_flops,
            trans=own * seg * seg * 1.25,
            onto=onto,
            relay=relay,
        )

    def scan(mine, reverse, first, second, relay):
        got = at.across(mine, 1)
        first()
        pair, *relayed = run(
            functools.partial(pair_scan_kernel, reverse), (1,), [full(mine), full(got)], [fixed(mine.shape)], relay=relay
        )
        pairs = [pair] + [at.across(pair, 2 * r) for r in range(1, chips)]
        second(*relayed)
        (out,) = run(
            functools.partial(chip_scan_kernel, reverse, chips),
            (1,),
            [full(got)] + [full(a) for a in pairs],
            [fixed((heads, HD, HD), BF16)],
        )
        return out, *relayed

    kept = {}

    part_w, w_a = lax.optimization_barrier((part_w, w_a))
    parts_w = spread(part_w)
    projected = project(0, w_a, table_a)
    ffn_in, ffn_out, _ = lax.optimization_barrier((ffn_in, ffn_out, projected[3]))
    f_a = ffn_joined(ffn_in, ffn_out)
    line.wait(f_a)
    *attended, part_f = attend(0, projected[0], projected[2], per_a, table_a, decay_rows_a, relay=(part_f,))
    parts_f = spread(part_f)
    decay_b, _ = lax.optimization_barrier((decay_b, attended[2]))
    w_b = assemble(*stacked(parts_w))
    table_b, decay_rows_b = token_table(decay_b)
    line.wait(per_b)
    qkv, gate, mem, inv, state = project(1, w_b, table_b, projected)

    def attend_other(*_):
        kept["att"] = attend(1, qkv, mem, per_b, table_b, decay_rows_b, attended)

    nothing = lambda: None
    state_in, *parts_f = scan(state, False, nothing, attend_other, parts_f)
    att, rec, logs = kept["att"]
    parts_f = stacked(parts_f)
    tables = jnp.stack([table_a, table_b])
    decay_rows = jnp.concatenate([decay_rows_a, decay_rows_b], axis=0)
    per_two = jnp.concatenate([per_a, per_b], axis=1)
    out_block = lambda w: (w, (width, cols), lambda i, s: (0, 7))

    half = steps // 2

    def half_in(a, part, n=None):
        return (a, (BLOCK, n or a.shape[1]), lambda i, s: (i + part * half, 0))

    def half_out(n, dtype, part):
        return ((seg, n), dtype, (BLOCK, n), lambda i, s: (i + part * half, 0))

    def half_batch(a, part):
        return (a, (1,) + blk, lambda i, s: (s[BATCH], i + part * half, 0))

    sent_half = ((seg // 2, width), BF16, blk, rows_map)

    def group_sum(part):
        got = [at.group(part, n) for n in range(1, at.nl)]
        total = got[0]
        for more in got[1:]:
            total = (total.astype(F32) + more.astype(F32)).astype(BF16)
        return total

    mixed, mixed_got, onto = [], [], ()
    for part in range(2):
        recalled, branch, mixed_part = run(
            mix_kernel,
            (half,),
            [half_in(a, part) for a in (att, rec, gate, mem, table_a, table_b)]
            + [full(state_in), out_block(w_a), out_block(w_b)],
            [half_out(2 * cols, F32, part), half_out(2 * cols, BF16, part), sent_half],
            placed=False,
            flops=seg * width * 2 * cols,
            onto=onto,
        )
        onto = (recalled, branch)
        mixed.append(mixed_part)
        mixed_got.append(group_sum(mixed_part))

    f_b = assemble(*parts_f)
    back, back_got, onto = [], [], ()
    for part in range(2):
        normed_t, cot_t, acts, *ffn_parts, back_part = run(
            ffn_kernel,
            (half,),
            [half_batch(stream, part), tiled(mixed[part]), tiled(mixed_got[part]), half_batch(cotangent, part)]
            + [gains_in, full(f_a), full(f_b)],
            [((width, seg), BF16, (width, BLOCK), lambda i, s, part=part: (0, i + part * half))] * 2
            + [half_out(6 * wide, BF16, part)]
            + [half_out(batches * col, BF16, part)] * at.nl
            + [sent_half],
            scratch=[pltpu.VMEM(blk, F32)],
            flops=seg * width * wide * 12,
            onto=onto,
        )
        onto = (normed_t, cot_t, acts, *ffn_parts)
        back.append(back_part)
        back_got.append(group_sum(back_part))
    chip_bits = [bit // 2 for bit in at.bits[1:]]
    orders = (list(reversed(chip_bits)), chip_bits)

    def exchange(parts, step):
        return [parts[0], parts[2]], [at.across(parts[2 * i + 1], 2 * orders[i][step]) for i in range(2)]

    def core_sum(keep_part, got):
        n = got.shape[2]
        there = lambda r, s: (s[last_place] ^ r, 0, 0)
        parts = run(
            functools.partial(core_sum_kernel, (orders[0][0], orders[1][0])),
            (chips,),
            [(a, (1, share, n), there) for a in (keep_part, got)],
            [fixed((chips // 2, share, n // 2), BF16)] * 4,
        )
        return exchange(parts, 0)

    def chip_step(keeps, gots, step):
        half_n = keeps[0].shape[2]
        ins = [full(a) for a in (*keeps, *gots)]
        if step == len(chip_bits):
            mine, theirs = run(
                functools.partial(chip_step_kernel, None),
                (1,),
                ins,
                [fixed((share, half_n)), fixed((share, half_n), BF16)],
                placed=False,
            )
            return mine, at.other(theirs)
        rests = []
        for order in orders:
            gone = sum(order[:step])
            held = [r for r in range(chips) if not r & gone]
            rests.append(tuple([i for i, r in enumerate(held) if bool(r & order[step]) == sent] for sent in (False, True)))
        parts = run(
            functools.partial(chip_step_kernel, rests),
            (1,),
            ins,
            [fixed((len(places), share, half_n), BF16) for rest in rests for places in rest],
            placed=False,
        )
        return exchange(parts, step)

    def middle_steps(sums):
        for step in range(1, len(chip_bits)):
            sums = chip_step(*sums, step)
        return sums

    def ffn_grads(left, count, chunk, onto=()):
        return run(
            ffn_grad_kernel,
            (count,),
            [full(left), (acts, (seg, wide), lambda i, s: (0, chunk(i)))],
            [((chips, share, 6 * wide), BF16, (chips, share, wide), lambda i, s: (0, 0, chunk(i)))] * 2,
            flops=2 * seg * width * wide * count,
            onto=onto,
        )

    half_f = ffn_grads(normed_t, 4, lambda i: i + i // 2)
    line.wait(back_got[0])
    keep_f, send_f = ffn_grads(cot_t, 2, lambda i: 3 * i + 2, half_f)
    gain_two, state_terms = jnp.zeros((8, width), F32), jnp.zeros((heads, HD + 8, HD), F32)
    onto = ()
    for part in range(2):
        grad_mid, grad_mix, grad_branch, grad_rec, grad_gate, gain_two, state_terms, *relayed = run(
            mid_back_kernel,
            (half,),
            [half_batch(stream, part)]
            + [tiled(a[part]) for a in (mixed, mixed_got, back, back_got)]
            + [half_batch(cotangent, part), gains_in, out_block(w_a), out_block(w_b)]
            + [half_in(a, part) for a in (gate, recalled, mem, table_a, table_b)]
            + [full(gain_two), full(state_terms)],
            [half_out(width, F32, part), half_out(width, BF16, part)]
            + [half_out(2 * cols, BF16, part)] * 3
            + [fixed((8, width)), fixed((heads, HD + 8, HD))],
            flops=seg * width * 2 * cols,
            onto=onto,
            relay=tuple(ffn_parts[1:]) if part == 0 else (),
        )
        if part == 0:
            ffn_shares = [ffn_parts[0]] + [at.group(a, r + 1) for r, a in enumerate(relayed)]
        onto = (grad_mid, grad_mix, grad_branch, grad_rec, grad_gate)

    def of_side(a):
        return (a, (1, *a.shape[1:]), lambda h, s: (jnp.minimum(h, heads - 1) // own, 0, 0))

    def of_head(a):
        return (a, (1, *a.shape[1:]), lambda h, s: (jnp.minimum(h, heads - 1), 0, 0))

    def head_block(a):
        return (a, (seg, HD), lambda h, s: (0, jnp.minimum(h, heads - 1)))

    def attend_back(side, onto=()):
        first = side * own
        return run(
            functools.partial(attend_back_kernel, scale),
            (own,),
            [head_cols(qkv, i, first) for i in range(3)]
            + [(grad_branch, (seg, HD), lambda h, s: (0, first + h))]
            + [(per_two, (persist, HD), lambda h, s: (0, first + h)), (per_two, (persist, HD), lambda h, s: (1, first + h))]
            + [(a, (1, seg, LANES), lambda h, s: (side, 0, 0)) for a in (tables, logs)],
            [
                ((seg, 6 * cols), BF16, (seg, 3 * cols), lambda h, s: (0, side)),
                ((heads, 2 * persist, HD), F32, (1, 2 * persist, HD), lambda h, s: (first + h, 0, 0)),
            ],
            scratch=[pltpu.VMEM((seg, HD), F32)] * 2,
            placed=False,
            flops=5 * pair_flops,
            trans=own * seg * seg * 0.6,
            onto=onto,
        )

    def during_scan(send_f):
        kept["f"] = at.across(send_f, 1)
        kept["back"] = attend_back(0)

    grad_state, send_f = scan(state_terms, True, nothing, during_scan, (send_f,))
    got_f = kept["f"]
    line.wait(*ffn_shares[1:])
    sums_f = core_sum(keep_f, got_f)


    def share_ins(arrays, side):
        return [(a, (BLOCK, col), lambda i, s: (i, lax.rem(s[BATCH] + side, batches))) for a in arrays]

    def wide_in(a, side):
        return (a, (BLOCK, col), lambda i, s: (i, lax.rem(s[BATCH] + side, batches) * at.nl + s[GROUP]))

    ins = []
    for side in range(2):
        ins.append(
            (
                stream,
                (1, BLOCK, col),
                lambda i, s, side=side: (s[BATCH], i, lax.rem(s[BATCH] + side, batches) * at.nl + s[GROUP]),
            )
        )
        ins += [
            (
                a,
                (BLOCK, col),
                lambda i, s, side=side, part=part: (
                    jnp.clip(i - part * half, 0, half - 1),
                    lax.rem(s[BATCH] + side, batches) * at.nl + s[GROUP],
                ),
            )
            for part in range(2)
            for a in (mixed[part], mixed_got[part])
        ] + share_ins(ffn_shares, side)
    result_mine, result_send, squares = run(
        functools.partial(result_kernel, at.nl),
        (steps,),
        ins,
        [out_rows(col, F32), out_rows(col, BF16), fixed((8, col))],
    )
    result_got = at.other(result_send)
    (dmem,) = run(
        memory_back_kernel,
        (heads,),
        [head_cols(mem, i) for i in range(3)]
        + [head_block(grad_rec), of_side(inv), of_side(tables), of_head(decay_rows), of_head(state_in), of_head(grad_state)],
        [fixed((seg, 6 * cols), BF16)],
        scratch=[pltpu.VMEM((seg, HD), F32)] * 2,
        flops=10 * pair_flops,
        trans=2 * own * seg * seg * 0.6,
        placed=False,
    )
    first_grad = dot(dmem[:8, : 3 * cols], w_a[:, 4 * cols : 7 * cols], ((1,), (1,))) + dot(
        dmem[:8, 3 * cols :], w_b[:, 4 * cols : 7 * cols], ((1,), (1,))
    )
    first_ages = (positions - starts)[:8, None]
    rim_back = jnp.zeros((8, width), F32)
    for tap in range(1, taps):
        term = jnp.where(first_ages >= tap, first_grad, 0.0)[:tap] * conv_weight[tap]
        rim_back = rim_back + jnp.pad(term, ((8 - tap, 0), (0, 0)))
    rim_back = at.along(rim_back, -1)

    sums_f = middle_steps(sums_f)
    line.wait(result_got)
    dqkv, per_grad = attend_back(1, kept["back"])
    f_mine, f_got = chip_step(*sums_f, len(chip_bits))
    line.wait(rim_back)
    span = max(2 * share, 256)
    pairs = span // (2 * share)
    left_in = lambda a: (a, (seg, span), lambda i, s: (0, i))
    keep_x, send_x = run(
        weight_grad_kernel,
        (width // span,),
        [left_in(normed), left_in(conv_out), left_in(grad_mix), full(dqkv), full(grad_gate), full(branch), full(dmem)],
        [((chips, share, 16 * cols), BF16, (pairs, share, 16 * cols), lambda i, s: (i, 0, 0))] * 2,
        flops=2 * seg * width * 16 * cols,
    )


    def placed(*parts):
        return run(placed_kernel, (1,), [full(a) for a in parts], [fixed((batches, seg, col))])[0]

    line.wait(f_got)
    result = placed(result_mine, result_got)
    got_x = at.across(lax.optimization_barrier((send_x, result))[0], 1)
    weights_in = lambda w: (w, (width, 7 * cols), lambda i, s: (0, 0))
    turned = lambda i, s: (steps - 1 - i, 0)
    turn = lambda a: (a, (BLOCK, a.shape[1]), turned)
    gain_one, grad_conv, *in_parts = run(
        in_back_kernel,
        (steps,),
        [
            (stream, (1,) + blk, lambda i, s: (s[BATCH], steps - 1 - i, 0)),
            full(normed), full(rim_rows), turn(table_a), gains_in, taps_in, full(rim_back),
        ]
        + [turn(a) for a in (dqkv, grad_gate, dmem)]
        + [weights_in(w_a), weights_in(w_b)],
        [fixed((8, width))] * 2 + [((seg, batches * col), BF16, (BLOCK, batches * col), turned)] * at.nl,
        scratch=[pltpu.VMEM((8, width), F32), pltpu.VMEM(blk, F32)],
        flops=2 * seg * width * 14 * cols,
    )
    in_shares = [in_parts[0]] + [at.group(a, r) for r, a in enumerate(in_parts) if r > 0]
    sums_x = core_sum(keep_x, got_x)

    small = jnp.concatenate(
        [
            gain_one[:1], gain_two[:1] / at.nl, grad_conv[:taps],
            jnp.pad(jnp.sum(squares[:4], axis=-1), (0, width - 4))[None],
            per_grad.reshape(-1, width),
        ],
        axis=0,
    )
    small = jnp.pad(small, ((0, -small.shape[0] % 8), (0, 0)))

    def added(parts):
        return run(add_kernel, (1,), [full(a) for a in parts], [fixed(parts[0].shape)], placed=False)[0]

    small_got = at.across(small, 1)
    small = added([small, small_got])

    ins = []
    for side in range(2):
        ins += [wide_in(grad_mid, side)] + share_ins(in_shares, side)
    stream_mine, stream_send = run(
        functools.partial(stream_grad_kernel, at.nl), (steps,), ins, [out_rows(col, F32), out_rows(col, BF16)]
    )
    stream_got = at.other(stream_send)
    sums_x = middle_steps(sums_x)
    line.wait(stream_got)
    grad_ffn_in, grad_ffn_out = run(
        functools.partial(final_ffn_kernel, hidden),
        (1,),
        [full(f_mine), full(f_got)],
        [fixed((share, 2, hidden)), fixed((hidden, share))],
        placed=False,
    )
    x_mine, x_got = chip_step(*sums_x, len(chip_bits))
    for bit in at.bits[1:-1]:
        small = added([small, at.across(small, bit)])
    small = added([small, at.across(small, at.bits[-1])])
    head_parts = [small] + [
        lax.ppermute(small, "head", [(i, (i + n) % at.nz) for i in range(at.nz)]) for n in range(1, at.nz)
    ]
    grad_stream = placed(stream_mine, stream_got)
    grad_mixer_in, grad_memory_in, grad_mixer_out = run(
        final_mixer_kernel,
        (1,),
        [full(x_mine), full(x_got)],
        [fixed((share, 4, cols)), fixed((share, 3, cols)), fixed((cols, share))],
        placed=False,
    )

    sums = sum(a[: 3 + taps] for a in head_parts[1:]) + small[: 3 + taps]
    rows_p = persistent.shape[0] // at.ns

    def persist_rows(a):
        a = a[3 + taps : 3 + taps + heads * 2 * persist * HD // width].reshape(heads, 2 * persist, HD)
        a = lax.dynamic_slice_in_dim(a, at.seq * rows_p, rows_p, 1)
        return jnp.transpose(a, (1, 0, 2)).reshape(rows_p, -1)

    grad_persistent = persist_rows(small)[:, :cols] + persist_rows(head_parts[at.nl])[:, cols:]
    cells = float(batches * seg * at.ns * width)
    rms_values = jnp.sqrt(sums[2 + taps, :4] / cells)
    return (
        result,
        grad_stream,
        grad_mixer_in,
        grad_memory_in,
        grad_mixer_out,
        grad_ffn_in,
        grad_ffn_out,
        grad_persistent,
        sums[:2],
        sums[2 : 2 + taps],
        rms_values,
    )


def solution(mesh):
    placed = (
        P(None, "seq", None),
        P(None, "seq", None),
        P(None, None, "head"),
        P(None, None, "head"),
        P("head", None),
        P(None, None, "head"),
        P("head", None),
        P(None, "head"),
        P(),
        P(),
        P(None, "head", "seq"),
        P(),
    )
    return jax.shard_map(
        local,
        mesh=mesh,
        in_specs=placed,
        out_specs=(
            P(None, "seq", "head"),
            P(None, "seq", "head"),
            P("seq", None, "head"),
            P("seq", None, "head"),
            P("head", "seq"),
            P("seq", None, "head"),
            P("head", "seq"),
            P("seq", "head"),
            P(),
            P(),
            P(),
        ),
        check_vma=False,
    )
```

```python
import functools
import math

import jax
import jax.numpy as jnp
from jax import lax
from jax.experimental import pallas as pl
from jax.experimental.pallas import tpu as pltpu
from jax.sharding import PartitionSpec as P

HD = 128
EPS = 1e-06
F32 = jnp.float32
BF16 = jnp.bfloat16


def dot(a, b, dims):
    return lax.dot_general(a, b, (dims, ((), ())), preferred_element_type=F32)


class Place:
    def __init__(self, batches):
        self.ns = lax.axis_size("seq")
        self.nz = lax.axis_size("head")
        self.nl = self.nz // batches
        self.seq = lax.axis_index("seq")
        self.z = lax.axis_index("head")
        self.p = self.z // self.nl
        self.l = self.z % self.nl
        self.bits = [1 << i for i in range(self.ns.bit_length() - 1)]

    def across(self, value, bit):
        return lax.ppermute(value, "seq", [(i, i ^ bit) for i in range(self.ns)])

    def along(self, value, steps):
        first, last = max(0, -steps), min(self.ns, self.ns - steps)
        return lax.ppermute(value, "seq", [(i, i + steps) for i in range(first, last)])

    def other(self, value):
        return lax.ppermute(value, "head", [(i, (i + self.nl) % self.nz) for i in range(self.nz)])

    def group(self, value, steps):
        nl = self.nl
        return lax.ppermute(
            value,
            "head",
            [(i, i // nl * nl + (i % nl + steps) % nl) for i in range(self.nz)],
        )

    def bit_of(self, bit):
        return (self.seq // bit) % 2


LOG2E = 1.4426950408889634
BLOCK = 256
LANES = 128
BATCH, GROUP, CORE, CHIP = 0, 1, 2, 3
DECAY, INFLOW, KEEP, START, AGE = 0, 4, 8, 12, 13


def in_hbm(a):
    if math.prod(a.shape) * jnp.dtype(a.dtype).itemsize < 2**21:
        return a
    return pltpu.with_memory_space_constraint(a, pltpu.HBM)


class Line:
    def __init__(self, place):
        self.place = place
        self.waits = []
        self.last = None

    def wait(self, *arrays):
        self.waits += arrays

    def run(self, kernel, grid, ins, outs, scratch=(), flops=0, trans=0, onto=(), relay=(), placed=True):
        moved = sum(a.size * a.dtype.itemsize for a, _, _ in ins)
        moved += sum(math.prod(s) * jnp.dtype(d).itemsize for s, d, _, _ in outs)
        blocks = sum(2 * math.prod(b) * a.dtype.itemsize for a, b, _ in ins if b is not None)
        blocks += sum(2 * math.prod(b) * jnp.dtype(d).itemsize for _, d, b, _ in outs)
        blocks += sum(math.prod(a.shape) * jnp.dtype(a.dtype).itemsize for a in scratch)
        waits, self.waits = self.waits, []
        if self.last is not None and not any(self.last is a for a in (*[a for a, _, _ in ins], *onto, *relay, *waits)):
            waits = [*waits, self.last]
        extra = (*onto, *relay, *waits)
        n_ins, n_outs, lead = len(ins), len(outs), 1 if placed else 0

        def body(*refs):
            place_ref, refs = (refs[0] if placed else None), refs[lead:]
            inputs, outputs = refs[:n_ins], refs[n_ins + len(extra) : n_ins + len(extra) + n_outs]
            kernel(place_ref, *inputs, *outputs, *refs[n_ins + len(extra) + n_outs + len(relay) :])

        def mapped(index_map):
            return index_map if placed else lambda *at: index_map(*at, None)

        anywhere = pl.BlockSpec(memory_space=pl.ANY)
        spec = pltpu.PrefetchScalarGridSpec(
            num_scalar_prefetch=lead,
            grid=grid,
            in_specs=[
                pl.BlockSpec(memory_space=pltpu.VMEM) if b is None else pl.BlockSpec(b, mapped(m)) for _, b, m in ins
            ]
            + [anywhere] * len(extra),
            out_specs=[pl.BlockSpec(b, mapped(m)) for _, _, b, m in outs] + [anywhere] * len(relay),
            scratch_shapes=list(scratch),
        )
        aliases = {lead + n_ins + i: i for i in range(len(onto))}
        aliases |= {lead + n_ins + len(onto) + i: n_outs + i for i in range(len(relay))}
        got = pl.pallas_call(
            body,
            grid_spec=spec,
            out_shape=[jax.ShapeDtypeStruct(s, d) for s, d, _, _ in outs]
            + [jax.ShapeDtypeStruct(a.shape, a.dtype) for a in relay],
            input_output_aliases=aliases,
            compiler_params=pltpu.CompilerParams(
                dimension_semantics=("arbitrary",) * len(grid), vmem_limit_bytes=blocks + 8 * 2**20
            ),
            cost_estimate=pl.CostEstimate(flops=int(flops), bytes_accessed=int(moved), transcendentals=int(trans)),
        )(*((self.place,) if placed else ()), *[a if b is None else in_hbm(a) for a, b, _ in ins], *map(in_hbm, onto), *extra[len(onto) :])
        self.last = min(got[:n_outs], key=lambda a: a.size * a.dtype.itemsize)
        return got


def rows_map(i, *_):
    return (i, 0)


def whole(rank):
    return lambda *_: (0,) * rank


def column(table, index):
    return table[:, index : index + 1]


def pick_column(table, index):
    lane = lax.broadcasted_iota(jnp.int32, table.shape, 1)
    return jnp.sum(jnp.where(lane == index, table, 0.0), axis=-1, keepdims=True)


def norm_conv_kernel(p_ref, x_ref, gain_ref, rim_ref, table_ref, taps_ref, normed_ref, conv_ref, tail):
    x = x_ref[0]
    inv = lax.rsqrt(jnp.mean(x * x, axis=-1, keepdims=True) + EPS)
    normed = (x * inv * gain_ref[0:1]).astype(BF16)
    normed_ref[...] = normed
    wide = normed.astype(F32)

    @pl.when(pl.program_id(0) == 0)
    def _():
        tail[...] = rim_ref[...].astype(F32)

    ext = jnp.concatenate([tail[...], wide], axis=0)
    age = column(table_ref[...], 0)
    total = wide * taps_ref[0:1]
    for tap in range(1, taps_ref.shape[0]):
        back = pltpu.roll(ext, tap, 0)[8:]
        total = total + jnp.where(age >= tap, back, 0.0) * taps_ref[tap : tap + 1]
    conv_ref[...] = total.astype(BF16)
    tail[...] = wide[-8:]


def project_kernel(place, x_ref, c_ref, w_ref, table_ref, qkv_ref, gate_ref, mem_ref, inv_ref, state_ref):
    cols = gate_ref.shape[1]
    count = cols // HD
    proj = dot(x_ref[...], w_ref[:, : 4 * cols], ((1,), (0,)))
    qkv_ref[...] = proj[:, : 3 * cols].astype(BF16)
    gate_ref[...] = jax.nn.sigmoid(proj[:, 3 * cols :])
    mem = dot(c_ref[...], w_ref[:, 4 * cols : 7 * cols], ((1,), (0,)))
    lane = lax.broadcasted_iota(jnp.int32, inv_ref.shape[1:], 1)
    invs = jnp.zeros(inv_ref.shape[1:], F32)
    units = []
    for i in range(2 * count):
        raw = mem[:, i * HD : (i + 1) * HD]
        inv = lax.rsqrt(jnp.sum(raw * raw, axis=-1, keepdims=True) + EPS)
        units.append((raw * inv).astype(BF16))
        mem_ref[:, i * HD : (i + 1) * HD] = units[-1]
        invs = jnp.where(lane == i, inv, invs)
    inv_ref[0] = invs
    value = mem[:, 2 * cols :].astype(BF16)
    mem_ref[:, 2 * cols :] = value

    @pl.when(pl.program_id(0) == 0)
    def _():
        state_ref[...] = jnp.zeros_like(state_ref)

    table = table_ref[...]
    for h in range(count):
        kept = (units[count + h].astype(F32) * column(table, KEEP + h)).astype(BF16)
        state_ref[h, :HD] += dot(kept, value[:, h * HD : (h + 1) * HD], ((0,), (0,)))
        carry = column(table, INFLOW + h)[-8:]
        state_ref[h, HD:] = jnp.broadcast_to(carry[7:8], (8, HD))


def joined(early, late):
    state = early[:, :HD] * late[:, HD : HD + 1] + late[:, :HD]
    return jnp.concatenate([state, early[:, HD:] * late[:, HD:]], axis=1)


def pair_scan_kernel(reverse, place, mine_ref, got_ref, out_ref):
    mine, got = mine_ref[...], got_ref[...]
    high = (place[CORE] == 1) ^ reverse
    out_ref[...] = joined(jnp.where(high, got, mine), jnp.where(high, mine, got))


def chip_scan_kernel(reverse, chips, place, got_ref, *refs):
    pairs, out_ref = refs[:-1], refs[-1]
    here = place[place.shape[0] - 1]
    total = None
    for step in range(chips):
        chip = chips - 1 - step if reverse else step
        away = here ^ chip
        block = pairs[0][...]
        for r in range(1, chips):
            block = jnp.where(away == r, pairs[r][...], block)
        before = chip > here if reverse else chip < here
        row = lax.broadcasted_iota(jnp.int32, block.shape, 1)
        block = jnp.where(before, block, jnp.where(row < HD, 0.0, 1.0))
        total = block if total is None else joined(total, block)
    high = (place[CORE] == 1) ^ reverse
    total = jnp.where(high, joined(total, got_ref[...]), total)
    out_ref[...] = total[:, :HD].astype(BF16)


def add_kernel(place, *refs):
    total = refs[0][...]
    for part in refs[1:-1]:
        total = total + part[...]
    refs[-1][...] = total


def stack_kernel(place, *refs):
    for i, ref in enumerate(refs[:-1]):
        refs[-1][i] = ref[...]


def assemble_kernel(place, mine_ref, theirs_ref, out_ref):
    share = mine_ref.shape[1]
    first = place[CORE] == 0
    mine, theirs = mine_ref[0], theirs_ref[0]
    out_ref[0, :share] = jnp.where(first, mine, theirs)
    out_ref[0, share:] = jnp.where(first, theirs, mine)


def parted(chips, bit):
    return [r for r in range(chips) if not r & bit], [r for r in range(chips) if r & bit]


def core_sum_kernel(bits, place, keep_ref, got_ref, *outs):
    total = keep_ref[0].astype(F32) + got_ref[0].astype(F32)
    half = total.shape[1] // 2
    for side, bit in enumerate(bits):
        part = total[:, side * half : (side + 1) * half].astype(BF16)
        for out, rs in zip(outs[2 * side : 2 * side + 2], parted(2 * outs[0].shape[0], bit)):
            for i, r in enumerate(rs):

                @pl.when(pl.program_id(0) == r)
                def _():
                    out[i] = part


def chip_step_kernel(rests, place, *refs):
    keeps, gots, outs = refs[:2], refs[2:4], refs[4:]
    for side, (keep, got) in enumerate(zip(keeps, gots)):
        total = [keep[i].astype(F32) + got[i].astype(F32) for i in range(keep.shape[0])]
        if rests is None:
            outs[side][...] = total[0].astype(outs[side].dtype)
            continue
        for out, places in zip(outs[2 * side : 2 * side + 2], rests[side]):
            for i, at in enumerate(places):
                out[i] = total[at].astype(BF16)


def split_columns(place, held, outs):
    batches = 2
    col = outs[0].shape[1] // batches
    group = len(outs)
    for r, out in enumerate(outs):
        target = lax.rem(place[GROUP] + r, group)
        for b in range(batches):
            first = pl.multiple_of((b * group + target) * col, col)
            out[:, b * col : (b + 1) * col] = held[:, pl.ds(first, col)].astype(BF16)


def result_kernel(parts, place, *refs):
    mine_ref, send_ref, squares = refs[-3:]

    @pl.when(pl.program_id(0) == 0)
    def _():
        squares[...] = jnp.zeros_like(squares)

    for side, out in enumerate((mine_ref, send_ref)):
        x_ref, m_a, m_b, n_a, n_b, *shares = refs[side * (5 + parts) : (side + 1) * (5 + parts)]
        x = x_ref[0]
        early = pl.program_id(0) < pl.num_programs(0) // 2
        mixed = jnp.where(early, m_a[...].astype(F32) + m_b[...].astype(F32), n_a[...].astype(F32) + n_b[...].astype(F32))
        ffn = shares[0][...].astype(F32)
        for share in shares[1:]:
            ffn = ffn + share[...].astype(F32)
        result = x + mixed + ffn
        for i, a in enumerate((x, mixed, ffn, result)):
            squares[i : i + 1] += jnp.sum(a * a, axis=0, keepdims=True)
        out[...] = result.astype(out.dtype)


def stream_grad_kernel(parts, place, *refs):
    mine_ref, send_ref = refs[-2:]
    for side, out in enumerate((mine_ref, send_ref)):
        mid, *shares = refs[side * (1 + parts) : (side + 1) * (1 + parts)]
        total = mid[...]
        for share in shares:
            total = total + share[...].astype(F32)
        out[...] = total.astype(out.dtype)


def allowed_block(table, first, rows, count):
    start = column(table, START)[first : first + rows].astype(jnp.int32)
    col = lax.broadcasted_iota(jnp.int32, (rows, count), 1)
    row = lax.broadcasted_iota(jnp.int32, (rows, count), 0) + first
    return (col >= start) & (col <= row)


def attend_kernel(
    scale, place, q_ref, k_ref, v_ref, mq_ref, mk_ref, mv_ref, pk_ref, pv_ref, table_ref, decay_ref,
    att_ref, rec_ref, log_ref,
):
    h = pl.program_id(0)
    seg = q_ref.shape[0]
    table = table_ref[0]
    down = pick_column(table, DECAY + h)
    across = decay_ref[0]
    lane = lax.broadcasted_iota(jnp.int32, (BLOCK, LANES), 1)
    pk, pv = pk_ref[...], pv_ref[...]
    for first in range(0, seg, BLOCK):
        rows, end = slice(first, first + BLOCK), first + BLOCK
        ok = allowed_block(table, first, BLOCK, end)
        query = q_ref[rows]
        s = jnp.where(ok, dot(query, k_ref[:end], ((1,), (1,))) * (scale * LOG2E), -1e30)
        ps = dot(query, pk, ((1,), (1,))) * (scale * LOG2E)
        top = jnp.maximum(jnp.max(s, axis=-1, keepdims=True), jnp.max(ps, axis=-1, keepdims=True))
        e, pe = jnp.exp2(s - top), jnp.exp2(ps - top)
        total = jnp.sum(e, axis=-1, keepdims=True) + jnp.sum(pe, axis=-1, keepdims=True)
        att = dot(e.astype(BF16), v_ref[:end], ((1,), (0,))) + dot(pe.astype(BF16), pv, ((1,), (0,)))
        att_ref[rows] = att / total
        logs = top + jnp.log2(total)
        before = jnp.where(h == 0, 0.0, log_ref[0, rows])
        log_ref[0, rows] = jnp.where(lane == h, logs, before)
        w = dot(mq_ref[rows], mk_ref[:end], ((1,), (1,)))
        grid = jnp.exp2(jnp.minimum(down[rows] - across[:, :end], 0.0))
        w = jnp.where(ok, w * grid, 0.0).astype(BF16)
        rec_ref[rows] = dot(w, mv_ref[:end], ((1,), (0,)))


def mix_kernel(
    place, att_ref, rec_ref, gate_ref, mem_ref, table_a, table_b, state_ref, out_a, out_b,
    recalled_ref, branch_ref, mixed_ref,
):
    cols = out_a.shape[1]
    count = cols // HD
    mixed = None
    for side, (table_ref, out) in enumerate(((table_a, out_a), (table_b, out_b))):
        table = table_ref[...]
        for h in range(count):
            query = mem_ref[:, (3 * side * count + h) * HD : (3 * side * count + h + 1) * HD]
            inward = (query.astype(F32) * column(table, INFLOW + h)).astype(BF16)
            here = slice((side * count + h) * HD, (side * count + h + 1) * HD)
            recalled = rec_ref[:, here] + dot(inward, state_ref[side * count + h], ((1,), (0,)))
            recalled_ref[:, here] = recalled
            branch_ref[:, here] = (att_ref[:, here] + gate_ref[:, here] * recalled).astype(BF16)
        part = dot(branch_ref[:, side * cols : (side + 1) * cols], out[...], ((1,), (1,)))
        mixed = part if mixed is None else mixed + part
    mixed_ref[...] = mixed.astype(BF16)


def ffn_kernel(place, x_ref, m_a, m_b, cot_ref, gain_ref, w_a, w_b, normed_ref, cot_out, acts_ref, *outs):
    outs, back_ref, held = outs[:-2], outs[-2], outs[-1]
    middle = x_ref[0] + m_a[...].astype(F32) + m_b[...].astype(F32)
    inv = lax.rsqrt(jnp.mean(middle * middle, axis=-1, keepdims=True) + EPS)
    normed = (middle * inv * gain_ref[1:2]).astype(BF16)
    normed_ref[...] = normed.T
    grad_ffn = cot_ref[0].astype(BF16)
    cot_out[...] = grad_ffn.T
    n = w_a.shape[1] // 3
    part, back = None, None
    for side, w in enumerate((w_a, w_b)):
        pair = dot(normed, w[:, : 2 * n], ((1,), (0,)))
        pre, up = pair[:, :n], pair[:, n:]
        grad_hidden = dot(grad_ffn, w[:, 2 * n :], ((1,), (0,)))
        sig = jax.nn.sigmoid(pre)
        silu = pre * sig
        hidden = (silu * up).astype(BF16)
        slope = sig + silu * (1.0 - sig)
        grad_pre = (grad_hidden * up * slope).astype(BF16)
        grad_up = (grad_hidden * silu).astype(BF16)
        grad_pair = jnp.concatenate([grad_pre, grad_up], axis=1)
        acts_ref[:, 3 * side * n : (3 * side + 2) * n] = grad_pair
        acts_ref[:, (3 * side + 2) * n : (3 * side + 3) * n] = hidden
        one = dot(hidden, w[:, 2 * n :], ((1,), (1,)))
        two = dot(grad_pair, w[:, : 2 * n], ((1,), (1,)))
        part = one if part is None else part + one
        back = two if back is None else back + two
    held[...] = part
    split_columns(place, held, outs)
    back_ref[...] = back.astype(BF16)


def mid_back_kernel(
    place, x_ref, m_a, m_b, g_a, g_b, cot_ref, gain_ref, out_a, out_b, gate_in, recalled_ref, mem_ref,
    table_a, table_b, gain_in, state_in, mid_ref, mix_ref, branch_ref, rec_ref, gate_ref, gain_out, state_ref,
):
    @pl.when(pl.program_id(0) == 0)
    def _():
        gain_out[...] = gain_in[...]
        state_ref[...] = state_in[...]

    middle = x_ref[0] + m_a[...].astype(F32) + m_b[...].astype(F32)
    inv = lax.rsqrt(jnp.mean(middle * middle, axis=-1, keepdims=True) + EPS)
    hat = middle * inv
    grad = g_a[...].astype(F32) + g_b[...].astype(F32)
    scaled = grad * gain_ref[1:2]
    grad_mid = inv * (scaled - hat * jnp.mean(scaled * hat, axis=-1, keepdims=True)) + cot_ref[0]
    gain_out[0:1] += jnp.sum(grad * hat, axis=0, keepdims=True)
    mid_ref[...] = grad_mid
    mix = grad_mid.astype(BF16)
    mix_ref[...] = mix
    cols = out_a.shape[1]
    count = cols // HD
    for side, (out, table_ref) in enumerate(((out_a, table_a), (out_b, table_b))):
        table = table_ref[...]
        here = slice(side * cols, (side + 1) * cols)
        branch = dot(mix, out[...], ((1,), (0,))).astype(BF16)
        branch_ref[:, here] = branch
        wide = branch.astype(F32)
        gate = gate_in[:, here]
        rec = (wide * gate).astype(BF16)
        rec_ref[:, here] = rec
        gate_ref[:, here] = (wide * recalled_ref[:, here] * gate * (1.0 - gate)).astype(BF16)
        for h in range(count):
            query = mem_ref[:, (3 * side * count + h) * HD : (3 * side * count + h + 1) * HD]
            inward = (query.astype(F32) * column(table, INFLOW + h)).astype(BF16)
            state_ref[side * count + h, :HD] += dot(inward, rec[:, h * HD : (h + 1) * HD], ((0,), (0,)))
            carry = column(table, INFLOW + h)[-8:]
            state_ref[side * count + h, HD:] = jnp.broadcast_to(carry[7:8], (8, HD))


def side_columns(head, own):
    first = head // own * 3 * own + lax.rem(head, own)
    return [pl.ds(pl.multiple_of((first + part * own) * HD, HD), HD) for part in range(3)]


def attend_back_kernel(
    scale, place, q_ref, k_ref, v_ref, g_ref, pk_ref, pv_ref, table_ref, log_ref,
    out_ref, dper_ref, dk_sum, dv_sum,
):
    h = pl.program_id(0)
    own = pl.num_programs(0)
    seg = q_ref.shape[0]
    table = table_ref[0]
    logs = pick_column(log_ref[0], h)
    dq_at, dk_at, dv_at = side_columns(h, own)
    pk, pv = pk_ref[...], pv_ref[...]
    persist = pk.shape[0]
    dk_sum[...] = jnp.zeros_like(dk_sum)
    dv_sum[...] = jnp.zeros_like(dv_sum)
    dpk = jnp.zeros(pk.shape, F32)
    dpv = jnp.zeros(pv.shape, F32)
    for first in range(0, seg, BLOCK):
        rows, end = slice(first, first + BLOCK), first + BLOCK
        ok = allowed_block(table, first, BLOCK, end)
        query, grad = q_ref[rows], g_ref[rows]
        s = dot(query, k_ref[:end], ((1,), (1,))) * (scale * LOG2E)
        p = jnp.where(ok, jnp.exp2(s - logs[rows]), 0.0)
        pp = jnp.exp2(dot(query, pk, ((1,), (1,))) * (scale * LOG2E) - logs[rows])
        dp = dot(grad, v_ref[:end], ((1,), (1,)))
        dpp = dot(grad, pv, ((1,), (1,)))
        delta = jnp.sum(p * dp, axis=-1, keepdims=True) + jnp.sum(pp * dpp, axis=-1, keepdims=True)
        ds = (p * (dp - delta)).astype(BF16)
        dps = (pp * (dpp - delta)).astype(BF16)
        dq = dot(ds, k_ref[:end], ((1,), (0,))) + dot(dps, pk, ((1,), (0,)))
        out_ref[rows, dq_at] = (scale * dq).astype(BF16)
        dk_sum[:end] += dot(ds, query, ((0,), (0,)))
        dv_sum[:end] += dot(p.astype(BF16), grad, ((0,), (0,)))
        dpk = dpk + dot(dps, query, ((0,), (0,)))
        dpv = dpv + dot(pp.astype(BF16), grad, ((0,), (0,)))
    out_ref[:, dk_at] = (scale * dk_sum[...]).astype(BF16)
    out_ref[:, dv_at] = dv_sum[...].astype(BF16)
    dper_ref[0, :persist] = scale * dpk
    dper_ref[0, persist:] = dpv


def unit_grad(unit, inv, grad):
    unit = unit.astype(F32)
    return inv * (grad - unit * jnp.sum(unit * grad, axis=-1, keepdims=True))


def memory_back(
    head, count, mq_ref, mk_ref, mv_ref, g_ref, inv_ref, table_ref, decay_ref, state_ref, gstate_ref,
    out_ref, dk_sum, dv_sum,
):
    h = lax.rem(head, count)
    dq_at, dk_at, dv_at = side_columns(head, count)
    seg = mq_ref.shape[0]
    table = table_ref[0]
    invs = inv_ref[0]
    down = pick_column(table, DECAY + h)
    inflow = pick_column(table, INFLOW + h)
    keep = pick_column(table, KEEP + h)
    query_inv, key_inv = pick_column(invs, h), pick_column(invs, count + h)
    across = decay_ref[0]
    state, gstate = state_ref[0], gstate_ref[0]
    dk_sum[...] = jnp.zeros_like(dk_sum)
    dv_sum[...] = jnp.zeros_like(dv_sum)
    for first in range(0, seg, BLOCK):
        rows, end = slice(first, first + BLOCK), first + BLOCK
        ok = allowed_block(table, first, BLOCK, end)
        query, grad = mq_ref[rows], g_ref[rows]
        grid = jnp.where(ok, jnp.exp2(jnp.minimum(down[rows] - across[:, :end], 0.0)), 0.0)
        w = (dot(query, mk_ref[:end], ((1,), (1,))) * grid).astype(BF16)
        dw = (dot(grad, mv_ref[:end], ((1,), (1,))) * grid).astype(BF16)
        dq = dot(dw, mk_ref[:end], ((1,), (0,))) + inflow[rows] * dot(grad, state, ((1,), (1,)))
        out_ref[rows, dq_at] = unit_grad(query, query_inv[rows], dq).astype(BF16)
        dk_sum[:end] += dot(dw, query, ((0,), (0,)))
        dv_sum[:end] += dot(w, grad, ((0,), (0,)))
    key, value = mk_ref[...], mv_ref[...]
    dk = dk_sum[...] + keep * dot(value, gstate, ((1,), (1,)))
    out_ref[:, dk_at] = unit_grad(key, key_inv, dk).astype(BF16)
    kept = (key.astype(F32) * keep).astype(BF16)
    out_ref[:, dv_at] = (dv_sum[...] + dot(kept, gstate, ((1,), (0,)))).astype(BF16)


def in_back_kernel(
    place, x_ref, normed_ref, rim_ref, table_ref, gain_ref, taps_ref, rim_grad_ref,
    dqkv_ref, gate_ref, dmem_ref, w_a, w_b, gain_out, taps_out, *outs,
):
    outs, carried, held = outs[:-2], outs[-2], outs[-1]
    step = pl.program_id(0)
    block = pl.num_programs(0) - 1 - step
    rows = x_ref.shape[1]
    cols = gate_ref.shape[1] // 2
    taps = taps_ref.shape[0]

    @pl.when(step == 0)
    def _():
        gain_out[...] = jnp.zeros_like(gain_out)
        taps_out[...] = jnp.zeros_like(taps_out)
        carried[...] = rim_grad_ref[...]

    mix_a = jnp.concatenate([dqkv_ref[:, : 3 * cols], gate_ref[:, :cols]], axis=1)
    mix_b = jnp.concatenate([dqkv_ref[:, 3 * cols :], gate_ref[:, cols:]], axis=1)
    conv_grad = dot(dmem_ref[:, : 3 * cols], w_a[:, 4 * cols : 7 * cols], ((1,), (1,)))
    conv_grad = conv_grad + dot(dmem_ref[:, 3 * cols :], w_b[:, 4 * cols : 7 * cols], ((1,), (1,)))
    grad = dot(mix_a, w_a[:, : 4 * cols], ((1,), (1,))) + dot(mix_b, w_b[:, : 4 * cols], ((1,), (1,)))
    normed = normed_ref[pl.ds(pl.multiple_of(block * rows, rows), rows)].astype(F32)
    before = normed_ref[pl.ds(pl.multiple_of(jnp.maximum(block * rows - 16, 0), 16), 16)].astype(F32)[8:]
    before = jnp.where(block == 0, rim_ref[...].astype(F32), before)
    ext = jnp.concatenate([before, normed], axis=0)
    age = column(table_ref[...], AGE)
    taps_out[0:1] += jnp.sum(conv_grad * normed, axis=0, keepdims=True)
    grad = grad + conv_grad * taps_ref[0:1]
    spread = jnp.zeros((rows + 8, x_ref.shape[2]), F32)
    zeros = jnp.zeros((8, x_ref.shape[2]), F32)
    for tap in range(1, taps):
        masked = jnp.where(age >= tap, conv_grad, 0.0)
        taps_out[tap : tap + 1] += jnp.sum(masked * pltpu.roll(ext, tap, 0)[8:], axis=0, keepdims=True)
        term = jnp.concatenate([zeros, masked * taps_ref[tap : tap + 1]], axis=0)
        spread = spread + pltpu.roll(term, rows + 8 - tap, 0)
    grad = grad + spread[8:]
    grad = jnp.concatenate([grad[: rows - 8], grad[rows - 8 :] + carried[...]], axis=0)
    carried[...] = spread[:8]
    x = x_ref[0]
    inv = lax.rsqrt(jnp.mean(x * x, axis=-1, keepdims=True) + EPS)
    hat = x * inv
    scaled = grad * gain_ref[0:1]
    held[...] = inv * (scaled - hat * jnp.mean(scaled * hat, axis=-1, keepdims=True))
    split_columns(place, held, outs)
    gain_out[0:1] += jnp.sum(grad * hat, axis=0, keepdims=True)


def put_grad(place, grad, keep_ref, keep_at, sends):
    mine = place[CORE] == 0
    share = keep_ref.shape[1]
    grad = grad.astype(BF16)
    n = grad.shape[1]
    wide = sends[0].shape[2]
    for i in range(grad.shape[0] // (2 * share)):
        low = grad[2 * i * share : (2 * i + 1) * share]
        high = grad[(2 * i + 1) * share : (2 * i + 2) * share]
        keep_ref[i, :, keep_at : keep_at + n] = jnp.where(mine, low, high)
        send = jnp.where(mine, high, low)
        for first in range(keep_at // wide * wide, keep_at + n, wide):
            low_at, high_at = max(first, keep_at), min(first + wide, keep_at + n)
            sends[first // wide][i, :, low_at - first : high_at - first] = send[:, low_at - keep_at : high_at - keep_at]


def memory_back_kernel(place, *refs):
    memory_back(pl.program_id(0), pl.num_programs(0) // 2, *refs)


def weight_grad_kernel(
    place, normed_ref, conv_ref, mix_ref, dqkv_ref, gate_ref, branch_ref, dmem_ref, keep_ref, send_ref
):
    cols = gate_ref.shape[1] // 2
    sends = [send_ref]
    normed, conv, mix = normed_ref[...].T, conv_ref[...].T, mix_ref[...].T
    for side in range(2):
        one, three = slice(side * cols, (side + 1) * cols), slice(3 * side * cols, 3 * (side + 1) * cols)
        first = 8 * side * cols
        put_grad(place, dot(normed, dqkv_ref[:, three], ((1,), (0,))), keep_ref, first, sends)
        put_grad(place, dot(normed, gate_ref[:, one], ((1,), (0,))), keep_ref, first + 3 * cols, sends)
        put_grad(place, dot(mix, branch_ref[:, one], ((1,), (0,))), keep_ref, first + 4 * cols, sends)
        put_grad(place, dot(conv, dmem_ref[:, three], ((1,), (0,))), keep_ref, first + 5 * cols, sends)


def final_ffn_kernel(hidden, place, mine_ref, got_ref, in_ref, out_ref):
    total = mine_ref[...] + got_ref[...].astype(F32)
    wide = total.shape[1] // 3
    in_ref[:, 0, :] = total[:, :hidden]
    in_ref[:, 1, :] = total[:, wide : wide + hidden]
    out_ref[...] = total[:, 2 * wide :].T[:hidden]


def final_mixer_kernel(place, mine_ref, got_ref, mixer_ref, memory_ref, out_ref):
    total = mine_ref[...] + got_ref[...].astype(F32)
    cols = total.shape[1] // 8
    for i in range(4):
        mixer_ref[:, i, :] = total[:, i * cols : (i + 1) * cols]
    for i in range(3):
        memory_ref[:, i, :] = total[:, (5 + i) * cols : (6 + i) * cols]
    out_ref[...] = total[:, 4 * cols : 5 * cols].T


def placed_kernel(place, *refs):
    parts, out_ref = refs[:-1], refs[-1]
    first = place[BATCH] == 0
    rows = parts[0].shape[0]
    count = len(parts) // 2
    for i in range(count):
        mine, got = parts[i][...], parts[count + i][...].astype(F32)
        out_ref[0, i * rows : (i + 1) * rows] = jnp.where(first, mine, got)
        out_ref[1, i * rows : (i + 1) * rows] = jnp.where(first, got, mine)


def ffn_grad_kernel(place, left_ref, acts_ref, keep_ref, send_ref):
    put_grad(place, dot(left_ref[...], acts_ref[...], ((1,), (0,))), keep_ref, 0, [send_ref])


def local(
    stream,
    cotangent,
    mixer_in,
    memory_in,
    mixer_out,
    ffn_in,
    ffn_out,
    persistent,
    norm_gains,
    conv_weight,
    decays,
    doc_starts,
):
    batches, seg, width = stream.shape
    at = Place(batches)
    cols = mixer_out.shape[0]
    own = cols // HD
    heads = 2 * own
    hidden = ffn_out.shape[0]
    wide = -(-hidden // LANES) * LANES
    taps = conv_weight.shape[0]
    persist = persistent.shape[0] // 2
    scale = HD**-0.5
    steps = seg // BLOCK
    chips = at.ns // 2
    share = width // at.ns
    col = width // at.nz
    pick = lambda a: lax.dynamic_index_in_dim(a, at.p, 0, False)
    drop = lambda a: lax.dynamic_index_in_dim(a, 1 - at.p, 0, False)
    place = jnp.stack([at.p, at.l] + [at.bit_of(bit) for bit in at.bits] + [at.seq // 2])
    last_place = place.shape[0] - 1
    line = Line(place.astype(jnp.int32))
    run = line.run

    per_a, decay_a = persistent, pick(decays)
    decay_b = at.other(drop(decays))

    last = lax.dynamic_slice(stream, (at.p, seg - 8, 0), (1, 8, width))[0]
    last = last * lax.rsqrt(jnp.mean(last * last, axis=-1, keepdims=True) + EPS)
    rim_rows = at.along((last * norm_gains[0]).astype(BF16), 1)

    first_row = at.seq * share
    rows_of = lambda a: lax.dynamic_slice_in_dim(a, first_row, share, 0)
    cols_of = lambda a: lax.dynamic_slice_in_dim(a, first_row, share, 1)

    def joined(into, memory, out):
        return jnp.concatenate(
            [into.reshape(into.shape[0], -1), memory.reshape(into.shape[0], -1), out.T], axis=1
        )

    pad = lambda a: jnp.pad(a, ((0, 0), (0, wide - hidden)))

    def ffn_joined(into, out):
        return jnp.concatenate([pad(into[:, 0]), pad(into[:, 1]), pad(out.T)], axis=1)

    part_w = at.other(joined(rows_of(mixer_in), rows_of(memory_in), cols_of(mixer_out)))
    part_f = ffn_joined(rows_of(ffn_in), cols_of(ffn_out))

    def spread(part):
        return (part, *[at.across(part, 2 * r) for r in range(1, chips)])

    def stacked(parts, relay=()):
        n = parts[0].shape[1]
        mine, *relayed = run(
            stack_kernel, (1,), [full(a) for a in parts], [fixed((chips, share, n), BF16)], placed=False, relay=relay
        )
        return (mine, at.across(mine, 1)), *relayed

    def assemble(mine, theirs):
        n = mine.shape[2]
        block = lambda r, s: (r, 0, 0)
        (out,) = run(
            assemble_kernel,
            (chips,),
            [(mine, (1, share, n), block), (theirs, (1, share, n), block)],
            [((chips, 2 * share, n), BF16, (1, 2 * share, n), lambda r, s: (s[last_place] ^ r, 0, 0))],
        )
        return out.reshape(width, n)

    first_pos = at.seq * seg
    positions = first_pos + jnp.arange(seg, dtype=jnp.int32)
    marks = pick(doc_starts)
    starts = jnp.max(jnp.where(marks[None, :] <= positions[:, None], marks[None, :], 0), axis=-1)

    def token_table(decay):
        log_sums = jnp.cumsum(jnp.log(decay), axis=-1)
        inflow = jnp.exp(log_sums) * (starts < first_pos).astype(F32)
        keep = jnp.exp(log_sums[:, seg - 1 :] - log_sums) * (positions >= starts[seg - 1]).astype(F32)
        scaled_sums = log_sums * LOG2E
        gap = jnp.zeros((4 - own, seg), F32)
        table = jnp.concatenate(
            [
                scaled_sums, gap, inflow, gap, keep, gap,
                jnp.maximum(starts - first_pos, 0).astype(F32)[None],
                (positions - starts).astype(F32)[None],
            ],
            axis=0,
        )
        return jnp.pad(table, ((0, LANES - table.shape[0]), (0, 0))).T, scaled_sums[:, None]


    blk = (BLOCK, width)
    batch_rows = lambda i, s: (s[BATCH], i, 0)
    gains_in = (norm_gains, norm_gains.shape, whole(2))
    taps_in = (conv_weight, conv_weight.shape, whole(2))
    stream_in = (stream, (1,) + blk, batch_rows)
    cot_in = (cotangent, (1,) + blk, batch_rows)

    def full(a):
        return (a, a.shape, whole(a.ndim))

    def held(a):
        return (a, None, None)

    def tiled(a, n=None):
        return (a, (BLOCK, n or a.shape[1]), rows_map)

    def out_rows(n, dtype):
        return ((seg, n), dtype, (BLOCK, n), rows_map)

    def fixed(shape, dtype=F32):
        return (shape, dtype, shape, whole(len(shape)))

    ages = jnp.broadcast_to((positions - starts)[:, None], (seg, LANES))
    normed, conv_out, part_f = run(
        norm_conv_kernel,
        (steps,),
        [stream_in, gains_in, full(rim_rows), tiled(ages), taps_in],
        [out_rows(width, BF16), out_rows(width, BF16)],
        scratch=[pltpu.VMEM((8, width), F32)],
        flops=20 * seg * width,
        relay=(part_f,),
    )
    part_f = at.other(part_f)
    mixer_in, memory_in, mixer_out, decay_a, _ = lax.optimization_barrier(
        (mixer_in, memory_in, mixer_out, decay_a, conv_out)
    )
    w_a = joined(mixer_in, memory_in, mixer_out)
    table_a, decay_rows_a = token_table(decay_a)
    per_b = at.other(persistent)

    def project(side, w, table, onto=(), relay=()):
        half_cols = lambda n, dtype: ((seg, 2 * n), dtype, (BLOCK, n), lambda i, s: (i, side))
        return run(
            project_kernel,
            (steps,),
            [tiled(normed), tiled(conv_out), held(w), tiled(table)],
            [
                half_cols(3 * cols, BF16), half_cols(cols, F32), half_cols(3 * cols, BF16),
                ((2, seg, LANES), F32, (1, BLOCK, LANES), lambda i, s: (side, i, 0)),
                ((heads, HD + 8, HD), F32, (own, HD + 8, HD), lambda i, s: (side, 0, 0)),
            ],
            placed=False,
            flops=2 * seg * width * 7 * cols,
            onto=onto,
            relay=relay,
        )

    def head_cols(a, part, first=0):
        return (
            a,
            (seg, HD),
            lambda h, s: (0, (first + jnp.minimum(h, heads - 1 - first)) // own * 3 * own + part * own + lax.rem(first + jnp.minimum(h, heads - 1 - first), own)),
        )

    pair_flops = own * seg * seg * HD * 1.25

    def attend(side, qkv, mem, per, table, rows, onto=(), relay=()):
        first = side * own
        return run(
            functools.partial(attend_kernel, scale),
            (own,),
            [head_cols(qkv, i, first) for i in range(3)]
            + [head_cols(mem, i, first) for i in range(3)]
            + [(per, (persist, HD), lambda h, s: (0, h)), (per, (persist, HD), lambda h, s: (1, h))]
            + [full(table[None]), (rows, (1, 1, seg), lambda h, s: (h, 0, 0))],
            [((seg, 2 * cols), F32, (seg, HD), lambda h, s: (0, first + h))] * 2
            + [((2, seg, LANES), F32, (1, seg, LANES), lambda h, s: (side, 0, 0))],
            placed=False,
            flops=4 * pair_flops,
            trans=own * seg * seg * 1.25,
            onto=onto,
            relay=relay,
        )

    def scan(mine, reverse, first, second, relay):
        got = at.across(mine, 1)
        first()
        pair, *relayed = run(
            functools.partial(pair_scan_kernel, reverse), (1,), [full(mine), full(got)], [fixed(mine.shape)], relay=relay
        )
        pairs = [pair] + [at.across(pair, 2 * r) for r in range(1, chips)]
        second(*relayed)
        (out,) = run(
            functools.partial(chip_scan_kernel, reverse, chips),
            (1,),
            [full(got)] + [full(a) for a in pairs],
            [fixed((heads, HD, HD), BF16)],
        )
        return out, *relayed

    kept = {}

    part_w, w_a = lax.optimization_barrier((part_w, w_a))
    parts_w = spread(part_w)
    projected = project(0, w_a, table_a)
    attended = attend(0, projected[0], projected[2], per_a, table_a, decay_rows_a)
    decay_b, _ = lax.optimization_barrier((decay_b, projected[3]))
    parts_w, part_f = stacked(parts_w, (part_f,))
    parts_f = spread(part_f)
    w_b = assemble(*parts_w)
    table_b, decay_rows_b = token_table(decay_b)
    line.wait(per_b)
    qkv, gate, mem, inv, state = project(1, w_b, table_b, projected)

    def attend_other(*_):
        kept["att"] = attend(1, qkv, mem, per_b, table_b, decay_rows_b, attended)

    ffn_in, ffn_out, _ = lax.optimization_barrier((ffn_in, ffn_out, inv))
    f_a = ffn_joined(ffn_in, ffn_out)
    line.wait(f_a)
    nothing = lambda: None
    state_in, *parts_f = scan(state, False, nothing, attend_other, parts_f)
    att, rec, logs = kept["att"]
    (parts_f,) = stacked(parts_f)
    tables = jnp.stack([table_a, table_b])
    decay_rows = jnp.concatenate([decay_rows_a, decay_rows_b], axis=0)
    per_two = jnp.concatenate([per_a, per_b], axis=1)
    out_block = lambda w: (w, (width, cols), lambda i, s: (0, 7))

    half = steps // 2

    def half_in(a, part, n=None):
        return (a, (BLOCK, n or a.shape[1]), lambda i, s: (i + part * half, 0))

    def half_out(n, dtype, part):
        return ((seg, n), dtype, (BLOCK, n), lambda i, s: (i + part * half, 0))

    def half_batch(a, part):
        return (a, (1,) + blk, lambda i, s: (s[BATCH], i + part * half, 0))

    sent_half = ((seg // 2, width), BF16, blk, rows_map)

    def group_sum(part):
        got = [at.group(part, n) for n in range(1, at.nl)]
        total = got[0]
        for more in got[1:]:
            total = (total.astype(F32) + more.astype(F32)).astype(BF16)
        return total

    mixed, mixed_got, onto = [], [], ()
    for part in range(2):
        recalled, branch, mixed_part = run(
            mix_kernel,
            (half,),
            [half_in(a, part) for a in (att, rec, gate, mem, table_a, table_b)]
            + [full(state_in), out_block(w_a), out_block(w_b)],
            [half_out(2 * cols, F32, part), half_out(2 * cols, BF16, part), sent_half],
            placed=False,
            flops=seg * width * 2 * cols,
            onto=onto,
        )
        onto = (recalled, branch)
        mixed.append(mixed_part)
        mixed_got.append(group_sum(mixed_part))

    f_b = assemble(*parts_f)
    back, back_got, onto = [], [], ()
    for part in range(2):
        normed_t, cot_t, acts, *ffn_parts, back_part = run(
            ffn_kernel,
            (half,),
            [half_batch(stream, part), tiled(mixed[part]), tiled(mixed_got[part]), half_batch(cotangent, part)]
            + [gains_in, held(f_a), held(f_b)],
            [((width, seg), BF16, (width, BLOCK), lambda i, s, part=part: (0, i + part * half))] * 2
            + [half_out(6 * wide, BF16, part)]
            + [half_out(batches * col, BF16, part)] * at.nl
            + [sent_half],
            scratch=[pltpu.VMEM(blk, F32)],
            flops=seg * width * wide * 12,
            onto=onto,
        )
        onto = (normed_t, cot_t, acts, *ffn_parts)
        back.append(back_part)
        back_got.append(group_sum(back_part))
    chip_bits = [bit // 2 for bit in at.bits[1:]]
    orders = (list(reversed(chip_bits)), chip_bits)

    def exchange(parts, step):
        return [parts[0], parts[2]], [at.across(parts[2 * i + 1], 2 * orders[i][step]) for i in range(2)]

    def core_sum(keep_part, got):
        n = got.shape[2]
        there = lambda r, s: (s[last_place] ^ r, 0, 0)
        parts = run(
            functools.partial(core_sum_kernel, (orders[0][0], orders[1][0])),
            (chips,),
            [(a, (1, share, n), there) for a in (keep_part, got)],
            [fixed((chips // 2, share, n // 2), BF16)] * 4,
        )
        return exchange(parts, 0)

    def chip_step(keeps, gots, step):
        half_n = keeps[0].shape[2]
        ins = [full(a) for a in (*keeps, *gots)]
        if step == len(chip_bits):
            mine, theirs = run(
                functools.partial(chip_step_kernel, None),
                (1,),
                ins,
                [fixed((share, half_n)), fixed((share, half_n), BF16)],
                placed=False,
            )
            return mine, at.other(theirs)
        rests = []
        for order in orders:
            gone = sum(order[:step])
            held = [r for r in range(chips) if not r & gone]
            rests.append(tuple([i for i, r in enumerate(held) if bool(r & order[step]) == sent] for sent in (False, True)))
        parts = run(
            functools.partial(chip_step_kernel, rests),
            (1,),
            ins,
            [fixed((len(places), share, half_n), BF16) for rest in rests for places in rest],
            placed=False,
        )
        return exchange(parts, step)

    def middle_steps(sums):
        for step in range(1, len(chip_bits)):
            sums = chip_step(*sums, step)
        return sums

    def ffn_grads(left, count, chunk, onto=()):
        return run(
            ffn_grad_kernel,
            (count,),
            [full(left), (acts, (seg, wide), lambda i, s: (0, chunk(i)))],
            [((chips, share, 6 * wide), BF16, (chips, share, wide), lambda i, s: (0, 0, chunk(i)))] * 2,
            flops=2 * seg * width * wide * count,
            onto=onto,
        )

    half_f = ffn_grads(normed_t, 4, lambda i: i + i // 2)
    line.wait(back_got[0])
    keep_f, send_f = ffn_grads(cot_t, 2, lambda i: 3 * i + 2, half_f)
    gain_two, state_terms = jnp.zeros((8, width), F32), jnp.zeros((heads, HD + 8, HD), F32)
    onto = ()
    for part in range(2):
        grad_mid, grad_mix, grad_branch, grad_rec, grad_gate, gain_two, state_terms, *relayed = run(
            mid_back_kernel,
            (half,),
            [half_batch(stream, part)]
            + [tiled(a[part]) for a in (mixed, mixed_got, back, back_got)]
            + [half_batch(cotangent, part), gains_in, out_block(w_a), out_block(w_b)]
            + [half_in(a, part) for a in (gate, recalled, mem, table_a, table_b)]
            + [full(gain_two), full(state_terms)],
            [half_out(width, F32, part), half_out(width, BF16, part)]
            + [half_out(2 * cols, BF16, part)] * 3
            + [fixed((8, width)), fixed((heads, HD + 8, HD))],
            flops=seg * width * 2 * cols,
            onto=onto,
            relay=tuple(ffn_parts[1:]) if part == 0 else (),
        )
        if part == 0:
            ffn_shares = [ffn_parts[0]] + [at.group(a, r + 1) for r, a in enumerate(relayed)]
        onto = (grad_mid, grad_mix, grad_branch, grad_rec, grad_gate)

    def of_side(a):
        return (a, (1, *a.shape[1:]), lambda h, s: (jnp.minimum(h, heads - 1) // own, 0, 0))

    def of_head(a):
        return (a, (1, *a.shape[1:]), lambda h, s: (jnp.minimum(h, heads - 1), 0, 0))

    def head_block(a):
        return (a, (seg, HD), lambda h, s: (0, jnp.minimum(h, heads - 1)))

    def attend_back(side, onto=()):
        first = side * own
        return run(
            functools.partial(attend_back_kernel, scale),
            (own,),
            [head_cols(qkv, i, first) for i in range(3)]
            + [(grad_branch, (seg, HD), lambda h, s: (0, first + h))]
            + [(per_two, (persist, HD), lambda h, s: (0, first + h)), (per_two, (persist, HD), lambda h, s: (1, first + h))]
            + [(a, (1, seg, LANES), lambda h, s: (side, 0, 0)) for a in (tables, logs)],
            [
                ((seg, 6 * cols), BF16, (seg, 3 * cols), lambda h, s: (0, side)),
                ((heads, 2 * persist, HD), F32, (1, 2 * persist, HD), lambda h, s: (first + h, 0, 0)),
            ],
            scratch=[pltpu.VMEM((seg, HD), F32)] * 2,
            placed=False,
            flops=5 * pair_flops,
            trans=own * seg * seg * 0.6,
            onto=onto,
        )

    def during_scan(send_f):
        kept["f"] = at.across(send_f, 1)
        kept["back"] = attend_back(0)

    grad_state, send_f = scan(state_terms, True, nothing, during_scan, (send_f,))
    got_f = kept["f"]
    sums_f = core_sum(keep_f, got_f)


    def share_ins(arrays, side):
        return [(a, (BLOCK, col), lambda i, s: (i, lax.rem(s[BATCH] + side, batches))) for a in arrays]

    def wide_in(a, side):
        return (a, (BLOCK, col), lambda i, s: (i, lax.rem(s[BATCH] + side, batches) * at.nl + s[GROUP]))

    (dmem,) = run(
        memory_back_kernel,
        (heads,),
        [head_cols(mem, i) for i in range(3)]
        + [head_block(grad_rec), of_side(inv), of_side(tables), of_head(decay_rows), of_head(state_in), of_head(grad_state)],
        [fixed((seg, 6 * cols), BF16)],
        scratch=[pltpu.VMEM((seg, HD), F32)] * 2,
        flops=10 * pair_flops,
        trans=2 * own * seg * seg * 0.6,
        placed=False,
    )
    first_grad = dot(dmem[:8, : 3 * cols], w_a[:, 4 * cols : 7 * cols], ((1,), (1,))) + dot(
        dmem[:8, 3 * cols :], w_b[:, 4 * cols : 7 * cols], ((1,), (1,))
    )
    first_ages = (positions - starts)[:8, None]
    rim_back = jnp.zeros((8, width), F32)
    for tap in range(1, taps):
        term = jnp.where(first_ages >= tap, first_grad, 0.0)[:tap] * conv_weight[tap]
        rim_back = rim_back + jnp.pad(term, ((8 - tap, 0), (0, 0)))
    rim_back = at.along(rim_back, -1)

    ins = []
    for side in range(2):
        ins.append(
            (
                stream,
                (1, BLOCK, col),
                lambda i, s, side=side: (s[BATCH], i, lax.rem(s[BATCH] + side, batches) * at.nl + s[GROUP]),
            )
        )
        ins += [
            (
                a,
                (BLOCK, col),
                lambda i, s, side=side, part=part: (
                    jnp.clip(i - part * half, 0, half - 1),
                    lax.rem(s[BATCH] + side, batches) * at.nl + s[GROUP],
                ),
            )
            for part in range(2)
            for a in (mixed[part], mixed_got[part])
        ] + share_ins(ffn_shares, side)
    result_mine, result_send, squares = run(
        functools.partial(result_kernel, at.nl),
        (steps,),
        ins,
        [out_rows(col, F32), out_rows(col, BF16), fixed((8, col))],
    )
    result_got = at.other(result_send)
    sums_f = middle_steps(sums_f)
    dqkv, per_grad = attend_back(1, kept["back"])
    line.wait(result_got)
    f_mine, f_got = chip_step(*sums_f, len(chip_bits))
    line.wait(rim_back)
    span = max(2 * share, 256)
    pairs = span // (2 * share)
    left_in = lambda a: (a, (seg, span), lambda i, s: (0, i))
    keep_x, send_x = run(
        weight_grad_kernel,
        (width // span,),
        [left_in(normed), left_in(conv_out), left_in(grad_mix), full(dqkv), full(grad_gate), full(branch), full(dmem)],
        [((chips, share, 16 * cols), BF16, (pairs, share, 16 * cols), lambda i, s: (i, 0, 0))] * 2,
        flops=2 * seg * width * 16 * cols,
    )


    def placed(*parts):
        return run(placed_kernel, (1,), [full(a) for a in parts], [fixed((batches, seg, col))])[0]

    line.wait(f_got)
    result = placed(result_mine, result_got)
    got_x = at.across(lax.optimization_barrier((send_x, result))[0], 1)
    turned = lambda i, s: (steps - 1 - i, 0)
    turn = lambda a: (a, (BLOCK, a.shape[1]), turned)
    gain_one, grad_conv, *in_parts = run(
        in_back_kernel,
        (steps,),
        [
            (stream, (1,) + blk, lambda i, s: (s[BATCH], steps - 1 - i, 0)),
            full(normed), full(rim_rows), turn(table_a), gains_in, taps_in, full(rim_back),
        ]
        + [turn(a) for a in (dqkv, grad_gate, dmem)]
        + [held(w_a), held(w_b)],
        [fixed((8, width))] * 2 + [((seg, batches * col), BF16, (BLOCK, batches * col), turned)] * at.nl,
        scratch=[pltpu.VMEM((8, width), F32), pltpu.VMEM(blk, F32)],
        flops=2 * seg * width * 14 * cols,
    )
    in_shares = [in_parts[0]] + [at.group(a, r) for r, a in enumerate(in_parts) if r > 0]
    sums_x = core_sum(keep_x, got_x)

    small = jnp.concatenate(
        [
            gain_one[:1], gain_two[:1] / at.nl, grad_conv[:taps],
            jnp.pad(jnp.sum(squares[:4], axis=-1), (0, width - 4))[None],
            per_grad.reshape(-1, width),
        ],
        axis=0,
    )
    small = jnp.pad(small, ((0, -small.shape[0] % 8), (0, 0)))

    def added(parts):
        return run(add_kernel, (1,), [full(a) for a in parts], [fixed(parts[0].shape)], placed=False)[0]

    small_got = at.across(small, 1)
    small = added([small, small_got])

    ins = []
    for side in range(2):
        ins += [wide_in(grad_mid, side)] + share_ins(in_shares, side)
    stream_mine, stream_send = run(
        functools.partial(stream_grad_kernel, at.nl), (steps,), ins, [out_rows(col, F32), out_rows(col, BF16)]
    )
    stream_got = at.other(stream_send)
    sums_x = middle_steps(sums_x)
    grad_ffn_in, grad_ffn_out = run(
        functools.partial(final_ffn_kernel, hidden),
        (1,),
        [full(f_mine), full(f_got)],
        [fixed((share, 2, hidden)), fixed((hidden, share))],
        placed=False,
    )
    x_mine, x_got = chip_step(*sums_x, len(chip_bits))
    for bit in at.bits[1:-1]:
        small = added([small, at.across(small, bit)])
    small = added([small, at.across(small, at.bits[-1])])
    head_parts = [small] + [
        lax.ppermute(small, "head", [(i, (i + n) % at.nz) for i in range(at.nz)]) for n in range(1, at.nz)
    ]
    grad_stream = placed(stream_mine, stream_got)
    grad_mixer_in, grad_memory_in, grad_mixer_out = run(
        final_mixer_kernel,
        (1,),
        [full(x_mine), full(x_got)],
        [fixed((share, 4, cols)), fixed((share, 3, cols)), fixed((cols, share))],
        placed=False,
    )

    sums = sum(a[: 3 + taps] for a in head_parts[1:]) + small[: 3 + taps]
    rows_p = persistent.shape[0] // at.ns

    def persist_rows(a):
        a = a[3 + taps : 3 + taps + heads * 2 * persist * HD // width].reshape(heads, 2 * persist, HD)
        a = lax.dynamic_slice_in_dim(a, at.seq * rows_p, rows_p, 1)
        return jnp.transpose(a, (1, 0, 2)).reshape(rows_p, -1)

    grad_persistent = persist_rows(small)[:, :cols] + persist_rows(head_parts[at.nl])[:, cols:]
    cells = float(batches * seg * at.ns * width)
    rms_values = jnp.sqrt(sums[2 + taps, :4] / cells)
    return (
        result,
        grad_stream,
        grad_mixer_in,
        grad_memory_in,
        grad_mixer_out,
        grad_ffn_in,
        grad_ffn_out,
        grad_persistent,
        sums[:2],
        sums[2 : 2 + taps],
        rms_values,
    )


def solution(mesh):
    placed = (
        P(None, "seq", None),
        P(None, "seq", None),
        P(None, None, "head"),
        P(None, None, "head"),
        P("head", None),
        P(None, None, "head"),
        P("head", None),
        P(None, "head"),
        P(),
        P(),
        P(None, "head", "seq"),
        P(),
    )
    return jax.shard_map(
        local,
        mesh=mesh,
        in_specs=placed,
        out_specs=(
            P(None, "seq", "head"),
            P(None, "seq", "head"),
            P("seq", None, "head"),
            P("seq", None, "head"),
            P("head", "seq"),
            P("seq", None, "head"),
            P("head", "seq"),
            P("seq", "head"),
            P(),
            P(),
            P(),
        ),
        check_vma=False,
    )
```

```python
import functools
import math

import jax
import jax.numpy as jnp
from jax import lax
from jax.experimental import pallas as pl
from jax.experimental.pallas import tpu as pltpu
from jax.sharding import PartitionSpec as P

HD = 128
EPS = 1e-06
F32 = jnp.float32
BF16 = jnp.bfloat16


def dot(a, b, dims):
    return lax.dot_general(a, b, (dims, ((), ())), preferred_element_type=F32)


class Place:
    def __init__(self, batches):
        self.ns = lax.axis_size("seq")
        self.nz = lax.axis_size("head")
        self.nl = self.nz // batches
        self.seq = lax.axis_index("seq")
        self.z = lax.axis_index("head")
        self.p = self.z // self.nl
        self.l = self.z % self.nl
        self.bits = [1 << i for i in range(self.ns.bit_length() - 1)]

    def across(self, value, bit):
        return lax.ppermute(value, "seq", [(i, i ^ bit) for i in range(self.ns)])

    def along(self, value, steps):
        first, last = max(0, -steps), min(self.ns, self.ns - steps)
        return lax.ppermute(value, "seq", [(i, i + steps) for i in range(first, last)])

    def other(self, value):
        return lax.ppermute(value, "head", [(i, (i + self.nl) % self.nz) for i in range(self.nz)])

    def group(self, value, steps):
        nl = self.nl
        return lax.ppermute(
            value,
            "head",
            [(i, i // nl * nl + (i % nl + steps) % nl) for i in range(self.nz)],
        )

    def bit_of(self, bit):
        return (self.seq // bit) % 2


LOG2E = 1.4426950408889634
BLOCK = 256
LANES = 128
BATCH, GROUP, CORE, CHIP = 0, 1, 2, 3
DECAY, INFLOW, KEEP, START, AGE = 0, 4, 8, 12, 13


def in_hbm(a):
    if math.prod(a.shape) * jnp.dtype(a.dtype).itemsize < 2**21:
        return a
    return pltpu.with_memory_space_constraint(a, pltpu.HBM)


class Line:
    def __init__(self, place):
        self.place = place
        self.waits = []
        self.last = None

    def wait(self, *arrays):
        self.waits += arrays

    def run(self, kernel, grid, ins, outs, scratch=(), flops=0, trans=0, onto=(), relay=(), placed=True, far=()):
        moved = sum(a.size * a.dtype.itemsize for a, _, _ in ins)
        moved += sum(math.prod(s) * jnp.dtype(d).itemsize for s, d, _, _ in outs)
        blocks = sum(2 * math.prod(b) * a.dtype.itemsize for a, b, _ in ins if b is not None)
        blocks += sum(2 * math.prod(b) * jnp.dtype(d).itemsize for _, d, b, _ in outs)
        blocks += sum(math.prod(a.shape) * jnp.dtype(a.dtype).itemsize for a in scratch)
        waits, self.waits = self.waits, []
        if self.last is not None and not any(self.last is a for a in (*[a for a, _, _ in ins], *onto, *relay, *waits)):
            waits = [*waits, self.last]
        extra = (*onto, *relay, *waits)
        n_ins, n_outs, lead = len(ins), len(outs), 1 if placed else 0

        def body(*refs):
            place_ref, refs = (refs[0] if placed else None), refs[lead:]
            inputs, outputs = refs[:n_ins], refs[n_ins + len(extra) : n_ins + len(extra) + n_outs]
            kernel(place_ref, *inputs, *outputs, *refs[n_ins + len(extra) + n_outs + len(relay) :])

        def mapped(index_map):
            return index_map if placed else lambda *at: index_map(*at, None)

        anywhere = pl.BlockSpec(memory_space=pl.ANY)
        spec = pltpu.PrefetchScalarGridSpec(
            num_scalar_prefetch=lead,
            grid=grid,
            in_specs=[
                pl.BlockSpec(memory_space=pltpu.VMEM) if b is None else pl.BlockSpec(b, mapped(m)) for _, b, m in ins
            ]
            + [anywhere] * len(extra),
            out_specs=[pl.BlockSpec(b, mapped(m)) for _, _, b, m in outs] + [anywhere] * len(relay),
            scratch_shapes=list(scratch),
        )
        aliases = {lead + n_ins + i: i for i in range(len(onto))}
        aliases |= {lead + n_ins + len(onto) + i: n_outs + i for i in range(len(relay))}
        got = pl.pallas_call(
            body,
            grid_spec=spec,
            out_shape=[
                pltpu.HBM(s, d) if i in far else jax.ShapeDtypeStruct(s, d) for i, (s, d, _, _) in enumerate(outs)
            ]
            + [jax.ShapeDtypeStruct(a.shape, a.dtype) for a in relay],
            input_output_aliases=aliases,
            compiler_params=pltpu.CompilerParams(
                dimension_semantics=("arbitrary",) * len(grid), vmem_limit_bytes=blocks + 8 * 2**20
            ),
            cost_estimate=pl.CostEstimate(flops=int(flops), bytes_accessed=int(moved), transcendentals=int(trans)),
        )(*((self.place,) if placed else ()), *[a if b is None else in_hbm(a) for a, b, _ in ins], *map(in_hbm, onto), *extra[len(onto) :])
        self.last = min(got[:n_outs], key=lambda a: a.size * a.dtype.itemsize)
        return got


def rows_map(i, *_):
    return (i, 0)


def whole(rank):
    return lambda *_: (0,) * rank


def column(table, index):
    return table[:, index : index + 1]


def pick_column(table, index):
    lane = lax.broadcasted_iota(jnp.int32, table.shape, 1)
    return jnp.sum(jnp.where(lane == index, table, 0.0), axis=-1, keepdims=True)


def norm_conv_kernel(p_ref, x_ref, gain_ref, rim_ref, table_ref, taps_ref, normed_ref, conv_ref, tail):
    x = x_ref[0]
    inv = lax.rsqrt(jnp.mean(x * x, axis=-1, keepdims=True) + EPS)
    normed = (x * inv * gain_ref[0:1]).astype(BF16)
    normed_ref[...] = normed
    wide = normed.astype(F32)

    @pl.when(pl.program_id(0) == 0)
    def _():
        tail[...] = rim_ref[...].astype(F32)

    ext = jnp.concatenate([tail[...], wide], axis=0)
    age = column(table_ref[...], 0)
    total = wide * taps_ref[0:1]
    for tap in range(1, taps_ref.shape[0]):
        back = pltpu.roll(ext, tap, 0)[8:]
        total = total + jnp.where(age >= tap, back, 0.0) * taps_ref[tap : tap + 1]
    conv_ref[...] = total.astype(BF16)
    tail[...] = wide[-8:]


def project_kernel(place, x_ref, c_ref, w_ref, table_ref, qkv_ref, gate_ref, mem_ref, inv_ref, state_ref):
    cols = gate_ref.shape[1]
    count = cols // HD
    proj = dot(x_ref[...], w_ref[:, : 4 * cols], ((1,), (0,)))
    qkv_ref[...] = proj[:, : 3 * cols].astype(BF16)
    gate_ref[...] = jax.nn.sigmoid(proj[:, 3 * cols :])
    mem = dot(c_ref[...], w_ref[:, 4 * cols : 7 * cols], ((1,), (0,)))
    lane = lax.broadcasted_iota(jnp.int32, inv_ref.shape[1:], 1)
    invs = jnp.zeros(inv_ref.shape[1:], F32)
    units = []
    for i in range(2 * count):
        raw = mem[:, i * HD : (i + 1) * HD]
        inv = lax.rsqrt(jnp.sum(raw * raw, axis=-1, keepdims=True) + EPS)
        units.append((raw * inv).astype(BF16))
        mem_ref[:, i * HD : (i + 1) * HD] = units[-1]
        invs = jnp.where(lane == i, inv, invs)
    inv_ref[0] = invs
    value = mem[:, 2 * cols :].astype(BF16)
    mem_ref[:, 2 * cols :] = value

    @pl.when(pl.program_id(0) == 0)
    def _():
        state_ref[...] = jnp.zeros_like(state_ref)

    table = table_ref[...]
    for h in range(count):
        kept = (units[count + h].astype(F32) * column(table, KEEP + h)).astype(BF16)
        state_ref[h, :HD] += dot(kept, value[:, h * HD : (h + 1) * HD], ((0,), (0,)))
        carry = column(table, INFLOW + h)[-8:]
        state_ref[h, HD:] = jnp.broadcast_to(carry[7:8], (8, HD))


def joined(early, late):
    state = early[:, :HD] * late[:, HD : HD + 1] + late[:, :HD]
    return jnp.concatenate([state, early[:, HD:] * late[:, HD:]], axis=1)


def pair_scan_kernel(reverse, place, mine_ref, got_ref, out_ref):
    mine, got = mine_ref[...], got_ref[...]
    high = (place[CORE] == 1) ^ reverse
    out_ref[...] = joined(jnp.where(high, got, mine), jnp.where(high, mine, got))


def chip_scan_kernel(reverse, chips, place, got_ref, *refs):
    pairs, out_ref = refs[:-1], refs[-1]
    here = place[place.shape[0] - 1]
    total = None
    for step in range(chips):
        chip = chips - 1 - step if reverse else step
        away = here ^ chip
        block = pairs[0][...]
        for r in range(1, chips):
            block = jnp.where(away == r, pairs[r][...], block)
        before = chip > here if reverse else chip < here
        row = lax.broadcasted_iota(jnp.int32, block.shape, 1)
        block = jnp.where(before, block, jnp.where(row < HD, 0.0, 1.0))
        total = block if total is None else joined(total, block)
    high = (place[CORE] == 1) ^ reverse
    total = jnp.where(high, joined(total, got_ref[...]), total)
    out_ref[...] = total[:, :HD].astype(BF16)


def add_kernel(place, *refs):
    total = refs[0][...]
    for part in refs[1:-1]:
        total = total + part[...]
    refs[-1][...] = total


def stack_kernel(place, *refs):
    for i, ref in enumerate(refs[:-1]):
        refs[-1][i] = ref[...]


def assemble_kernel(place, mine_ref, theirs_ref, out_ref):
    share = mine_ref.shape[1]
    first = place[CORE] == 0
    mine, theirs = mine_ref[0], theirs_ref[0]
    out_ref[0, :share] = jnp.where(first, mine, theirs)
    out_ref[0, share:] = jnp.where(first, theirs, mine)


def parted(chips, bit):
    return [r for r in range(chips) if not r & bit], [r for r in range(chips) if r & bit]


def core_sum_kernel(bits, place, keep_ref, got_ref, *outs):
    total = keep_ref[0].astype(F32) + got_ref[0].astype(F32)
    half = total.shape[1] // 2
    for side, bit in enumerate(bits):
        part = total[:, side * half : (side + 1) * half].astype(BF16)
        for out, rs in zip(outs[2 * side : 2 * side + 2], parted(2 * outs[0].shape[0], bit)):
            for i, r in enumerate(rs):

                @pl.when(pl.program_id(0) == r)
                def _():
                    out[i] = part


def chip_step_kernel(rests, place, *refs):
    keeps, gots, outs = refs[:2], refs[2:4], refs[4:]
    for side, (keep, got) in enumerate(zip(keeps, gots)):
        total = [keep[i].astype(F32) + got[i].astype(F32) for i in range(keep.shape[0])]
        if rests is None:
            outs[side][...] = total[0].astype(outs[side].dtype)
            continue
        for out, places in zip(outs[2 * side : 2 * side + 2], rests[side]):
            for i, at in enumerate(places):
                out[i] = total[at].astype(BF16)


def split_columns(place, held, outs):
    batches = 2
    col = outs[0].shape[1] // batches
    group = len(outs)
    for r, out in enumerate(outs):
        target = lax.rem(place[GROUP] + r, group)
        for b in range(batches):
            first = pl.multiple_of((b * group + target) * col, col)
            out[:, b * col : (b + 1) * col] = held[:, pl.ds(first, col)].astype(BF16)


def result_kernel(parts, place, *refs):
    mine_ref, send_ref, squares = refs[-3:]

    @pl.when(pl.program_id(0) == 0)
    def _():
        squares[...] = jnp.zeros_like(squares)

    for side, out in enumerate((mine_ref, send_ref)):
        x_ref, m_a, m_b, n_a, n_b, *shares = refs[side * (5 + parts) : (side + 1) * (5 + parts)]
        x = x_ref[0]
        early = pl.program_id(0) < pl.num_programs(0) // 2
        mixed = jnp.where(early, m_a[...].astype(F32) + m_b[...].astype(F32), n_a[...].astype(F32) + n_b[...].astype(F32))
        ffn = shares[0][...].astype(F32)
        for share in shares[1:]:
            ffn = ffn + share[...].astype(F32)
        result = x + mixed + ffn
        for i, a in enumerate((x, mixed, ffn, result)):
            squares[i : i + 1] += jnp.sum(a * a, axis=0, keepdims=True)
        out[...] = result.astype(out.dtype)


def stream_grad_kernel(parts, place, *refs):
    mine_ref, send_ref = refs[-2:]
    for side, out in enumerate((mine_ref, send_ref)):
        mid, *shares = refs[side * (1 + parts) : (side + 1) * (1 + parts)]
        total = mid[...]
        for share in shares:
            total = total + share[...].astype(F32)
        out[...] = total.astype(out.dtype)


def allowed_block(table, first, rows, count):
    start = column(table, START)[first : first + rows].astype(jnp.int32)
    col = lax.broadcasted_iota(jnp.int32, (rows, count), 1)
    row = lax.broadcasted_iota(jnp.int32, (rows, count), 0) + first
    return (col >= start) & (col <= row)


def attend_kernel(
    scale, place, q_ref, k_ref, v_ref, mq_ref, mk_ref, mv_ref, pk_ref, pv_ref, table_ref, decay_ref,
    att_ref, rec_ref, log_ref,
):
    h = pl.program_id(0)
    seg = q_ref.shape[0]
    table = table_ref[0]
    down = pick_column(table, DECAY + h)
    across = decay_ref[0]
    lane = lax.broadcasted_iota(jnp.int32, (BLOCK, LANES), 1)
    pk, pv = pk_ref[...], pv_ref[...]
    for first in range(0, seg, BLOCK):
        rows, end = slice(first, first + BLOCK), first + BLOCK
        ok = allowed_block(table, first, BLOCK, end)
        query = q_ref[rows]
        s = jnp.where(ok, dot(query, k_ref[:end], ((1,), (1,))) * (scale * LOG2E), -1e30)
        ps = dot(query, pk, ((1,), (1,))) * (scale * LOG2E)
        top = jnp.maximum(jnp.max(s, axis=-1, keepdims=True), jnp.max(ps, axis=-1, keepdims=True))
        e, pe = jnp.exp2(s - top), jnp.exp2(ps - top)
        total = jnp.sum(e, axis=-1, keepdims=True) + jnp.sum(pe, axis=-1, keepdims=True)
        att = dot(e.astype(BF16), v_ref[:end], ((1,), (0,))) + dot(pe.astype(BF16), pv, ((1,), (0,)))
        att_ref[rows] = att / total
        logs = top + jnp.log2(total)
        before = jnp.where(h == 0, 0.0, log_ref[0, rows])
        log_ref[0, rows] = jnp.where(lane == h, logs, before)
        w = dot(mq_ref[rows], mk_ref[:end], ((1,), (1,)))
        grid = jnp.exp2(jnp.minimum(down[rows] - across[:, :end], 0.0))
        w = jnp.where(ok, w * grid, 0.0).astype(BF16)
        rec_ref[rows] = dot(w, mv_ref[:end], ((1,), (0,)))


def mix_kernel(
    place, att_ref, rec_ref, gate_ref, mem_ref, table_a, table_b, state_ref, out_a, out_b,
    recalled_ref, branch_ref, mixed_ref,
):
    cols = out_a.shape[1]
    count = cols // HD
    mixed = None
    for side, (table_ref, out) in enumerate(((table_a, out_a), (table_b, out_b))):
        table = table_ref[...]
        for h in range(count):
            query = mem_ref[:, (3 * side * count + h) * HD : (3 * side * count + h + 1) * HD]
            inward = (query.astype(F32) * column(table, INFLOW + h)).astype(BF16)
            here = slice((side * count + h) * HD, (side * count + h + 1) * HD)
            recalled = rec_ref[:, here] + dot(inward, state_ref[side * count + h], ((1,), (0,)))
            recalled_ref[:, here] = recalled
            branch_ref[:, here] = (att_ref[:, here] + gate_ref[:, here] * recalled).astype(BF16)
        part = dot(branch_ref[:, side * cols : (side + 1) * cols], out[...], ((1,), (1,)))
        mixed = part if mixed is None else mixed + part
    mixed_ref[...] = mixed.astype(BF16)


def ffn_kernel(place, x_ref, m_a, m_b, cot_ref, gain_ref, w_a, w_b, normed_ref, cot_out, acts_ref, *outs):
    outs, back_ref, held = outs[:-2], outs[-2], outs[-1]
    middle = x_ref[0] + m_a[...].astype(F32) + m_b[...].astype(F32)
    inv = lax.rsqrt(jnp.mean(middle * middle, axis=-1, keepdims=True) + EPS)
    normed = (middle * inv * gain_ref[1:2]).astype(BF16)
    normed_ref[...] = normed.T
    grad_ffn = cot_ref[0].astype(BF16)
    cot_out[...] = grad_ffn.T
    n = w_a.shape[1] // 3
    part, back = None, None
    for side, w in enumerate((w_a, w_b)):
        pair = dot(normed, w[:, : 2 * n], ((1,), (0,)))
        pre, up = pair[:, :n], pair[:, n:]
        grad_hidden = dot(grad_ffn, w[:, 2 * n :], ((1,), (0,)))
        sig = jax.nn.sigmoid(pre)
        silu = pre * sig
        hidden = (silu * up).astype(BF16)
        slope = sig + silu * (1.0 - sig)
        grad_pre = (grad_hidden * up * slope).astype(BF16)
        grad_up = (grad_hidden * silu).astype(BF16)
        grad_pair = jnp.concatenate([grad_pre, grad_up], axis=1)
        acts_ref[:, 3 * side * n : (3 * side + 2) * n] = grad_pair
        acts_ref[:, (3 * side + 2) * n : (3 * side + 3) * n] = hidden
        one = dot(hidden, w[:, 2 * n :], ((1,), (1,)))
        two = dot(grad_pair, w[:, : 2 * n], ((1,), (1,)))
        part = one if part is None else part + one
        back = two if back is None else back + two
    held[...] = part
    split_columns(place, held, outs)
    back_ref[...] = back.astype(BF16)


def mid_back_kernel(
    place, x_ref, m_a, m_b, g_a, g_b, cot_ref, gain_ref, out_a, out_b, gate_in, recalled_ref, mem_ref,
    table_a, table_b, gain_in, state_in, mid_ref, mix_ref, branch_ref, rec_ref, gate_ref, gain_out, state_ref,
):
    @pl.when(pl.program_id(0) == 0)
    def _():
        gain_out[...] = gain_in[...]
        state_ref[...] = state_in[...]

    middle = x_ref[0] + m_a[...].astype(F32) + m_b[...].astype(F32)
    inv = lax.rsqrt(jnp.mean(middle * middle, axis=-1, keepdims=True) + EPS)
    hat = middle * inv
    grad = g_a[...].astype(F32) + g_b[...].astype(F32)
    scaled = grad * gain_ref[1:2]
    grad_mid = inv * (scaled - hat * jnp.mean(scaled * hat, axis=-1, keepdims=True)) + cot_ref[0]
    gain_out[0:1] += jnp.sum(grad * hat, axis=0, keepdims=True)
    mid_ref[...] = grad_mid
    mix = grad_mid.astype(BF16)
    mix_ref[...] = mix
    cols = out_a.shape[1]
    count = cols // HD
    for side, (out, table_ref) in enumerate(((out_a, table_a), (out_b, table_b))):
        table = table_ref[...]
        here = slice(side * cols, (side + 1) * cols)
        branch = dot(mix, out[...], ((1,), (0,))).astype(BF16)
        branch_ref[:, here] = branch
        wide = branch.astype(F32)
        gate = gate_in[:, here]
        rec = (wide * gate).astype(BF16)
        rec_ref[:, here] = rec
        gate_ref[:, here] = (wide * recalled_ref[:, here] * gate * (1.0 - gate)).astype(BF16)
        for h in range(count):
            query = mem_ref[:, (3 * side * count + h) * HD : (3 * side * count + h + 1) * HD]
            inward = (query.astype(F32) * column(table, INFLOW + h)).astype(BF16)
            state_ref[side * count + h, :HD] += dot(inward, rec[:, h * HD : (h + 1) * HD], ((0,), (0,)))
            carry = column(table, INFLOW + h)[-8:]
            state_ref[side * count + h, HD:] = jnp.broadcast_to(carry[7:8], (8, HD))


def side_columns(head, own):
    first = head // own * 3 * own + lax.rem(head, own)
    return [pl.ds(pl.multiple_of((first + part * own) * HD, HD), HD) for part in range(3)]


def attend_back_kernel(
    scale, place, q_ref, k_ref, v_ref, g_ref, pk_ref, pv_ref, table_ref, log_ref,
    out_ref, dper_ref, dk_sum, dv_sum,
):
    h = pl.program_id(0)
    own = pl.num_programs(0)
    seg = q_ref.shape[0]
    table = table_ref[0]
    logs = pick_column(log_ref[0], h)
    dq_at, dk_at, dv_at = side_columns(h, own)
    pk, pv = pk_ref[...], pv_ref[...]
    persist = pk.shape[0]
    dk_sum[...] = jnp.zeros_like(dk_sum)
    dv_sum[...] = jnp.zeros_like(dv_sum)
    dpk = jnp.zeros(pk.shape, F32)
    dpv = jnp.zeros(pv.shape, F32)
    for first in range(0, seg, BLOCK):
        rows, end = slice(first, first + BLOCK), first + BLOCK
        ok = allowed_block(table, first, BLOCK, end)
        query, grad = q_ref[rows], g_ref[rows]
        s = dot(query, k_ref[:end], ((1,), (1,))) * (scale * LOG2E)
        p = jnp.where(ok, jnp.exp2(s - logs[rows]), 0.0)
        pp = jnp.exp2(dot(query, pk, ((1,), (1,))) * (scale * LOG2E) - logs[rows])
        dp = dot(grad, v_ref[:end], ((1,), (1,)))
        dpp = dot(grad, pv, ((1,), (1,)))
        delta = jnp.sum(p * dp, axis=-1, keepdims=True) + jnp.sum(pp * dpp, axis=-1, keepdims=True)
        ds = (p * (dp - delta)).astype(BF16)
        dps = (pp * (dpp - delta)).astype(BF16)
        dq = dot(ds, k_ref[:end], ((1,), (0,))) + dot(dps, pk, ((1,), (0,)))
        out_ref[rows, dq_at] = (scale * dq).astype(BF16)
        dk_sum[:end] += dot(ds, query, ((0,), (0,)))
        dv_sum[:end] += dot(p.astype(BF16), grad, ((0,), (0,)))
        dpk = dpk + dot(dps, query, ((0,), (0,)))
        dpv = dpv + dot(pp.astype(BF16), grad, ((0,), (0,)))
    out_ref[:, dk_at] = (scale * dk_sum[...]).astype(BF16)
    out_ref[:, dv_at] = dv_sum[...].astype(BF16)
    dper_ref[0, :persist] = scale * dpk
    dper_ref[0, persist:] = dpv


def unit_grad(unit, inv, grad):
    unit = unit.astype(F32)
    return inv * (grad - unit * jnp.sum(unit * grad, axis=-1, keepdims=True))


def memory_back(
    head, count, mq_ref, mk_ref, mv_ref, g_ref, inv_ref, table_ref, decay_ref, state_ref, gstate_ref,
    out_ref, dk_sum, dv_sum,
):
    h = lax.rem(head, count)
    dq_at, dk_at, dv_at = side_columns(head, count)
    seg = mq_ref.shape[0]
    table = table_ref[0]
    invs = inv_ref[0]
    down = pick_column(table, DECAY + h)
    inflow = pick_column(table, INFLOW + h)
    keep = pick_column(table, KEEP + h)
    query_inv, key_inv = pick_column(invs, h), pick_column(invs, count + h)
    across = decay_ref[0]
    state, gstate = state_ref[0], gstate_ref[0]
    dk_sum[...] = jnp.zeros_like(dk_sum)
    dv_sum[...] = jnp.zeros_like(dv_sum)
    for first in range(0, seg, BLOCK):
        rows, end = slice(first, first + BLOCK), first + BLOCK
        ok = allowed_block(table, first, BLOCK, end)
        query, grad = mq_ref[rows], g_ref[rows]
        grid = jnp.where(ok, jnp.exp2(jnp.minimum(down[rows] - across[:, :end], 0.0)), 0.0)
        w = (dot(query, mk_ref[:end], ((1,), (1,))) * grid).astype(BF16)
        dw = (dot(grad, mv_ref[:end], ((1,), (1,))) * grid).astype(BF16)
        dq = dot(dw, mk_ref[:end], ((1,), (0,))) + inflow[rows] * dot(grad, state, ((1,), (1,)))
        out_ref[rows, dq_at] = unit_grad(query, query_inv[rows], dq).astype(BF16)
        dk_sum[:end] += dot(dw, query, ((0,), (0,)))
        dv_sum[:end] += dot(w, grad, ((0,), (0,)))
    key, value = mk_ref[...], mv_ref[...]
    dk = dk_sum[...] + keep * dot(value, gstate, ((1,), (1,)))
    out_ref[:, dk_at] = unit_grad(key, key_inv, dk).astype(BF16)
    kept = (key.astype(F32) * keep).astype(BF16)
    out_ref[:, dv_at] = (dv_sum[...] + dot(kept, gstate, ((1,), (0,)))).astype(BF16)


def in_back_kernel(
    place, x_ref, normed_ref, rim_ref, table_ref, gain_ref, taps_ref, rim_grad_ref,
    dqkv_ref, gate_ref, dmem_ref, w_a, w_b, gain_out, taps_out, *outs,
):
    outs, carried, held = outs[:-2], outs[-2], outs[-1]
    step = pl.program_id(0)
    block = pl.num_programs(0) - 1 - step
    rows = x_ref.shape[1]
    cols = gate_ref.shape[1] // 2
    taps = taps_ref.shape[0]

    @pl.when(step == 0)
    def _():
        gain_out[...] = jnp.zeros_like(gain_out)
        taps_out[...] = jnp.zeros_like(taps_out)
        carried[...] = rim_grad_ref[...]

    mix_a = jnp.concatenate([dqkv_ref[:, : 3 * cols], gate_ref[:, :cols]], axis=1)
    mix_b = jnp.concatenate([dqkv_ref[:, 3 * cols :], gate_ref[:, cols:]], axis=1)
    conv_grad = dot(dmem_ref[:, : 3 * cols], w_a[:, 4 * cols : 7 * cols], ((1,), (1,)))
    conv_grad = conv_grad + dot(dmem_ref[:, 3 * cols :], w_b[:, 4 * cols : 7 * cols], ((1,), (1,)))
    grad = dot(mix_a, w_a[:, : 4 * cols], ((1,), (1,))) + dot(mix_b, w_b[:, : 4 * cols], ((1,), (1,)))
    normed = normed_ref[pl.ds(pl.multiple_of(block * rows, rows), rows)].astype(F32)
    before = normed_ref[pl.ds(pl.multiple_of(jnp.maximum(block * rows - 16, 0), 16), 16)].astype(F32)[8:]
    before = jnp.where(block == 0, rim_ref[...].astype(F32), before)
    ext = jnp.concatenate([before, normed], axis=0)
    age = column(table_ref[...], AGE)
    taps_out[0:1] += jnp.sum(conv_grad * normed, axis=0, keepdims=True)
    grad = grad + conv_grad * taps_ref[0:1]
    spread = jnp.zeros((rows + 8, x_ref.shape[2]), F32)
    zeros = jnp.zeros((8, x_ref.shape[2]), F32)
    for tap in range(1, taps):
        masked = jnp.where(age >= tap, conv_grad, 0.0)
        taps_out[tap : tap + 1] += jnp.sum(masked * pltpu.roll(ext, tap, 0)[8:], axis=0, keepdims=True)
        term = jnp.concatenate([zeros, masked * taps_ref[tap : tap + 1]], axis=0)
        spread = spread + pltpu.roll(term, rows + 8 - tap, 0)
    grad = grad + spread[8:]
    grad = jnp.concatenate([grad[: rows - 8], grad[rows - 8 :] + carried[...]], axis=0)
    carried[...] = spread[:8]
    x = x_ref[0]
    inv = lax.rsqrt(jnp.mean(x * x, axis=-1, keepdims=True) + EPS)
    hat = x * inv
    scaled = grad * gain_ref[0:1]
    held[...] = inv * (scaled - hat * jnp.mean(scaled * hat, axis=-1, keepdims=True))
    split_columns(place, held, outs)
    gain_out[0:1] += jnp.sum(grad * hat, axis=0, keepdims=True)


def put_grad(place, grad, keep_ref, keep_at, sends):
    mine = place[CORE] == 0
    share = keep_ref.shape[1]
    grad = grad.astype(BF16)
    n = grad.shape[1]
    wide = sends[0].shape[2]
    for i in range(grad.shape[0] // (2 * share)):
        low = grad[2 * i * share : (2 * i + 1) * share]
        high = grad[(2 * i + 1) * share : (2 * i + 2) * share]
        keep_ref[i, :, keep_at : keep_at + n] = jnp.where(mine, low, high)
        send = jnp.where(mine, high, low)
        for first in range(keep_at // wide * wide, keep_at + n, wide):
            low_at, high_at = max(first, keep_at), min(first + wide, keep_at + n)
            sends[first // wide][i, :, low_at - first : high_at - first] = send[:, low_at - keep_at : high_at - keep_at]


def memory_back_kernel(place, *refs):
    memory_back(pl.program_id(0), pl.num_programs(0) // 2, *refs)


def weight_grad_kernel(
    place, normed_ref, conv_ref, mix_ref, dqkv_ref, gate_ref, branch_ref, dmem_ref, keep_ref, send_ref
):
    cols = gate_ref.shape[1] // 2
    sends = [send_ref]
    normed, conv, mix = normed_ref[...].T, conv_ref[...].T, mix_ref[...].T
    for side in range(2):
        one, three = slice(side * cols, (side + 1) * cols), slice(3 * side * cols, 3 * (side + 1) * cols)
        first = 8 * side * cols
        put_grad(place, dot(normed, dqkv_ref[:, three], ((1,), (0,))), keep_ref, first, sends)
        put_grad(place, dot(normed, gate_ref[:, one], ((1,), (0,))), keep_ref, first + 3 * cols, sends)
        put_grad(place, dot(mix, branch_ref[:, one], ((1,), (0,))), keep_ref, first + 4 * cols, sends)
        put_grad(place, dot(conv, dmem_ref[:, three], ((1,), (0,))), keep_ref, first + 5 * cols, sends)


def final_ffn_kernel(hidden, place, mine_ref, got_ref, in_ref, out_ref):
    total = mine_ref[...] + got_ref[...].astype(F32)
    wide = total.shape[1] // 3
    in_ref[:, 0, :] = total[:, :hidden]
    in_ref[:, 1, :] = total[:, wide : wide + hidden]
    out_ref[...] = total[:, 2 * wide :].T[:hidden]


def final_mixer_kernel(place, mine_ref, got_ref, mixer_ref, memory_ref, out_ref):
    total = mine_ref[...] + got_ref[...].astype(F32)
    cols = total.shape[1] // 8
    for i in range(4):
        mixer_ref[:, i, :] = total[:, i * cols : (i + 1) * cols]
    for i in range(3):
        memory_ref[:, i, :] = total[:, (5 + i) * cols : (6 + i) * cols]
    out_ref[...] = total[:, 4 * cols : 5 * cols].T


def placed_kernel(place, *refs):
    parts, out_ref = refs[:-1], refs[-1]
    first = place[BATCH] == 0
    rows = parts[0].shape[0]
    count = len(parts) // 2
    for i in range(count):
        mine, got = parts[i][...], parts[count + i][...].astype(F32)
        out_ref[0, i * rows : (i + 1) * rows] = jnp.where(first, mine, got)
        out_ref[1, i * rows : (i + 1) * rows] = jnp.where(first, got, mine)


def ffn_grad_kernel(place, left_ref, acts_ref, keep_ref, send_ref):
    put_grad(place, dot(left_ref[...], acts_ref[...], ((1,), (0,))), keep_ref, 0, [send_ref])


def local(
    stream,
    cotangent,
    mixer_in,
    memory_in,
    mixer_out,
    ffn_in,
    ffn_out,
    persistent,
    norm_gains,
    conv_weight,
    decays,
    doc_starts,
):
    batches, seg, width = stream.shape
    at = Place(batches)
    cols = mixer_out.shape[0]
    own = cols // HD
    heads = 2 * own
    hidden = ffn_out.shape[0]
    wide = -(-hidden // LANES) * LANES
    taps = conv_weight.shape[0]
    persist = persistent.shape[0] // 2
    scale = HD**-0.5
    steps = seg // BLOCK
    chips = at.ns // 2
    share = width // at.ns
    col = width // at.nz
    pick = lambda a: lax.dynamic_index_in_dim(a, at.p, 0, False)
    drop = lambda a: lax.dynamic_index_in_dim(a, 1 - at.p, 0, False)
    place = jnp.stack([at.p, at.l] + [at.bit_of(bit) for bit in at.bits] + [at.seq // 2])
    last_place = place.shape[0] - 1
    line = Line(place.astype(jnp.int32))
    run = line.run

    per_a, decay_a = persistent, pick(decays)
    decay_b = at.other(drop(decays))

    last = lax.dynamic_slice(stream, (at.p, seg - 8, 0), (1, 8, width))[0]
    last = last * lax.rsqrt(jnp.mean(last * last, axis=-1, keepdims=True) + EPS)
    rim_rows = at.along((last * norm_gains[0]).astype(BF16), 1)

    first_row = at.seq * share
    rows_of = lambda a: lax.dynamic_slice_in_dim(a, first_row, share, 0)
    cols_of = lambda a: lax.dynamic_slice_in_dim(a, first_row, share, 1)

    def joined(into, memory, out):
        return jnp.concatenate(
            [into.reshape(into.shape[0], -1), memory.reshape(into.shape[0], -1), out.T], axis=1
        )

    pad = lambda a: jnp.pad(a, ((0, 0), (0, wide - hidden)))

    def ffn_joined(into, out):
        return jnp.concatenate([pad(into[:, 0]), pad(into[:, 1]), pad(out.T)], axis=1)

    part_w = at.other(joined(rows_of(mixer_in), rows_of(memory_in), cols_of(mixer_out)))
    part_f = ffn_joined(rows_of(ffn_in), cols_of(ffn_out))

    def spread(part):
        return (part, *[at.across(part, 2 * r) for r in range(1, chips)])

    def stacked(parts, relay=()):
        n = parts[0].shape[1]
        mine, *relayed = run(
            stack_kernel, (1,), [full(a) for a in parts], [fixed((chips, share, n), BF16)], placed=False, relay=relay
        )
        return (mine, at.across(mine, 1)), *relayed

    def assemble(mine, theirs):
        n = mine.shape[2]
        block = lambda r, s: (r, 0, 0)
        (out,) = run(
            assemble_kernel,
            (chips,),
            [(mine, (1, share, n), block), (theirs, (1, share, n), block)],
            [((chips, 2 * share, n), BF16, (1, 2 * share, n), lambda r, s: (s[last_place] ^ r, 0, 0))],
        )
        return out.reshape(width, n)

    first_pos = at.seq * seg
    positions = first_pos + jnp.arange(seg, dtype=jnp.int32)
    marks = pick(doc_starts)
    starts = jnp.max(jnp.where(marks[None, :] <= positions[:, None], marks[None, :], 0), axis=-1)

    def token_table(decay):
        log_sums = jnp.cumsum(jnp.log(decay), axis=-1)
        inflow = jnp.exp(log_sums) * (starts < first_pos).astype(F32)
        keep = jnp.exp(log_sums[:, seg - 1 :] - log_sums) * (positions >= starts[seg - 1]).astype(F32)
        scaled_sums = log_sums * LOG2E
        gap = jnp.zeros((4 - own, seg), F32)
        table = jnp.concatenate(
            [
                scaled_sums, gap, inflow, gap, keep, gap,
                jnp.maximum(starts - first_pos, 0).astype(F32)[None],
                (positions - starts).astype(F32)[None],
            ],
            axis=0,
        )
        return jnp.pad(table, ((0, LANES - table.shape[0]), (0, 0))).T, scaled_sums[:, None]


    blk = (BLOCK, width)
    batch_rows = lambda i, s: (s[BATCH], i, 0)
    gains_in = (norm_gains, norm_gains.shape, whole(2))
    taps_in = (conv_weight, conv_weight.shape, whole(2))
    stream_in = (stream, (1,) + blk, batch_rows)
    cot_in = (cotangent, (1,) + blk, batch_rows)

    def full(a):
        return (a, a.shape, whole(a.ndim))

    def held(a):
        return (a, None, None)

    def tiled(a, n=None):
        return (a, (BLOCK, n or a.shape[1]), rows_map)

    def out_rows(n, dtype):
        return ((seg, n), dtype, (BLOCK, n), rows_map)

    def fixed(shape, dtype=F32):
        return (shape, dtype, shape, whole(len(shape)))

    ages = jnp.broadcast_to((positions - starts)[:, None], (seg, LANES))
    normed, conv_out, part_f = run(
        norm_conv_kernel,
        (steps,),
        [stream_in, gains_in, full(rim_rows), tiled(ages), taps_in],
        [out_rows(width, BF16), out_rows(width, BF16)],
        scratch=[pltpu.VMEM((8, width), F32)],
        flops=20 * seg * width,
        relay=(part_f,),
    )
    part_f = at.other(part_f)
    mixer_in, memory_in, mixer_out, decay_a, _ = lax.optimization_barrier(
        (mixer_in, memory_in, mixer_out, decay_a, conv_out)
    )
    w_a = joined(mixer_in, memory_in, mixer_out)
    table_a, decay_rows_a = token_table(decay_a)
    per_b = at.other(persistent)

    def project(side, w, table, onto=(), relay=()):
        half_cols = lambda n, dtype: ((seg, 2 * n), dtype, (BLOCK, n), lambda i, s: (i, side))
        return run(
            project_kernel,
            (steps,),
            [tiled(normed), tiled(conv_out), held(w), tiled(table)],
            [
                half_cols(3 * cols, BF16), half_cols(cols, F32), half_cols(3 * cols, BF16),
                ((2, seg, LANES), F32, (1, BLOCK, LANES), lambda i, s: (side, i, 0)),
                ((heads, HD + 8, HD), F32, (own, HD + 8, HD), lambda i, s: (side, 0, 0)),
            ],
            placed=False,
            flops=2 * seg * width * 7 * cols,
            onto=onto,
            relay=relay,
        )

    def head_cols(a, part, first=0):
        return (
            a,
            (seg, HD),
            lambda h, s: (0, (first + jnp.minimum(h, heads - 1 - first)) // own * 3 * own + part * own + lax.rem(first + jnp.minimum(h, heads - 1 - first), own)),
        )

    pair_flops = own * seg * seg * HD * 1.25

    def attend(side, qkv, mem, per, table, rows, onto=(), relay=()):
        first = side * own
        return run(
            functools.partial(attend_kernel, scale),
            (own,),
            [head_cols(qkv, i, first) for i in range(3)]
            + [head_cols(mem, i, first) for i in range(3)]
            + [(per, (persist, HD), lambda h, s: (0, h)), (per, (persist, HD), lambda h, s: (1, h))]
            + [full(table[None]), (rows, (1, 1, seg), lambda h, s: (h, 0, 0))],
            [((seg, 2 * cols), F32, (seg, HD), lambda h, s: (0, first + h))] * 2
            + [((2, seg, LANES), F32, (1, seg, LANES), lambda h, s: (side, 0, 0))],
            placed=False,
            flops=4 * pair_flops,
            trans=own * seg * seg * 1.25,
            onto=onto,
            relay=relay,
        )

    def scan(mine, reverse, first, second, relay):
        got = at.across(mine, 1)
        first()
        pair, *relayed = run(
            functools.partial(pair_scan_kernel, reverse), (1,), [full(mine), full(got)], [fixed(mine.shape)], relay=relay
        )
        pairs = [pair] + [at.across(pair, 2 * r) for r in range(1, chips)]
        second(*relayed)
        (out,) = run(
            functools.partial(chip_scan_kernel, reverse, chips),
            (1,),
            [full(got)] + [full(a) for a in pairs],
            [fixed((heads, HD, HD), BF16)],
        )
        return out, *relayed

    kept = {}

    part_w, w_a = lax.optimization_barrier((part_w, w_a))
    parts_w = spread(part_w)
    projected = project(0, w_a, table_a)
    attended = attend(0, projected[0], projected[2], per_a, table_a, decay_rows_a)
    decay_b, _ = lax.optimization_barrier((decay_b, projected[3]))
    parts_w, part_f = stacked(parts_w, (part_f,))
    parts_f = spread(part_f)
    w_b = assemble(*parts_w)
    table_b, decay_rows_b = token_table(decay_b)
    line.wait(per_b)
    qkv, gate, mem, inv, state = project(1, w_b, table_b, projected)

    def attend_other(*_):
        kept["att"] = attend(1, qkv, mem, per_b, table_b, decay_rows_b, attended)

    ffn_in, ffn_out, _ = lax.optimization_barrier((ffn_in, ffn_out, inv))
    f_a = ffn_joined(ffn_in, ffn_out)
    line.wait(f_a)
    nothing = lambda: None
    state_in, *parts_f = scan(state, False, nothing, attend_other, parts_f)
    att, rec, logs = kept["att"]
    (parts_f,) = stacked(parts_f)
    tables = jnp.stack([table_a, table_b])
    decay_rows = jnp.concatenate([decay_rows_a, decay_rows_b], axis=0)
    per_two = jnp.concatenate([per_a, per_b], axis=1)
    out_block = lambda w: (w, (width, cols), lambda i, s: (0, 7))

    half = steps // 2

    def half_in(a, part, n=None):
        return (a, (BLOCK, n or a.shape[1]), lambda i, s: (i + part * half, 0))

    def half_out(n, dtype, part):
        return ((seg, n), dtype, (BLOCK, n), lambda i, s: (i + part * half, 0))

    def half_batch(a, part):
        return (a, (1,) + blk, lambda i, s: (s[BATCH], i + part * half, 0))

    sent_half = ((seg // 2, width), BF16, blk, rows_map)

    def group_sum(part):
        got = [at.group(part, n) for n in range(1, at.nl)]
        total = got[0]
        for more in got[1:]:
            total = (total.astype(F32) + more.astype(F32)).astype(BF16)
        return total

    mixed, mixed_got, onto = [], [], ()
    for part in range(2):
        recalled, branch, mixed_part = run(
            mix_kernel,
            (half,),
            [half_in(a, part) for a in (att, rec, gate, mem, table_a, table_b)]
            + [full(state_in), out_block(w_a), out_block(w_b)],
            [half_out(2 * cols, F32, part), half_out(2 * cols, BF16, part), sent_half],
            placed=False,
            flops=seg * width * 2 * cols,
            onto=onto,
        )
        onto = (recalled, branch)
        mixed.append(mixed_part)
        mixed_got.append(group_sum(mixed_part))

    f_b = assemble(*parts_f)
    back, back_got, onto = [], [], ()
    for part in range(2):
        normed_t, cot_t, acts, *ffn_parts, back_part = run(
            ffn_kernel,
            (half,),
            [half_batch(stream, part), tiled(mixed[part]), tiled(mixed_got[part]), half_batch(cotangent, part)]
            + [gains_in, held(f_a), held(f_b)],
            [((width, seg), BF16, (width, BLOCK), lambda i, s, part=part: (0, i + part * half))] * 2
            + [half_out(6 * wide, BF16, part)]
            + [half_out(batches * col, BF16, part)] * at.nl
            + [sent_half],
            scratch=[pltpu.VMEM(blk, F32)],
            flops=seg * width * wide * 12,
            onto=onto,
        )
        onto = (normed_t, cot_t, acts, *ffn_parts)
        back.append(back_part)
        back_got.append(group_sum(back_part))
    chip_bits = [bit // 2 for bit in at.bits[1:]]
    orders = (list(reversed(chip_bits)), chip_bits)

    def exchange(parts, step):
        return [parts[0], parts[2]], [at.across(parts[2 * i + 1], 2 * orders[i][step]) for i in range(2)]

    def core_sum(keep_part, got):
        n = got.shape[2]
        there = lambda r, s: (s[last_place] ^ r, 0, 0)
        parts = run(
            functools.partial(core_sum_kernel, (orders[0][0], orders[1][0])),
            (chips,),
            [(a, (1, share, n), there) for a in (keep_part, got)],
            [fixed((chips // 2, share, n // 2), BF16)] * 4,
        )
        return exchange(parts, 0)

    def chip_step(keeps, gots, step):
        half_n = keeps[0].shape[2]
        ins = [full(a) for a in (*keeps, *gots)]
        if step == len(chip_bits):
            mine, theirs = run(
                functools.partial(chip_step_kernel, None),
                (1,),
                ins,
                [fixed((share, half_n)), fixed((share, half_n), BF16)],
                placed=False,
            )
            return mine, at.other(theirs)
        rests = []
        for order in orders:
            gone = sum(order[:step])
            held = [r for r in range(chips) if not r & gone]
            rests.append(tuple([i for i, r in enumerate(held) if bool(r & order[step]) == sent] for sent in (False, True)))
        parts = run(
            functools.partial(chip_step_kernel, rests),
            (1,),
            ins,
            [fixed((len(places), share, half_n), BF16) for rest in rests for places in rest],
            placed=False,
        )
        return exchange(parts, step)

    def middle_steps(sums):
        for step in range(1, len(chip_bits)):
            sums = chip_step(*sums, step)
        return sums

    def ffn_grads(left, count, chunk, onto=()):
        return run(
            ffn_grad_kernel,
            (count,),
            [full(left), (acts, (seg, wide), lambda i, s: (0, chunk(i)))],
            [((chips, share, 6 * wide), BF16, (chips, share, wide), lambda i, s: (0, 0, chunk(i)))] * 2,
            flops=2 * seg * width * wide * count,
            onto=onto,
            far=(0, 1),
        )

    half_f = ffn_grads(normed_t, 4, lambda i: i + i // 2)
    line.wait(back_got[0])
    keep_f, send_f = ffn_grads(cot_t, 2, lambda i: 3 * i + 2, half_f)
    gain_two, state_terms = jnp.zeros((8, width), F32), jnp.zeros((heads, HD + 8, HD), F32)
    onto = ()
    for part in range(2):
        grad_mid, grad_mix, grad_branch, grad_rec, grad_gate, gain_two, state_terms, *relayed = run(
            mid_back_kernel,
            (half,),
            [half_batch(stream, part)]
            + [tiled(a[part]) for a in (mixed, mixed_got, back, back_got)]
            + [half_batch(cotangent, part), gains_in, out_block(w_a), out_block(w_b)]
            + [half_in(a, part) for a in (gate, recalled, mem, table_a, table_b)]
            + [full(gain_two), full(state_terms)],
            [half_out(width, F32, part), half_out(width, BF16, part)]
            + [half_out(2 * cols, BF16, part)] * 3
            + [fixed((8, width)), fixed((heads, HD + 8, HD))],
            flops=seg * width * 2 * cols,
            onto=onto,
            relay=tuple(ffn_parts[1:]) if part == 0 else (),
        )
        if part == 0:
            ffn_shares = [ffn_parts[0]] + [at.group(a, r + 1) for r, a in enumerate(relayed)]
        onto = (grad_mid, grad_mix, grad_branch, grad_rec, grad_gate)

    def of_side(a):
        return (a, (1, *a.shape[1:]), lambda h, s: (jnp.minimum(h, heads - 1) // own, 0, 0))

    def of_head(a):
        return (a, (1, *a.shape[1:]), lambda h, s: (jnp.minimum(h, heads - 1), 0, 0))

    def head_block(a):
        return (a, (seg, HD), lambda h, s: (0, jnp.minimum(h, heads - 1)))

    def attend_back(side, onto=()):
        first = side * own
        return run(
            functools.partial(attend_back_kernel, scale),
            (own,),
            [head_cols(qkv, i, first) for i in range(3)]
            + [(grad_branch, (seg, HD), lambda h, s: (0, first + h))]
            + [(per_two, (persist, HD), lambda h, s: (0, first + h)), (per_two, (persist, HD), lambda h, s: (1, first + h))]
            + [(a, (1, seg, LANES), lambda h, s: (side, 0, 0)) for a in (tables, logs)],
            [
                ((seg, 6 * cols), BF16, (seg, 3 * cols), lambda h, s: (0, side)),
                ((heads, 2 * persist, HD), F32, (1, 2 * persist, HD), lambda h, s: (first + h, 0, 0)),
            ],
            scratch=[pltpu.VMEM((seg, HD), F32)] * 2,
            placed=False,
            flops=5 * pair_flops,
            trans=own * seg * seg * 0.6,
            onto=onto,
        )

    def during_scan(send_f):
        kept["f"] = at.across(send_f, 1)
        kept["back"] = attend_back(0)

    grad_state, send_f = scan(state_terms, True, nothing, during_scan, (send_f,))
    got_f = kept["f"]
    sums_f = core_sum(keep_f, got_f)


    def share_ins(arrays, side):
        return [(a, (BLOCK, col), lambda i, s: (i, lax.rem(s[BATCH] + side, batches))) for a in arrays]

    def wide_in(a, side):
        return (a, (BLOCK, col), lambda i, s: (i, lax.rem(s[BATCH] + side, batches) * at.nl + s[GROUP]))

    (dmem,) = run(
        memory_back_kernel,
        (heads,),
        [head_cols(mem, i) for i in range(3)]
        + [head_block(grad_rec), of_side(inv), of_side(tables), of_head(decay_rows), of_head(state_in), of_head(grad_state)],
        [fixed((seg, 6 * cols), BF16)],
        scratch=[pltpu.VMEM((seg, HD), F32)] * 2,
        flops=10 * pair_flops,
        trans=2 * own * seg * seg * 0.6,
        placed=False,
    )
    first_grad = dot(dmem[:8, : 3 * cols], w_a[:, 4 * cols : 7 * cols], ((1,), (1,))) + dot(
        dmem[:8, 3 * cols :], w_b[:, 4 * cols : 7 * cols], ((1,), (1,))
    )
    first_ages = (positions - starts)[:8, None]
    rim_back = jnp.zeros((8, width), F32)
    for tap in range(1, taps):
        term = jnp.where(first_ages >= tap, first_grad, 0.0)[:tap] * conv_weight[tap]
        rim_back = rim_back + jnp.pad(term, ((8 - tap, 0), (0, 0)))
    rim_back = at.along(rim_back, -1)

    ins = []
    for side in range(2):
        ins.append(
            (
                stream,
                (1, BLOCK, col),
                lambda i, s, side=side: (s[BATCH], i, lax.rem(s[BATCH] + side, batches) * at.nl + s[GROUP]),
            )
        )
        ins += [
            (
                a,
                (BLOCK, col),
                lambda i, s, side=side, part=part: (
                    jnp.clip(i - part * half, 0, half - 1),
                    lax.rem(s[BATCH] + side, batches) * at.nl + s[GROUP],
                ),
            )
            for part in range(2)
            for a in (mixed[part], mixed_got[part])
        ] + share_ins(ffn_shares, side)
    result_mine, result_send, squares = run(
        functools.partial(result_kernel, at.nl),
        (steps,),
        ins,
        [out_rows(col, F32), out_rows(col, BF16), fixed((8, col))],
    )
    result_got = at.other(result_send)
    sums_f = middle_steps(sums_f)
    dqkv, per_grad = attend_back(1, kept["back"])
    line.wait(result_got)
    f_mine, f_got = chip_step(*sums_f, len(chip_bits))
    line.wait(rim_back)
    span = max(2 * share, 256)
    pairs = span // (2 * share)
    left_in = lambda a: (a, (seg, span), lambda i, s: (0, i))
    keep_x, send_x = run(
        weight_grad_kernel,
        (width // span,),
        [left_in(normed), left_in(conv_out), left_in(grad_mix), full(dqkv), full(grad_gate), full(branch), full(dmem)],
        [((chips, share, 16 * cols), BF16, (pairs, share, 16 * cols), lambda i, s: (i, 0, 0))] * 2,
        flops=2 * seg * width * 16 * cols,
    )


    def placed(*parts):
        return run(placed_kernel, (1,), [full(a) for a in parts], [fixed((batches, seg, col))])[0]

    result = placed(result_mine, result_got)
    got_x = at.across(lax.optimization_barrier((send_x, result))[0], 1)
    turned = lambda i, s: (steps - 1 - i, 0)
    turn = lambda a: (a, (BLOCK, a.shape[1]), turned)
    gain_one, grad_conv, *in_parts = run(
        in_back_kernel,
        (steps,),
        [
            (stream, (1,) + blk, lambda i, s: (s[BATCH], steps - 1 - i, 0)),
            full(normed), full(rim_rows), turn(table_a), gains_in, taps_in, full(rim_back),
        ]
        + [turn(a) for a in (dqkv, grad_gate, dmem)]
        + [held(w_a), held(w_b)],
        [fixed((8, width))] * 2 + [((seg, batches * col), BF16, (BLOCK, batches * col), turned)] * at.nl,
        scratch=[pltpu.VMEM((8, width), F32), pltpu.VMEM(blk, F32)],
        flops=2 * seg * width * 14 * cols,
    )
    in_shares = [in_parts[0]] + [at.group(a, r) for r, a in enumerate(in_parts) if r > 0]
    sums_x = core_sum(keep_x, got_x)

    small = jnp.concatenate(
        [
            gain_one[:1], gain_two[:1] / at.nl, grad_conv[:taps],
            jnp.pad(jnp.sum(squares[:4], axis=-1), (0, width - 4))[None],
            per_grad.reshape(-1, width),
        ],
        axis=0,
    )
    small = jnp.pad(small, ((0, -small.shape[0] % 8), (0, 0)))

    def added(parts):
        return run(add_kernel, (1,), [full(a) for a in parts], [fixed(parts[0].shape)], placed=False)[0]

    small_got = at.across(small, 1)
    small = added([small, small_got])

    ins = []
    for side in range(2):
        ins += [wide_in(grad_mid, side)] + share_ins(in_shares, side)
    stream_mine, stream_send = run(
        functools.partial(stream_grad_kernel, at.nl), (steps,), ins, [out_rows(col, F32), out_rows(col, BF16)]
    )
    stream_got = at.other(stream_send)
    sums_x = middle_steps(sums_x)
    grad_ffn_in, grad_ffn_out = run(
        functools.partial(final_ffn_kernel, hidden),
        (1,),
        [full(f_mine), full(f_got)],
        [fixed((share, 2, hidden)), fixed((hidden, share))],
        placed=False,
    )
    x_mine, x_got = chip_step(*sums_x, len(chip_bits))
    for bit in at.bits[1:-1]:
        small = added([small, at.across(small, bit)])
    small = added([small, at.across(small, at.bits[-1])])
    head_parts = [small] + [
        lax.ppermute(small, "head", [(i, (i + n) % at.nz) for i in range(at.nz)]) for n in range(1, at.nz)
    ]
    grad_stream = placed(stream_mine, stream_got)
    grad_mixer_in, grad_memory_in, grad_mixer_out = run(
        final_mixer_kernel,
        (1,),
        [full(x_mine), full(x_got)],
        [fixed((share, 4, cols)), fixed((share, 3, cols)), fixed((cols, share))],
        placed=False,
    )

    sums = sum(a[: 3 + taps] for a in head_parts[1:]) + small[: 3 + taps]
    rows_p = persistent.shape[0] // at.ns

    def persist_rows(a):
        a = a[3 + taps : 3 + taps + heads * 2 * persist * HD // width].reshape(heads, 2 * persist, HD)
        a = lax.dynamic_slice_in_dim(a, at.seq * rows_p, rows_p, 1)
        return jnp.transpose(a, (1, 0, 2)).reshape(rows_p, -1)

    grad_persistent = persist_rows(small)[:, :cols] + persist_rows(head_parts[at.nl])[:, cols:]
    cells = float(batches * seg * at.ns * width)
    rms_values = jnp.sqrt(sums[2 + taps, :4] / cells)
    return (
        result,
        grad_stream,
        grad_mixer_in,
        grad_memory_in,
        grad_mixer_out,
        grad_ffn_in,
        grad_ffn_out,
        grad_persistent,
        sums[:2],
        sums[2 : 2 + taps],
        rms_values,
    )


def solution(mesh):
    placed = (
        P(None, "seq", None),
        P(None, "seq", None),
        P(None, None, "head"),
        P(None, None, "head"),
        P("head", None),
        P(None, None, "head"),
        P("head", None),
        P(None, "head"),
        P(),
        P(),
        P(None, "head", "seq"),
        P(),
    )
    return jax.shard_map(
        local,
        mesh=mesh,
        in_specs=placed,
        out_specs=(
            P(None, "seq", "head"),
            P(None, "seq", "head"),
            P("seq", None, "head"),
            P("seq", None, "head"),
            P("head", "seq"),
            P("seq", None, "head"),
            P("head", "seq"),
            P("seq", "head"),
            P(),
            P(),
            P(),
        ),
        check_vma=False,
    )
```
